32 devices in a mesh: clip: 4 (over z), tile: 8 (over y, x, core).
Axes of the slice: x: 2, y: 2, z: 4, core: 2. Of those that a mesh axis runs over, the one named last changes fastest.
Arguments:
- tokens: bfloat16 [256, 16, 16, 1024], P('tile', 'clip'), may hold values from -6 to 6
- mask_bits: int32 [256, 16, 16], P('tile', 'clip'), may hold values from 0 to 1, as said below
- action_ids: int32 [16, 16], P('clip'), may hold values from 0 to 7
- vectors: float32 [8, 1024], replicated, as said below
- action_table: float32 [8, 1024], replicated, may hold values from -4 to 4
- w_space_qkv: bfloat16 [1024, 3072], replicated, may hold values from -0.1875 to 0.1875
- w_space_out: bfloat16 [1024, 1024], replicated, may hold values from -1.5 to 1.5
- w_time_qkv: bfloat16 [1024, 3072], replicated, may hold values from -0.1875 to 0.1875
- w_time_out: bfloat16 [1024, 1024], replicated, may hold values from -0.5 to 0.5
- w_up: bfloat16 [1024, 4096], replicated, may hold values from -0.1875 to 0.1875
- b_up: float32 [4096], replicated, may hold values from -3 to 3
- w_down: bfloat16 [4096, 1024], replicated, may hold values from -0.09375 to 0.09375
- cotangent: bfloat16 [256, 16, 16, 1024], P('tile', 'clip'), may hold values from -6 to 6
Outputs:
- result: bfloat16 [256, 16, 16, 1024], P('tile', 'clip')
- input_grad: bfloat16 [256, 16, 16, 1024], P('tile', 'clip')
- vectors_grad: float32 [8, 1024], replicated
- table_grad: float32 [8, 1024], replicated
- space_qkv_grad: float32 [1024, 3072], P(('clip', 'tile'))
- space_out_grad: float32 [1024, 1024], P(('clip', 'tile'))
- time_qkv_grad: float32 [1024, 3072], P(('clip', 'tile'))
- time_out_grad: float32 [1024, 1024], P(('clip', 'tile'))
- up_grad: float32 [1024, 4096], P(('clip', 'tile'))
- bias_up_grad: float32 [4096], replicated
- down_grad: float32 [4096, 1024], P(('clip', 'tile'))
The draws below stay inside these ranges and needn't reach their ends.
Inputs may be any that keep to these rules, and one draw needn't show every extreme that they name: `mask_bits`: each clip draws a share between one half and one; each of its tokens is 1 with that probability. `vectors`: gains near one, shifts and biases of a few tenths, the mask embedding of order one.
All inputs are finite; a program needn't handle non-finite values.
Results may differ from the reference program's by a relative error of at most 0.017.
Values may be sent and summed in bfloat16 or wider, within the bound.
No kernel may reach another device: no remote copies, remote signals or barrier semaphores. Data moves between devices by JAX's collectives and lax.ppermute only.
A program may use at most 576 MiB of HBM per device.

```python
import jax
import jax.numpy as jnp
from jax import lax

D = 1024
HEADS = 16
HEAD_DIM = 64
FF = 4096
ACTIONS = 8
GRID = 256
FRAMES = 16
CLIPS = 16


def draw_mask_bits(key, part):
    key = jax.random.fold_in(key, 11)
    ratio_key, bit_key = jax.random.split(key)
    percent = jax.random.randint(ratio_key, (1, CLIPS, 1), 50, 101)
    dice_rolls = jax.random.randint(bit_key, (GRID, CLIPS, FRAMES), 0, 100)
    return (dice_rolls < percent).astype(jnp.int32)


def draw_vectors(key, part):
    key = jax.random.fold_in(key, 23)
    gain_key, shift_key = jax.random.split(key)
    gains = 1.0 + 0.2 * jax.random.normal(gain_key, (3, D), jnp.float32)
    shifts = 0.3 * jax.random.normal(shift_key, (5, D), jnp.float32)
    return jnp.stack([gains[0], shifts[0], gains[1], shifts[1], gains[2], shifts[2], shifts[3], 3.0 * shifts[4]]).astype(jnp.float32)


def place_ends(drawn, stream_key, smallest, largest):
    longest = drawn.shape.index(max(drawn.shape))
    spots = []
    for shift in (0, 1):
        where = [jax.random.randint(jax.random.fold_in(stream_key, axis), (), 0, length) for axis, length in enumerate(drawn.shape)]
        where[longest] = (where[longest] + shift) % drawn.shape[longest]
        spots.append(tuple(where))
    return drawn.at[spots[0]].set(smallest).at[spots[1]].set(largest)


def shard_levels(own_key, shape, pieces, smallest, largest):
    factor_of, own = 1.0, jax.random.fold_in(own_key, 6)
    for dim, blocks in pieces:
        heights = jnp.exp(jax.random.uniform(jax.random.fold_in(own, dim), (blocks,), jnp.float32, smallest / len(pieces), largest / len(pieces)))
        factor_of = factor_of * jnp.repeat(heights, shape[dim] // blocks).reshape([-1 if axis == dim else 1 for axis in range(len(shape))])
    return factor_of


def bell_draw(rng, shape, deviation, bound, pieces=(), kind=jnp.bfloat16):
    entries = jax.random.normal(rng, shape, jnp.float32) * deviation
    if len(pieces) > 0:
        entries = shard_levels(rng, shape, pieces, -0.22, 0.18) * entries
    return jnp.clip(entries, min=-bound, max=bound).astype(kind)


def setup_inputs(seed: int = 0) -> dict:
    splits = jax.random.split(jax.random.key(seed), 14)
    tokens = bell_draw(splits[0], (GRID, CLIPS, FRAMES, D), 1.0, 6.0, ((0, 8), (1, 4)))
    mask_bits = draw_mask_bits(jax.random.fold_in(splits[13], 71), 0)
    action_ids = place_ends(jax.random.randint(splits[2], (CLIPS, FRAMES), 0, ACTIONS), jax.random.fold_in(splits[2], 1), 0, ACTIONS - 1).astype(jnp.int32)
    vectors = draw_vectors(jax.random.fold_in(splits[13], 71), 0)
    action_table = bell_draw(splits[4], (ACTIONS, D), 0.5, 4.0, (), jnp.float32)
    w_space_qkv = bell_draw(splits[5], (D, 3 * D), D ** -0.5, 0.1875)
    w_space_out = bell_draw(splits[6], (D, D), (D // 64) ** -0.5, 1.5)
    w_time_qkv = bell_draw(splits[7], (D, 3 * D), D ** -0.5, 0.1875)
    w_time_out = bell_draw(splits[8], (D, D), (D // 8) ** -0.5, 0.5)
    w_up = bell_draw(splits[9], (D, FF), D ** -0.5, 0.1875)
    b_up = bell_draw(splits[10], (FF,), 0.5, 3.0, (), jnp.float32)
    w_down = bell_draw(splits[11], (FF, D), FF ** -0.5, 0.09375)
    cotangent = bell_draw(splits[12], (GRID, CLIPS, FRAMES, D), 1.0, 6.0, ((0, 8), (1, 4)))
    return dict(tokens=tokens, mask_bits=mask_bits, action_ids=action_ids, vectors=vectors, action_table=action_table, w_space_qkv=w_space_qkv, w_space_out=w_space_out, w_time_qkv=w_time_qkv, w_time_out=w_time_out, w_up=w_up, b_up=b_up, w_down=w_down, cotangent=cotangent)


HIGHEST = lax.Precision.HIGHEST
EPSILON = 1e-05
NEGATIVE = -1e+30

@jax.custom_vjp
def low(v):
    return lax.optimization_barrier(v.astype(jnp.bfloat16)).astype(jnp.float32)

@jax.custom_vjp
def low_back(v):
    return v

def low_keep(v):
    return (low(v), None)

def low_pass(kept, grad):
    return (grad,)

def back_keep(v):
    return (v, None)

def back_low(kept, grad):
    return (low(grad),)
low.defvjp(low_keep, low_pass)
low_back.defvjp(back_keep, back_low)

def both_ways(values):
    return low(low_back(values))

def norm_rows(values, gain_row, shift_row):
    average = lax.optimization_barrier(jnp.mean(values, -1, keepdims=True))
    centred = values - average
    variance = lax.optimization_barrier(jnp.mean(centred * centred, -1, keepdims=True))
    return centred * lax.rsqrt(variance + EPSILON) * gain_row + shift_row

def product(left_side, right_side):
    return jnp.dot(left_side, right_side, precision=HIGHEST)

def attend(queries, key_heads, values, form_scores, form_mix, allowed):
    scores = low_back(jnp.einsum(form_scores, queries, key_heads, precision=HIGHEST) * HEAD_DIM ** (-0.5))
    if allowed is not None:
        scores = jnp.where(allowed, scores, NEGATIVE)
    shares = low(jax.nn.softmax(scores, axis=-1))
    return both_ways(jnp.einsum(form_mix, shares, values, precision=HIGHEST))

def block(clip_tokens, masked, chosen, vectors, action_table, w_space_qkv, w_space_out, w_time_qkv, w_time_out, w_up, b_up, w_down):
    grid_count, frame_count, model_width = clip_tokens.shape
    embedded = jnp.where(masked[..., None], vectors[7], clip_tokens) + jnp.take(action_table, chosen, axis=0)[None]
    normed = low(norm_rows(embedded, vectors[0], vectors[1]))
    packed = both_ways(product(normed, w_space_qkv)).reshape(grid_count, frame_count, 3, HEADS, HEAD_DIM)
    blended = attend(packed[:, :, 0], packed[:, :, 1], packed[:, :, 2], 'qfhe,kfhe->fhqk', 'fhqk,kfhe->qfhe', None)
    after_space = embedded + low_back(product(blended.reshape(grid_count, frame_count, model_width), w_space_out))
    normed = low(norm_rows(after_space, vectors[2], vectors[3]))
    packed = both_ways(product(normed, w_time_qkv)).reshape(grid_count, frame_count, 3, HEADS, HEAD_DIM)
    allowed = jnp.arange(frame_count)[:, None] >= jnp.arange(frame_count)[None, :]
    blended = attend(packed[:, :, 0], packed[:, :, 1], packed[:, :, 2], 'gqhe,gkhe->ghqk', 'ghqk,gkhe->gqhe', allowed)
    after_time = after_space + low_back(product(blended.reshape(grid_count, frame_count, model_width), w_time_out))
    normed = low(norm_rows(after_time, vectors[4], vectors[5]))
    hidden = low_back(product(normed, w_up)) + b_up
    active = low(jax.nn.gelu(hidden, approximate=True))
    return after_time + low_back(product(active, w_down)) + vectors[6]

def reference(tokens, mask_bits, action_ids, vectors, action_table, w_space_qkv, w_space_out, w_time_qkv, w_time_out, w_up, b_up, w_down, cotangent):
    params = (vectors, action_table, w_space_qkv, w_space_out, w_time_qkv, w_time_out, w_up, b_up, w_down)
    params = tuple((element.astype(jnp.float32) for element in params))
    token_all = tokens.astype(jnp.float32)
    upstream_all = cotangent.astype(jnp.float32)

    def per_clip(running, clip_index):
        clip_tokens = jnp.take(token_all, clip_index, axis=1)
        masked = jnp.take(mask_bits, clip_index, axis=1) == 1
        chosen = jnp.take(action_ids, clip_index, axis=0)
        upstream = jnp.take(upstream_all, clip_index, axis=1)

        def local_block(clip_input, *weights):
            return block(clip_input, masked, chosen, *weights)
        output, pullback = jax.vjp(local_block, clip_tokens, *params)
        gradients = pullback(upstream)
        running = tuple((summed + gradient for summed, gradient in zip(running, gradients[1:])))
        return (running, (output.astype(jnp.bfloat16), gradients[0].astype(jnp.bfloat16)))
    initial = tuple((jnp.zeros_like(element) for element in params))
    running, (outputs, input_grads) = lax.scan(per_clip, initial, jnp.arange(CLIPS, dtype=jnp.int32))
    outputs = jnp.transpose(outputs, (1, 0, 2, 3))
    input_grads = jnp.transpose(input_grads, (1, 0, 2, 3))
    return (outputs, input_grads, running[0], running[1], running[2], running[3], running[4], running[5], running[6], running[7], running[8])
```

```python
import jax
import jax.numpy as jnp
from jax import lax
from jax.experimental import pallas as pl
from jax.experimental.pallas import tpu as pltpu
from jax.sharding import PartitionSpec as P

HEADS = 16
HEAD_DIM = 64
PAIR = 2 * HEAD_DIM
EPSILON = 1e-05
NEGATIVE = -1e30
MASKED = 2.0**100
SEEN = 2.0**99
LOG2E = 1.4426950408889634
SCALE = HEAD_DIM**-0.5
F32 = jnp.float32
BF16 = jnp.bfloat16
VMEM_LIMIT = 60 * 1024 * 1024

NN = (((1,), (0,)), ((), ()))
NT = (((1,), (1,)), ((), ()))
TN = (((0,), (0,)), ((), ()))


def dot(left, right, form=NN):
    return lax.dot_general(left, right, form, preferred_element_type=F32)


def normalise(values):
    centred = values - jnp.mean(values, -1, keepdims=True)
    spread = lax.rsqrt(jnp.mean(centred * centred, -1, keepdims=True) + EPSILON)
    return centred * spread, spread


def norm_back(unit, spread, gain, upstream):
    scaled = upstream * gain
    return spread * (
        scaled
        - jnp.mean(scaled, -1, keepdims=True)
        - unit * jnp.mean(scaled * unit, -1, keepdims=True)
    )


def half_masks():
    lane = lax.broadcasted_iota(jnp.int32, (1, PAIR), 1)
    low = (lane < HEAD_DIM).astype(F32).astype(BF16)
    high = (lane >= HEAD_DIM).astype(F32).astype(BF16)
    return low, high


def attend_forward(packed, rows, width, out, total, bias):
    masks = half_masks()
    count = rows.stop - rows.start
    lane = lax.broadcasted_iota(jnp.int32, (1, PAIR), 1)
    sums = jnp.zeros((count, PAIR), F32)
    for pair in range(width // PAIR):
        at = pair * PAIR
        queries = packed[rows, at : at + PAIR]
        keys = packed[rows, width + at : width + at + PAIR]
        values = packed[rows, 2 * width + at : 2 * width + at + PAIR]
        blended = []
        for side in range(2):
            scores = dot(queries * masks[side], keys, NT) * (SCALE * LOG2E)
            if bias is not None:
                scores = scores + bias
            highest = jnp.max(scores, -1, keepdims=True)
            shares = jnp.exp2(scores - highest)
            weight = jnp.sum(shares, -1, keepdims=True)
            blended.append(dot(shares.astype(BF16), values) * (1.0 / weight))
            sums = jnp.where(lane == 2 * pair + side, highest + jnp.log2(weight), sums)
        out[rows, at : at + PAIR] = jnp.where(lane < HEAD_DIM, blended[0], blended[1]).astype(BF16)
    total[rows, :] = sums


def attend_back(packed, rows, width, grad_out, total, bias, out):
    masks = half_masks()
    for pair in range(width // PAIR):
        at = pair * PAIR
        queries = packed[rows, at : at + PAIR]
        keys = packed[rows, width + at : width + at + PAIR]
        values = packed[rows, 2 * width + at : 2 * width + at + PAIR]
        upstream = grad_out[rows, at : at + PAIR]
        grad_q = grad_k = grad_v = 0.0
        for side in range(2):
            own_q = queries * masks[side]
            own_k = keys * masks[side]
            own_up = upstream * masks[side]
            head = 2 * pair + side
            scores = dot(own_q, keys, NT) * (SCALE * LOG2E)
            if bias is not None:
                scores = scores + bias
            shares = jnp.exp2(scores - total[rows, head : head + 1])
            grad_shares = dot(own_up, values, NT)
            weighted = shares * grad_shares
            inner = jnp.sum(weighted, -1, keepdims=True)
            grad_scores = (weighted - shares * inner).astype(BF16)
            grad_q += dot(grad_scores, own_k)
            grad_k += dot(grad_scores, own_q, TN)
            grad_v += dot(shares.astype(BF16), own_up, TN)
        out[rows, at : at + PAIR] = (grad_q * SCALE).astype(BF16)
        out[rows, width + at : width + at + PAIR] = (grad_k * SCALE).astype(BF16)
        out[rows, 2 * width + at : 2 * width + at + PAIR] = grad_v.astype(BF16)


def embed(raw, vectors, actions):
    raw = raw.astype(F32)
    masked = raw > SEEN
    return jnp.where(masked, vectors[7:8, :], raw) + actions, masked


def space_forward_kernel(x, act, vectors, w_qkv, packed, out, total):
    width = x.shape[-1]
    embedded, _ = embed(x[0], vectors, act[0])
    unit, _ = normalise(embedded)
    normed = (unit * vectors[0:1, :] + vectors[1:2, :]).astype(BF16)
    packed[0] = dot(normed, w_qkv[...]).astype(BF16)
    rows = slice(0, x.shape[1])
    attend_forward(packed.at[0], rows, width, out.at[0], total.at[0], None)


def time_forward_kernel(
    sub, x, o1, act, perm, bias, vectors, w_space_out, w_qkv, w_out, h1, h2, a2, packed, o2, total
):
    frames, places, width = x.shape
    count = frames * places
    raw = dot(perm[...], x[...].reshape(count, width))
    blended = dot(perm[...], o1[...].reshape(count, width)).astype(BF16)
    actions = jnp.broadcast_to(act[...][None], (places, frames, width)).reshape(count, width)
    embedded, _ = embed(raw, vectors, actions)
    after_space = embedded + dot(blended, w_space_out[...])
    h1[...] = after_space
    unit, _ = normalise(after_space)
    normed = (unit * vectors[2:3, :] + vectors[3:4, :]).astype(BF16)
    a2[...] = normed
    packed[...] = dot(normed, w_qkv[...]).astype(BF16)
    for start in range(0, count, sub):
        attend_forward(packed, slice(start, start + sub), width, o2, total, bias[...])
    h2[...] = after_space + dot(o2[...], w_out[...])


def feed_kernel(
    tile, h2, cot, vectors, b_up, w_up, w_down, result, z, dur, a3, r2, sums, bias_grad
):
    @pl.when(pl.program_id(0) == 0)
    def _():
        sums[...] = jnp.zeros_like(sums)
        bias_grad[...] = jnp.zeros_like(bias_grad)

    after = h2[...]
    unit, spread = normalise(after)
    gain = vectors[4:5, :]
    normed = (unit * gain + vectors[5:6, :]).astype(BF16)
    a3[...] = normed
    upstream_low = cot[...]
    c = 0.7978845608028654
    total = after + vectors[6:7, :]
    grad_normed = jnp.zeros_like(after)
    for at in range(0, w_up.shape[1], tile):
        cols = slice(at, at + tile)
        hidden = dot(normed, w_up[:, cols]) + b_up[:, cols]
        grad_active = dot(upstream_low, w_down[cols, :], NT)
        square = hidden * hidden
        gate = 0.5 * jnp.tanh(hidden * (c + (c * 0.044715) * square)) + 0.5
        active = hidden * gate
        slope = gate + active * (1.0 - gate) * (2.0 * c + (6.0 * c * 0.044715) * square)
        grad_hidden = grad_active * slope
        bias_grad[:, cols] += jnp.sum(grad_hidden, 0, keepdims=True)
        active = active.astype(BF16)
        grad_hidden = grad_hidden.astype(BF16)
        z[:, cols] = active
        dur[:, cols] = grad_hidden
        total = total + dot(active, w_down[cols, :])
        grad_normed = grad_normed + dot(grad_hidden, w_up[:, cols], NT)
    result[...] = total.astype(BF16)
    upstream = upstream_low.astype(F32)
    r2[...] = upstream + norm_back(unit, spread, gain, grad_normed)
    sums[0:1, :] += jnp.sum(grad_normed * unit, 0, keepdims=True)
    sums[1:2, :] += jnp.sum(grad_normed, 0, keepdims=True)
    sums[2:3, :] += jnp.sum(upstream, 0, keepdims=True)


def time_back_kernel(
    sub, r2, h1, packed, total, perm, bias, vectors, w_out, w_qkv, grad_packed, r2_low, r1, sums, grad_out
):
    @pl.when(pl.program_id(0) == 0)
    def _():
        sums[...] = jnp.zeros_like(sums)

    count, width = r2.shape
    stream = r2[...]
    low = stream.astype(BF16)
    r2_low[...] = low
    grad_out[...] = dot(low, w_out[...], NT).astype(BF16)
    for start in range(0, count, sub):
        attend_back(
            packed, slice(start, start + sub), width, grad_out, total, bias[...], grad_packed
        )
    grad_normed = dot(grad_packed[...], w_qkv[...], NT)
    unit, spread = normalise(h1[...])
    stream = stream + norm_back(unit, spread, vectors[2:3, :], grad_normed)
    sums[0:1, :] += jnp.sum(grad_normed * unit, 0, keepdims=True)
    sums[1:2, :] += jnp.sum(grad_normed, 0, keepdims=True)
    r1[...] = dot(perm[...], stream.astype(BF16)).astype(BF16).reshape(r1.shape)


def space_back_kernel(
    r1, x, act, packed, total, vectors, w_out, w_qkv, grad_packed, a1, input_grad, frame_sum, sums, grad_out
):
    @pl.when(pl.program_id(0) == 0)
    def _():
        sums[...] = jnp.zeros_like(sums)

    count, width = x.shape[1:]
    grad_out[...] = dot(r1[0], w_out[...], NT).astype(BF16)
    attend_back(
        packed.at[0], slice(0, count), width, grad_out, total.at[0], None, grad_packed.at[0]
    )
    grad_normed = dot(grad_packed[0], w_qkv[...], NT)
    embedded, masked = embed(x[0], vectors, act[0])
    unit, spread = normalise(embedded)
    gain = vectors[0:1, :]
    a1[0] = (unit * gain + vectors[1:2, :]).astype(BF16)
    stream = r1[0].astype(F32) + norm_back(unit, spread, gain, grad_normed)
    kept = jnp.where(masked, 0.0, stream)
    input_grad[0] = kept.astype(BF16)
    whole_sum = jnp.sum(stream, 0, keepdims=True)
    frame_sum[0] = whole_sum
    sums[0:1, :] += jnp.sum(grad_normed * unit, 0, keepdims=True)
    sums[1:2, :] += jnp.sum(grad_normed, 0, keepdims=True)
    sums[2:3, :] += whole_sum - jnp.sum(kept, 0, keepdims=True)


def whole(array):
    rank = len(array.shape)
    return pl.BlockSpec(array.shape, lambda *_: (0,) * rank, pipeline_mode=pl.Buffered(1))


def struct(shape, kind):
    return jax.ShapeDtypeStruct(shape, kind)


def call(kernel, grid, operands, outs, scratch=(), flops=0):
    in_specs = [
        whole(array) if block is None else pl.BlockSpec(block, index)
        for array, block, index in operands
    ]
    out_specs = [
        pl.BlockSpec(shape, lambda *_, rank=len(shape): (0,) * rank)
        if block is None
        else pl.BlockSpec(block, index)
        for shape, _, block, index in outs
    ]
    moved = sum(a.size * a.dtype.itemsize for a, _, _ in operands)
    return pl.pallas_call(
        kernel,
        grid=grid,
        in_specs=in_specs,
        out_specs=out_specs,
        out_shape=[struct(shape, kind) for shape, kind, _, _ in outs],
        scratch_shapes=scratch,
        cost_estimate=pl.CostEstimate(flops=flops, bytes_accessed=2 * moved, transcendentals=0),
        compiler_params=pltpu.CompilerParams(vmem_limit_bytes=VMEM_LIMIT),
    )(*[a for a, _, _ in operands])


def weight_grad_kernel(left, right, out):
    out[...] = dot(left[...], right[...], TN).astype(out.dtype)


def weight_grad(left, right, tile=512):
    depth, height = left.shape
    width = right.shape[1]
    flops = 2 * depth * height * width
    if height > width:
        operands = [(left, (depth, tile), lambda i: (0, i)), (right, None, None)]
        out = [((height, width), BF16, (tile, width), lambda i: (i, 0))]
        steps = height // tile
    else:
        operands = [(left, None, None), (right, (depth, tile), lambda i: (0, i))]
        out = [((height, width), BF16, (height, tile), lambda i: (0, i))]
        steps = width // tile
    return call(weight_grad_kernel, (steps,), operands, out, flops=flops)[0]


def body(
    tokens,
    mask_bits,
    action_ids,
    vectors,
    action_table,
    w_space_qkv,
    w_space_out,
    w_time_qkv,
    w_time_out,
    w_up,
    b_up,
    w_down,
    cotangent,
):
    p, clips, frames, width = tokens.shape
    n = lax.axis_size("tile")
    me = lax.axis_index("tile")
    group = n // clips
    own_frames = frames // group
    grid_all = n * p
    places = grid_all // group
    clip, part = me // group, me % group
    hidden = w_up.shape[1]
    rows = places * frames

    def swap(value, k):
        return lax.ppermute(value, "tile", [(i, i ^ k) for i in range(n)])

    def row_block(*shape):
        return shape, lambda i: (i,) + (0,) * (len(shape) - 1)

    order = [k for j in range(group) for k in range(j, n, group)]
    onehot = (action_ids[..., None] == lax.iota(jnp.int32, action_table.shape[0])).astype(F32)
    action_rows = jnp.einsum("cfa,ad->cfd", onehot, action_table, precision=lax.Precision.HIGHEST)
    act_time = lax.dynamic_index_in_dim(action_rows, clip, 0, keepdims=False)
    act_space = lax.dynamic_slice_in_dim(act_time, part * own_frames, own_frames, 0)[:, None, :]

    marked = jnp.where((mask_bits > 0)[..., None], jnp.asarray(MASKED, BF16), tokens)
    marked = marked.reshape(p, n, own_frames, width)
    pieces = []
    for k in order:
        piece = lax.dynamic_index_in_dim(marked, me ^ k, 1, keepdims=False).transpose(1, 0, 2)
        pieces.append(piece if k == 0 else swap(piece, k))
    x_space = jnp.concatenate(pieces, 1)

    cot_pieces = []
    for j in range(n // group):
        piece = lax.dynamic_index_in_dim(cotangent, clip ^ j, 1, keepdims=False)
        cot_pieces.append(piece if j == 0 else swap(piece, j * group))
    cot = jnp.concatenate(cot_pieces, 0).reshape(rows, width)

    head_flops = 2 * HEADS * HEAD_DIM
    frame_block = lambda *shape: ((1,) + shape, lambda i: (i, 0, 0))
    packed_one, o1, total_one = call(
        space_forward_kernel,
        (own_frames,),
        [
            (x_space, *frame_block(grid_all, width)),
            (act_space, *frame_block(1, width)),
            (vectors, None, None),
            (w_space_qkv, None, None),
        ],
        [
            ((own_frames, grid_all, 3 * width), BF16, *frame_block(grid_all, 3 * width)),
            ((own_frames, grid_all, width), BF16, *frame_block(grid_all, width)),
            ((own_frames, grid_all, PAIR), F32, *frame_block(grid_all, PAIR)),
        ],
        flops=2 * own_frames * grid_all * width * 3 * width
        + 8 * own_frames * grid_all * grid_all * head_flops,
    )

    def to_time(value):
        return jnp.concatenate(
            [
                value[:, :places] if j == 0 else swap(value[:, j * places : (j + 1) * places], j)
                for j in range(group)
            ],
            0,
        )

    def to_space(value):
        return jnp.concatenate(
            [
                value[:own_frames]
                if j == 0
                else swap(value[j * own_frames : (j + 1) * own_frames], j)
                for j in range(group)
            ],
            1,
        )

    x_time, o1_time = to_time(x_space), to_time(o1)

    block = 16
    count = block * frames
    sub = min(count, 128)
    index = lax.iota(jnp.int32, count)
    slot, place = index // block, index % block
    frame_of_slot = ((part ^ (slot // own_frames)) * own_frames) + slot % own_frames
    target = place * frames + frame_of_slot
    perm_back = (target[:, None] == index[None, :]).astype(BF16)
    perm = (index[:, None] == target[None, :]).astype(BF16)
    seq = lax.iota(jnp.int32, sub)
    same = (seq[:, None] // frames) == (seq[None, :] // frames)
    bias = jnp.where(same & (seq[:, None] >= seq[None, :]), 0.0, NEGATIVE).astype(F32)

    slot_block = ((frames, block, width), lambda i: (0, i, 0))
    h1, h2, a2, packed_two, o2, total_two = call(
        lambda *refs: time_forward_kernel(sub, *refs),
        (places // block,),
        [
            (x_time, *slot_block),
            (o1_time, *slot_block),
            (act_time, None, None),
            (perm, None, None),
            (bias, None, None),
            (vectors, None, None),
            (w_space_out, None, None),
            (w_time_qkv, None, None),
            (w_time_out, None, None),
        ],
        [
            ((rows, width), F32, *row_block(count, width)),
            ((rows, width), F32, *row_block(count, width)),
            ((rows, width), BF16, *row_block(count, width)),
            ((rows, 3 * width), BF16, *row_block(count, 3 * width)),
            ((rows, width), BF16, *row_block(count, width)),
            ((rows, PAIR), F32, *row_block(count, PAIR)),
        ],
        flops=2 * rows * width * 5 * width + 8 * rows * sub * head_flops,
    )

    step = min(rows, 256)
    result, z, dur, a3, r2, sums_three, bias_up = call(
        lambda *refs: feed_kernel(1024, *refs),
        (rows // step,),
        [
            (h2, *row_block(step, width)),
            (cot, *row_block(step, width)),
            (vectors, None, None),
            (b_up[None, :], None, None),
            (w_up, None, None),
            (w_down, None, None),
        ],
        [
            ((rows, width), BF16, *row_block(step, width)),
            ((rows, hidden), BF16, *row_block(step, hidden)),
            ((rows, hidden), BF16, *row_block(step, hidden)),
            ((rows, width), BF16, *row_block(step, width)),
            ((rows, width), F32, *row_block(step, width)),
            ((8, width), F32, None, None),
            ((1, hidden), F32, None, None),
        ],
        flops=8 * rows * width * hidden,
    )

    result = result.reshape(n // group, p, 1, frames, width)
    result_out = jnp.zeros(tokens.shape, BF16)
    for j in range(n // group):
        piece = result[j] if j == 0 else swap(result[j], j * group)
        result_out = lax.dynamic_update_slice_in_dim(result_out, piece, clip ^ j, 1)

    down = weight_grad(z, cot)
    up = weight_grad(a3, dur)

    grad_packed_two, r2_low, r1_time, sums_two = call(
        lambda *refs: time_back_kernel(sub, *refs),
        (places // block,),
        [
            (r2, *row_block(count, width)),
            (h1, *row_block(count, width)),
            (packed_two, *row_block(count, 3 * width)),
            (total_two, *row_block(count, PAIR)),
            (perm_back, None, None),
            (bias, None, None),
            (vectors, None, None),
            (w_time_out, None, None),
            (w_time_qkv, None, None),
        ],
        [
            ((rows, 3 * width), BF16, *row_block(count, 3 * width)),
            ((rows, width), BF16, *row_block(count, width)),
            ((frames, places, width), BF16, *slot_block),
            ((8, width), F32, None, None),
        ],
        [pltpu.VMEM((count, width), BF16)],
        flops=2 * rows * width * 4 * width + 20 * rows * sub * head_flops,
    )
    r1_space = to_space(r1_time)
    time_out = weight_grad(o2, r2_low)
    time_qkv = weight_grad(a2, grad_packed_two)

    grad_packed_one, a1, input_low, frame_sums, sums_one = call(
        space_back_kernel,
        (own_frames,),
        [
            (r1_space, *frame_block(grid_all, width)),
            (x_space, *frame_block(grid_all, width)),
            (act_space, *frame_block(1, width)),
            (packed_one, *frame_block(grid_all, 3 * width)),
            (total_one, *frame_block(grid_all, PAIR)),
            (vectors, None, None),
            (w_space_out, None, None),
            (w_space_qkv, None, None),
        ],
        [
            ((own_frames, grid_all, 3 * width), BF16, *frame_block(grid_all, 3 * width)),
            ((own_frames, grid_all, width), BF16, *frame_block(grid_all, width)),
            ((own_frames, grid_all, width), BF16, *frame_block(grid_all, width)),
            ((own_frames, 1, width), F32, *frame_block(1, width)),
            ((8, width), F32, None, None),
        ],
        [pltpu.VMEM((grid_all, width), BF16)],
        flops=2 * rows * width * 4 * width + 20 * rows * grid_all * head_flops,
    )

    input_grad = jnp.zeros((p, n, own_frames, width), BF16)
    for slot_index, k in enumerate(order):
        piece = input_low[:, slot_index * p : (slot_index + 1) * p]
        piece = piece if k == 0 else swap(piece, k)
        input_grad = lax.dynamic_update_slice_in_dim(
            input_grad, piece.transpose(1, 0, 2)[:, None], me ^ k, 1
        )
    input_grad = input_grad.reshape(tokens.shape)

    space_out = weight_grad(o1.reshape(rows, width), r1_space.reshape(rows, width))
    space_qkv = weight_grad(a1.reshape(rows, width), grad_packed_one.reshape(rows, 3 * width))

    own_hot = lax.dynamic_slice_in_dim(
        lax.dynamic_index_in_dim(onehot, clip, 0, keepdims=False), part * own_frames, own_frames, 0
    )
    grad_table = jnp.einsum("fa,fd->ad", own_hot, frame_sums[:, 0], precision=lax.Precision.HIGHEST)
    grad_vectors = jnp.concatenate(
        [sums_one[0:2], sums_two[0:2], sums_three[0:3], sums_one[2:3]], 0
    )
    small = jnp.concatenate([grad_vectors, grad_table, bias_up.reshape(-1, width)], 0)
    small = lax.psum(small, ("clip", "tile"))
    count_v, count_t = grad_vectors.shape[0], grad_table.shape[0]

    def scatter(partial):
        summed = lax.psum_scatter(partial, ("clip", "tile"), scatter_dimension=0, tiled=True)
        return summed.astype(F32)

    return (
        result_out,
        input_grad,
        small[:count_v],
        small[count_v : count_v + count_t],
        scatter(space_qkv),
        scatter(space_out),
        scatter(time_qkv),
        scatter(time_out),
        scatter(up),
        small[count_v + count_t :].reshape(hidden),
        scatter(down),
    )


def solution(mesh):
    spread = P("tile", "clip", None, None)
    rows = P(("clip", "tile"), None)
    return jax.shard_map(
        body,
        mesh=mesh,
        in_specs=(spread, P("tile", "clip", None), P("clip", None)) + (P(),) * 9 + (spread,),
        out_specs=(spread, spread, P(), P(), rows, rows, rows, rows, rows, P(), rows),
        check_vma=False,
    )
```

```python
import jax
import jax.numpy as jnp
from jax import lax
from jax.experimental import pallas as pl
from jax.experimental.pallas import tpu as pltpu
from jax.sharding import PartitionSpec as P

HEADS = 16
HEAD_DIM = 64
PAIR = 2 * HEAD_DIM
EPSILON = 1e-05
NEGATIVE = -1e30
MASKED = 2.0**100
SEEN = 2.0**99
LOG2E = 1.4426950408889634
SCALE = HEAD_DIM**-0.5
F32 = jnp.float32
BF16 = jnp.bfloat16
VMEM_LIMIT = 60 * 1024 * 1024

NN = (((1,), (0,)), ((), ()))
NT = (((1,), (1,)), ((), ()))
TN = (((0,), (0,)), ((), ()))


def dot(left, right, form=NN):
    return lax.dot_general(left, right, form, preferred_element_type=F32)


def normalise(values):
    centred = values - jnp.mean(values, -1, keepdims=True)
    spread = lax.rsqrt(jnp.mean(centred * centred, -1, keepdims=True) + EPSILON)
    return centred * spread, spread


def norm_back(unit, spread, gain, upstream):
    scaled = upstream * gain
    return spread * (
        scaled
        - jnp.mean(scaled, -1, keepdims=True)
        - unit * jnp.mean(scaled * unit, -1, keepdims=True)
    )


def half_masks():
    lane = lax.broadcasted_iota(jnp.int32, (1, PAIR), 1)
    low = (lane < HEAD_DIM).astype(F32).astype(BF16)
    high = (lane >= HEAD_DIM).astype(F32).astype(BF16)
    return low, high


def pair_slices(packed, rows, width, pair):
    at = pair * PAIR
    return [packed[rows, part * width + at : part * width + at + PAIR] for part in range(3)]


def pair_slices(packed, rows, width, pair):
    at = pair * PAIR
    return [packed[rows, part * width + at : part * width + at + PAIR] for part in range(3)]


def attend_forward(packed, rows, width, out, total, bias, batch):
    masks = half_masks()
    lane = lax.broadcasted_iota(jnp.int32, (1, PAIR), 1)
    pairs = width // PAIR
    for first in range(0, pairs, batch):
        group = range(first, min(first + batch, pairs))
        loaded = [pair_slices(packed, rows, width, pair) for pair in group]
        scores = [
            dot(keys, queries * masks[side], NT) * (SCALE * LOG2E)
            for queries, keys, _ in loaded
            for side in range(2)
        ]
        if bias is not None:
            scores = [value + bias for value in scores]
        highest = [jnp.max(value, 0, keepdims=True) for value in scores]
        shares = [jnp.exp2(value - top) for value, top in zip(scores, highest)]
        weights = [jnp.sum(value, 0, keepdims=True) for value in shares]
        shares = [(value * (1.0 / weight)).astype(BF16) for value, weight in zip(shares, weights)]
        blended = [dot(value, loaded[i // 2][2], TN) for i, value in enumerate(shares)]
        total[2 * first : 2 * group.stop, rows] = jnp.concatenate(
            [top + jnp.log2(weight) for top, weight in zip(highest, weights)], 0
        )
        for i, pair in enumerate(group):
            out[rows, pair * PAIR : (pair + 1) * PAIR] = jnp.where(
                lane < HEAD_DIM, blended[2 * i], blended[2 * i + 1]
            ).astype(BF16)


def attend_forward_rows(packed, rows, width, out, total, batch):
    masks = half_masks()
    lane = lax.broadcasted_iota(jnp.int32, (1, PAIR), 1)
    pairs = width // PAIR
    for first in range(0, pairs, batch):
        group = range(first, min(first + batch, pairs))
        loaded = [pair_slices(packed, rows, width, pair) for pair in group]
        scores = [
            dot(queries * masks[side], keys, NT) * (SCALE * LOG2E)
            for queries, keys, _ in loaded
            for side in range(2)
        ]
        ones = [jnp.concatenate([v, jnp.ones_like(v)], 1) for _, _, v in loaded]
        highest = [jnp.max(value, 1, keepdims=True) for value in scores]
        shares = [jnp.exp2(value - top).astype(BF16) for value, top in zip(scores, highest)]
        blended = [dot(value, ones[i // 2]) for i, value in enumerate(shares)]
        sums = [b[:, PAIR:] for b in blended]
        blended = [b[:, :PAIR] * (1.0 / w) for b, w in zip(blended, sums)]
        logs = [top + jnp.log2(w) for top, w in zip(highest, sums)]
        for i, pair in enumerate(group):
            lg = jnp.where(lane < HEAD_DIM, logs[2*i], logs[2*i+1]).T
            total[2 * pair : 2 * pair + 1, rows] = lg[0:1]
            total[2 * pair + 1: 2 * pair + 2, rows] = lg[HEAD_DIM:HEAD_DIM+1]
            out[rows, pair * PAIR : (pair + 1) * PAIR] = jnp.where(
                lane < HEAD_DIM, blended[2 * i], blended[2 * i + 1]
            ).astype(BF16)


def attend_back(packed, rows, width, grad_out, total, bias, out, batch):
    masks = half_masks()
    pairs = width // PAIR
    for first in range(0, pairs, batch):
        group = range(first, min(first + batch, pairs))
        loaded = [pair_slices(packed, rows, width, pair) for pair in group]
        upstream = [grad_out[rows, pair * PAIR : (pair + 1) * PAIR] for pair in group]
        heads = [(i, side) for i in range(len(group)) for side in range(2)]
        own_q = [loaded[i][0] * masks[side] for i, side in heads]
        own_k = [loaded[i][1] * masks[side] for i, side in heads]
        own_up = [upstream[i] * masks[side] for i, side in heads]
        scores = [dot(loaded[i][1], own, NT) * (SCALE * LOG2E) for (i, _), own in zip(heads, own_q)]
        grad_shares = [dot(loaded[i][2], own, NT) for (i, _), own in zip(heads, own_up)]
        if bias is not None:
            scores = [value + bias for value in scores]
        sums = total[2 * first : 2 * group.stop, rows]
        shares = [jnp.exp2(value - sums[i : i + 1]) for i, value in enumerate(scores)]
        weighted = [value * grad for value, grad in zip(shares, grad_shares)]
        inner = [jnp.sum(value, 0, keepdims=True) for value in weighted]
        grad_scores = [
            (value - share * total_inner).astype(BF16)
            for value, share, total_inner in zip(weighted, shares, inner)
        ]
        grad_q = [dot(value, own, TN) for value, own in zip(grad_scores, own_k)]
        grad_k = [dot(value, own) for value, own in zip(grad_scores, own_q)]
        grad_v = [dot(value.astype(BF16), own) for value, own in zip(shares, own_up)]
        for i, pair in enumerate(group):
            at = pair * PAIR
            for part, (grad, scale) in enumerate(((grad_q, SCALE), (grad_k, SCALE), (grad_v, 1.0))):
                out[rows, part * width + at : part * width + at + PAIR] = (
                    (grad[2 * i] + grad[2 * i + 1]) * scale
                ).astype(BF16)


def embed(raw, vectors, actions):
    raw = raw.astype(F32)
    masked = raw > SEEN
    return jnp.where(masked, vectors[7:8, :], raw) + actions, masked


def space_forward_kernel(group, pieces, *refs):
    xs, (act, vectors, w_qkv, packed, out, total, *parts) = refs[:pieces], refs[pieces:]
    raw = jnp.concatenate([x[0] for x in xs], 0) if pieces > 1 else xs[0][0]
    count, width = raw.shape
    embedded, _ = embed(raw, vectors, act[0])
    unit, _ = normalise(embedded)
    normed = (unit * vectors[0:1, :] + vectors[1:2, :]).astype(BF16)
    packed[0] = dot(normed, w_qkv[...]).astype(BF16)
    attend_forward_rows(packed.at[0], slice(0, count), width, out.at[0], total.at[0], 4)
    share = count // group
    for j in range(group):
        parts[j][0, 0] = raw[j * share : (j + 1) * share]
        parts[j][0, 1] = out[0, j * share : (j + 1) * share]


def time_forward_kernel(sub, pieces, *refs):
    xs, o1s, refs = refs[:pieces], refs[pieces : 2 * pieces], refs[2 * pieces :]
    (act, perm, bias, vectors, w_space_out, w_qkv, w_out, h1, h2, a2, packed, o2, total) = refs
    x = jnp.concatenate([value[...] for value in xs], 0)
    o1 = jnp.concatenate([value[...] for value in o1s], 0)
    frames, places, width = x.shape
    count = frames * places
    raw = dot(perm[...], x.reshape(count, width))
    blended = dot(perm[...], o1.reshape(count, width)).astype(BF16)
    actions = jnp.broadcast_to(act[...][None], (places, frames, width)).reshape(count, width)
    embedded, _ = embed(raw, vectors, actions)
    after_space = embedded + dot(blended, w_space_out[...])
    h1[...] = after_space
    unit, _ = normalise(after_space)
    normed = (unit * vectors[2:3, :] + vectors[3:4, :]).astype(BF16)
    a2[...] = normed
    packed[...] = dot(normed, w_qkv[...]).astype(BF16)
    for start in range(0, count, sub):
        attend_forward(packed, slice(start, start + sub), width, o2, total, bias[...], 8)
    h2[...] = after_space + dot(o2[...], w_out[...])


def feed_kernel(tile, pieces, per, h2, *refs):
    cots, (vectors, b_up, w_up, w_down), refs = refs[:pieces], refs[pieces : pieces + 4], refs[pieces + 4 :]
    results, (cot, z, dur, a3, r2, sums, bias_grad) = refs[:pieces], refs[pieces:]
    piece = pl.program_id(0) // per
    for j in range(pieces):

        @pl.when(piece == j)
        def _(j=j):
            cot[...] = cots[j][...]

    @pl.when(pl.program_id(0) == 0)
    def _():
        sums[...] = jnp.zeros_like(sums)
        bias_grad[...] = jnp.zeros_like(bias_grad)

    after = h2[...]
    unit, spread = normalise(after)
    gain = vectors[4:5, :]
    normed = (unit * gain + vectors[5:6, :]).astype(BF16)
    a3[...] = normed
    upstream_low = cot[...]
    c = 0.7978845608028654
    total = after + vectors[6:7, :]
    grad_normed = jnp.zeros_like(after)
    for at in range(0, w_up.shape[1], tile):
        cols = slice(at, at + tile)
        hidden = dot(normed, w_up[:, cols]) + b_up[:, cols]
        grad_active = dot(upstream_low, w_down[cols, :], NT)
        square = hidden * hidden
        gate = 0.5 * jnp.tanh(hidden * (c + (c * 0.044715) * square)) + 0.5
        active = hidden * gate
        slope = gate + active * (1.0 - gate) * (2.0 * c + (6.0 * c * 0.044715) * square)
        grad_hidden = grad_active * slope
        bias_grad[:, cols] += jnp.sum(grad_hidden, 0, keepdims=True)
        active = active.astype(BF16)
        grad_hidden = grad_hidden.astype(BF16)
        z[:, cols] = active
        dur[:, cols] = grad_hidden
        total = total + dot(active, w_down[cols, :])
        grad_normed = grad_normed + dot(grad_hidden, w_up[:, cols], NT)
    for j in range(pieces):

        @pl.when(piece == j)
        def _(j=j):
            results[j][...] = total.astype(BF16)

    upstream = upstream_low.astype(F32)
    r2[...] = upstream + norm_back(unit, spread, gain, grad_normed)
    sums[0:1, :] += jnp.sum(grad_normed * unit, 0, keepdims=True)
    sums[1:2, :] += jnp.sum(grad_normed, 0, keepdims=True)
    sums[2:3, :] += jnp.sum(upstream, 0, keepdims=True)


def time_back_kernel(
    sub, r2, h1, packed, total, perm, bias, vectors, w_out, w_qkv, grad_packed, r2_low, sums, *rest
):
    *r1s, grad_out = rest

    @pl.when(pl.program_id(0) == 0)
    def _():
        sums[...] = jnp.zeros_like(sums)

    count, width = r2.shape
    stream = r2[...]
    low = stream.astype(BF16)
    r2_low[...] = low
    grad_out[...] = dot(low, w_out[...], NT).astype(BF16)
    for start in range(0, count, sub):
        attend_back(
            packed, slice(start, start + sub), width, grad_out, total, bias[...], grad_packed, 8
        )
    grad_normed = dot(grad_packed[...], w_qkv[...], NT)
    unit, spread = normalise(h1[...])
    stream = stream + norm_back(unit, spread, vectors[2:3, :], grad_normed)
    sums[0:1, :] += jnp.sum(grad_normed * unit, 0, keepdims=True)
    sums[1:2, :] += jnp.sum(grad_normed, 0, keepdims=True)
    r1 = dot(perm[...], stream.astype(BF16)).astype(BF16).reshape(-1, r1s[0].shape[1], width)
    share = r1s[0].shape[0]
    for j, piece in enumerate(r1s):
        piece[...] = r1[j * share : (j + 1) * share]


def space_back_kernel(pieces, group, dealt, *refs):
    xs, r1s, refs = refs[:pieces], refs[pieces : pieces + group], refs[pieces + group :]
    (act, packed, total, vectors, w_out, w_qkv) = refs[:6]
    (grad_packed, a1, r1_all, frame_sum, sums), refs = refs[6:11], refs[11:]
    input_grads, (grad_out,) = refs[:dealt], refs[dealt:]

    @pl.when(pl.program_id(0) == 0)
    def _():
        sums[...] = jnp.zeros_like(sums)

    raw = jnp.concatenate([x[0] for x in xs], 0) if pieces > 1 else xs[0][0]
    r1 = jnp.concatenate([value[0] for value in r1s], 0)
    r1_all[0] = r1
    count, width = raw.shape
    grad_out[...] = dot(r1, w_out[...], NT).astype(BF16)
    attend_back(
        packed.at[0], slice(0, count), width, grad_out, total.at[0], None, grad_packed.at[0], 4
    )
    grad_normed = dot(grad_packed[0], w_qkv[...], NT)
    embedded, masked = embed(raw, vectors, act[0])
    unit, spread = normalise(embedded)
    gain = vectors[0:1, :]
    a1[0] = (unit * gain + vectors[1:2, :]).astype(BF16)
    stream = r1.astype(F32) + norm_back(unit, spread, gain, grad_normed)
    kept = jnp.where(masked, 0.0, stream)
    share = count // dealt
    for j, input_grad in enumerate(input_grads):
        input_grad[0] = kept[j * share : (j + 1) * share].astype(BF16)
    whole_sum = jnp.sum(stream, 0, keepdims=True)
    frame_sum[0] = whole_sum
    sums[0:1, :] += jnp.sum(grad_normed * unit, 0, keepdims=True)
    sums[1:2, :] += jnp.sum(grad_normed, 0, keepdims=True)
    sums[2:3, :] += whole_sum - jnp.sum(kept, 0, keepdims=True)


def whole(array):
    rank = len(array.shape)
    return pl.BlockSpec(array.shape, lambda *_: (0,) * rank, pipeline_mode=pl.Buffered(1))


def struct(shape, kind):
    return jax.ShapeDtypeStruct(shape, kind)


def call(kernel, grid, operands, outs, scratch=(), flops=0, meta=None):
    in_specs = [
        whole(array) if block is None else pl.BlockSpec(block, index)
        for array, block, index in operands
    ]
    out_specs = [
        pl.BlockSpec(shape, lambda *_, rank=len(shape): (0,) * rank)
        if block is None
        else pl.BlockSpec(block, index)
        for shape, _, block, index in outs
    ]
    moved = sum(a.size * a.dtype.itemsize for a, _, _ in operands)
    return pl.pallas_call(
        kernel,
        grid_spec=pltpu.PrefetchScalarGridSpec(
            num_scalar_prefetch=0 if meta is None else 1,
            grid=grid,
            in_specs=in_specs,
            out_specs=out_specs,
            scratch_shapes=scratch,
        ),
        out_shape=[struct(shape, kind) for shape, kind, _, _ in outs],
        cost_estimate=pl.CostEstimate(flops=flops, bytes_accessed=2 * moved, transcendentals=0),
        compiler_params=pltpu.CompilerParams(vmem_limit_bytes=VMEM_LIMIT),
    )(*(() if meta is None else (meta,)), *[a for a, _, _ in operands])


def collect_kernel(parts, meta, *refs):
    *refs, perm, out, held = refs
    chip = pl.program_id(0)
    for i in range(len(refs) // (2 * parts)):

        @pl.when(chip == i)
        def _(i=i):
            found = [ref[...] for ref in refs[2 * parts * i : 2 * parts * (i + 1)]]
            held[...] = jnp.concatenate(found, 0).reshape(held.shape)

    out[...] = dot(perm[...], held[...]).astype(BF16).reshape(out.shape)


def collect(by_slot, chips, perm, shape):
    p, width = shape[0], shape[-1]
    block = 16
    steps = p // block
    parts = len(by_slot[0])
    span = sum(part.shape[0] for part in by_slot[0])
    count = len(by_slot)
    operands = []
    for k, pieces in enumerate(by_slot):

        def slot_index(i, h, meta, k=k):
            return 0, jnp.where(i == k // 2, h, jnp.where(i < k // 2, 0, steps - 1)), 0

        operands += [(piece, (piece.shape[0], block, width), slot_index) for piece in pieces]
    operands.append((perm, None, None))
    outs = [
        (
            (p, count * span, width),
            BF16,
            (block, 2 * span, width),
            lambda i, h, meta: (h, meta[i], 0),
        )
    ]
    return call(
        lambda *refs: collect_kernel(parts, *refs),
        (count // 2, steps),
        operands,
        outs,
        [pltpu.VMEM((block * 2 * span, width), BF16)],
        meta=chips,
    )[0].reshape(shape)


def collect_result_kernel(meta, *refs):
    *pieces, out = refs
    for j, piece in enumerate(pieces):

        @pl.when(pl.program_id(0) == j)
        def _(piece=piece):
            out[...] = piece[...]


def collect_result(pieces, where):
    p, _, frames, width = pieces[0].shape
    return call(
        collect_result_kernel,
        (len(pieces),),
        [(piece, None, None) for piece in pieces],
        [
            (
                (p, len(pieces), frames, width),
                BF16,
                (p, 1, frames, width),
                lambda j, meta: (0, meta[j], 0, 0),
            )
        ],
        meta=where,
    )[0]


def put(outs, slot, value):
    share = outs[0].shape[0]
    outs[slot // share][slot % share] = value


def columns_kernel(meta, *refs, counts, firsts, blocks, split, summed):
    step = pl.program_id(0)
    *refs, held = refs
    pairs = []
    for count in counts:
        pairs.append((refs[:count], refs[count : 2 * count]))
        refs = refs[2 * count :]
    received, outs = (refs[: len(split)], refs[len(split) :]) if summed else (None, refs)
    for i, (lefts, rights) in enumerate(pairs):

        @pl.when((step >= firsts[i]) & (step < firsts[i + 1]))
        def _(lefts=lefts, rights=rights):
            held[...] = sum(dot(l[...], r[...], TN) for l, r in zip(lefts, rights))

    size = held.shape[0] // blocks
    per = firsts[-1] // len(split)
    for share, two in enumerate(split):
        own, outs = outs[: 1 + two], outs[1 + two :]

        @pl.when(step // per == share)
        def _(share=share, own=own):
            for slot in range(blocks):
                source = meta[share * blocks + slot] * size
                value = held[pl.ds(pl.multiple_of(source, size), size), :]
                if summed:
                    value = value + received[share][slot].astype(F32)
                put(own, slot, value.astype(BF16))


def columns_grad(pairs, meta, received, split, tile=512):
    shares = len(split)
    blocks = (meta.shape[0] - 1) // shares
    height = pairs[0][0][0].shape[1]
    size = height // blocks
    tile = min([tile] + [rights[0].shape[1] // 2 for _, rights in pairs])
    steps = [rights[0].shape[1] // 2 // tile for _, rights in pairs]
    firsts = [sum(steps[:i]) for i in range(len(steps) + 1)]
    per = firsts[-1] // shares
    operands, flops = [], 0
    for (lefts, rights), first, count in zip(pairs, firsts, steps):
        operands += [(left, None, None) for left in lefts]
        for right in rights:

            def index(i, meta, first=first, count=count):
                return 0, meta[shares * blocks] * count + jnp.clip(i - first, 0, count - 1)

            operands.append((right, (right.shape[0], tile), index))
            flops += right.size * height

    def share_block(rows, share):
        return (rows, size, tile), lambda i, meta: (0, 0, jnp.clip(i - share * per, 0, per - 1))

    for share, value in enumerate(received or ()):
        operands.append((value, *share_block(blocks, share)))
    outs = [
        ((blocks // (1 + two), size, per * tile), BF16, *share_block(blocks // (1 + two), share))
        for share, two in enumerate(split)
        for _ in range(1 + two)
    ]
    kernel = lambda *refs: columns_kernel(
        *refs,
        counts=[len(lefts) for lefts, _ in pairs],
        firsts=firsts,
        blocks=blocks,
        split=split,
        summed=received is not None,
    )
    return call(kernel, (firsts[-1],), operands, outs, [pltpu.VMEM((height, tile), F32)], flops, meta)


def rows_kernel(meta, *refs, step_blocks, steps, summed):
    step = pl.program_id(0)
    lefts, right, refs = refs[:step_blocks], refs[step_blocks], refs[step_blocks + 1 :]
    received, outs = (refs[0], refs[1:]) if summed else (None, refs)
    value = dot(jnp.concatenate([left[...] for left in lefts], 1), right[...], TN)
    value = value.reshape(step_blocks, -1, value.shape[-1])
    if summed:
        value = value + received[...].astype(F32)
    value = value.astype(BF16)
    share = steps // len(outs)
    for i, out in enumerate(outs):

        @pl.when((step >= i * share) & (step < (i + 1) * share))
        def _(out=out):
            out[...] = value


def rows_grad(left, right, meta, received, split, step_blocks=2):
    blocks = meta.shape[0] - 1
    depth, height = left.shape
    size, columns = height // blocks, right.shape[1] // 2
    steps = blocks // step_blocks
    operands = [
        (left, (depth, size), lambda i, meta, j=j: (0, meta[i * step_blocks + j]))
        for j in range(step_blocks)
    ]
    operands.append((right, (depth, columns), lambda i, meta: (0, meta[blocks])))
    if received is not None:
        operands.append((received[0], (step_blocks, size, columns), lambda i, meta: (i, 0, 0)))
    parts = 1 + split[0]
    share = steps // parts
    outs = [
        (
            (blocks // parts, size, columns),
            BF16,
            (step_blocks, size, columns),
            lambda i, meta, first=j * share: (jnp.clip(i - first, 0, share - 1), 0, 0),
        )
        for j in range(parts)
    ]
    kernel = lambda *refs: rows_kernel(
        *refs, step_blocks=step_blocks, steps=steps, summed=received is not None
    )
    return call(kernel, (steps,), operands, outs, flops=depth * height * 2 * columns, meta=meta)


def body(
    tokens,
    mask_bits,
    action_ids,
    vectors,
    action_table,
    w_space_qkv,
    w_space_out,
    w_time_qkv,
    w_time_out,
    w_up,
    b_up,
    w_down,
    cotangent,
):
    p, clips, frames, width = tokens.shape
    n, layers = lax.axis_size("tile"), lax.axis_size("clip")
    me, layer = lax.axis_index("tile"), lax.axis_index("clip")
    core = me % 2
    group = n // clips
    own_frames = frames // group
    grid_all = n * p
    places = grid_all // group
    clip, part = me // group, me % group
    hidden = w_up.shape[1]
    rows = places * frames

    def swap(value, k, axis="tile"):
        size = lax.axis_size(axis)
        return lax.ppermute(value, axis, [(i, i ^ k) for i in range(size)])

    def row_block(*shape):
        return shape, lambda i: (i,) + (0,) * (len(shape) - 1)

    blocks = n * layers // 2
    tile_bits = [1 << b for b in range(1, n.bit_length() - 1)]

    def orders(hops):
        xor, clip_xor, clip_at = [0], [0], [None]
        for hop in hops:
            if hop == "scatter":
                choices = [(0, 0, c) for c in range(layers)]
            elif hop[0] == "tile":
                choices = [(0, 0, None), (hop[1], 0, None)]
            else:
                choices = [(0, 0, None), (0, hop[1], None)]
            xor, clip_xor, clip_at = (
                [a ^ c[0] for a in xor for c in choices],
                [a ^ c[1] for a in clip_xor for c in choices],
                [a if c[2] is None else c[2] for a in clip_at for c in choices],
            )
        where = [
            (c if c is not None else layer ^ cx) * (n // 2) + (me ^ x) // 2
            for x, cx, c in zip(xor, clip_xor, clip_at)
        ]
        return jnp.stack([jnp.asarray(w, jnp.int32) for w in where])

    def meta_of(orders_of, half):
        return jnp.concatenate(orders_of + [jnp.asarray(half, jnp.int32)[None]])

    def begin(make, chains):
        found = [orders(hops) for hops in chains]
        sent = make(meta_of(found, 1 - core), None, [False] * len(chains))
        return make, chains, found, [swap(value, 1) for value in sent]

    def proceed(started):
        make, chains, found, received = started
        split = [hops[0] != "scatter" for hops in chains]
        made = make(meta_of(found, core), received, split)
        parts = []
        for two in split:
            parts.append(made[: 1 + two])
            made = made[1 + two :]
        return chains, parts, 0

    def halves(value, hop):
        if hop is None or hop == "scatter":
            return [value]
        middle = value.shape[0] // 2
        return [value[:middle], value[middle:]]

    def depart(state):
        chains, parts, at = state
        coming = []
        for hops, own in zip(chains, parts):
            hop = hops[at]
            if hop == "scatter":
                coming.append(lax.psum_scatter(own[0], "clip", scatter_dimension=0, tiled=True))
            else:
                coming.append(swap(own[1], hop[1], hop[0]))
        return state, coming

    def arrive(departed):
        (chains, parts, at), coming = departed
        new_parts = []
        for hops, own, came in zip(chains, parts, coming):
            following = hops[at + 1] if at + 1 < len(hops) else None
            kind = F32 if following is None else BF16
            if hops[at] == "scatter":
                new_parts.append(halves(came, following))
            else:
                new_parts.append(
                    [
                        (a.astype(F32) + b.astype(F32)).astype(kind)
                        for a, b in zip(halves(own[0], following), halves(came, following))
                    ]
                )
        return chains, new_parts, at + 1

    def last_swap(state):
        own = jnp.concatenate([own[0][0].astype(F32) for own in state[1]], 1)
        size = own.shape[0] // 2
        mine = lax.dynamic_slice_in_dim(own, core * size, size, 0)
        other = lax.dynamic_slice_in_dim(own, (1 - core) * size, size, 0)
        return mine, swap(other.astype(BF16), 1)

    def join(mine, other, widths):
        whole_parts, at = [], 0
        for w in widths:
            a, b = mine[:, at : at + w // 2], other[:, at : at + w // 2].astype(F32)
            whole_parts.append(
                jnp.where(core == 0, jnp.concatenate([a, b], 1), jnp.concatenate([b, a], 1))
            )
            at += w // 2
        return whole_parts

    order = [k for j in range(group) for k in range(j, n, group)]
    onehot = (action_ids[..., None] == lax.iota(jnp.int32, action_table.shape[0])).astype(F32)
    action_rows = jnp.einsum("cfa,ad->cfd", onehot, action_table, precision=lax.Precision.HIGHEST)
    act_time = lax.dynamic_index_in_dim(action_rows, clip, 0, keepdims=False)
    act_space = lax.dynamic_slice_in_dim(act_time, part * own_frames, own_frames, 0)[:, None, :]

    regular = p % 16 == 0 and 2 * own_frames == 16
    if regular:
        at = lax.iota(jnp.int32, 16 * 2 * own_frames)
        place, frame = at % 16, at // 16
        source = place * 2 * own_frames + (frame + core * own_frames) % (2 * own_frames)
        deal_back = (at[:, None] == source[None, :]).astype(BF16)
    marked = jnp.where((mask_bits > 0)[..., None], jnp.asarray(MASKED, BF16), tokens)
    marked = marked.reshape(p, n, own_frames, width)
    by_slot = [
        lax.dynamic_index_in_dim(marked, me ^ k, 1, keepdims=False).transpose(1, 0, 2)
        for k in range(n)
    ]
    pieces = [by_slot[k] if k == 0 else swap(by_slot[k], k) for k in order]
    if p % 16:
        pieces = [jnp.concatenate(pieces, 1)]

    cot_pieces = []
    for j in range(n // group):
        piece = lax.dynamic_index_in_dim(cotangent, clip ^ j, 1, keepdims=False)
        cot_pieces.append(piece if j == 0 else swap(piece, j * group))
    cot_pieces = [piece.reshape(p * frames, width) for piece in cot_pieces]

    head_flops = 2 * HEADS * HEAD_DIM
    chunks = 2
    span = own_frames // chunks

    def frame_block(*shape):
        return (1,) + shape, lambda i: (i, 0, 0)

    def chunk_block(first, *shape):
        return (1,) + shape, lambda i: (first + i, 0, 0)

    space, both = [], []
    for c in range(chunks):
        packed, o1, total, *parts = call(
            lambda *refs: space_forward_kernel(group, len(pieces), *refs),
            (span,),
            [(x, *chunk_block(c * span, *x.shape[1:])) for x in pieces]
            + [
                (act_space, *chunk_block(c * span, 1, width)),
                (vectors, None, None),
                (w_space_qkv, None, None),
            ],
            [
                ((span, grid_all, 3 * width), BF16, *frame_block(grid_all, 3 * width)),
                ((span, grid_all, width), BF16, *frame_block(grid_all, width)),
                ((span, HEADS, grid_all), F32, *frame_block(HEADS, grid_all)),
            ]
            + [
                (
                    (span, 2, places, width),
                    BF16,
                    (1, 2, places, width),
                    lambda i: (i, 0, 0, 0),
                )
            ]
            * group,
            flops=2 * span * grid_all * width * 3 * width
            + 16 * span * grid_all * grid_all * head_flops,
        )
        space.append((packed, o1, total))
        both.append([part if j == 0 else swap(part, j) for j, part in enumerate(parts)])
    both = [both[c][j] for j in range(group) for c in range(chunks)]

    block = 16
    count = block * frames
    sub = min(count, 128)
    index = lax.iota(jnp.int32, count)
    slot, place = index // block, index % block
    frame_of_slot = ((part ^ (slot // own_frames)) * own_frames) + slot % own_frames
    target = place * frames + frame_of_slot
    perm_back = (target[:, None] == index[None, :]).astype(BF16)
    perm = (index[:, None] == target[None, :]).astype(BF16)
    seq = lax.iota(jnp.int32, sub)
    same = (seq[:, None] // frames) == (seq[None, :] // frames)
    bias = jnp.where(same & (seq[:, None] <= seq[None, :]), 0.0, NEGATIVE).astype(F32)

    def slot_block(size):
        return (size, block, width), lambda i: (0, i, 0)

    total_block = ((HEADS, count), lambda i: (0, i))
    h1, h2, a2, packed_two, o2, total_two = call(
        lambda *refs: time_forward_kernel(sub, len(both), *refs),
        (places // block,),
        [
            (value, (span, None, block, width), lambda i, which=which: (0, which, i, 0))
            for which in range(2)
            for value in both
        ]
        + [
            (act_time, None, None),
            (perm, None, None),
            (bias, None, None),
            (vectors, None, None),
            (w_space_out, None, None),
            (w_time_qkv, None, None),
            (w_time_out, None, None),
        ],
        [
            ((rows, width), F32, *row_block(count, width)),
            ((rows, width), F32, *row_block(count, width)),
            ((rows, width), BF16, *row_block(count, width)),
            ((rows, 3 * width), BF16, *row_block(count, 3 * width)),
            ((rows, width), BF16, *row_block(count, width)),
            ((HEADS, rows), F32, *total_block),
        ],
        flops=2 * rows * width * 5 * width + 16 * rows * sub * head_flops,
    )

    step = min(p * frames, 256)
    per = p * frames // step

    def piece_block(j):
        return (step, width), lambda i, j=j: (jnp.clip(i - j * per, 0, per - 1), 0)

    *result_pieces, cot, z, dur, a3, r2, sums_three, bias_up = call(
        lambda *refs: feed_kernel(1024, len(cot_pieces), per, *refs),
        (rows // step,),
        [(h2, *row_block(step, width))]
        + [(piece, *piece_block(j)) for j, piece in enumerate(cot_pieces)]
        + [
            (vectors, None, None),
            (b_up[None, :], None, None),
            (w_up, None, None),
            (w_down, None, None),
        ],
        [((p * frames, width), BF16, *piece_block(j)) for j in range(len(cot_pieces))]
        + [
            ((rows, width), BF16, *row_block(step, width)),
            ((rows, hidden), BF16, *row_block(step, hidden)),
            ((rows, hidden), BF16, *row_block(step, hidden)),
            ((rows, width), BF16, *row_block(step, width)),
            ((rows, width), F32, *row_block(step, width)),
            ((8, width), F32, None, None),
            ((1, hidden), F32, None, None),
        ],
        flops=8 * rows * width * hidden,
    )

    result_pieces = [
        (piece if j == 0 else swap(piece, j * group)).reshape(p, 1, frames, width)
        for j, piece in enumerate(result_pieces)
    ]

    one_way = [("tile", bit) for bit in tile_bits]
    other_way = one_way[::-1]
    clip_bits = [("clip", 1 << b) for b in range(layers.bit_length() - 1)]

    def make_down(meta, received, split):
        if hidden // blocks % 128:
            return columns_grad([([z], [cot])], meta, received, split, 256)
        return rows_grad(z, cot, meta, received, split)

    def make_up(meta, received, split):
        return columns_grad([([a3], [dur])], meta, received, split)

    down = begin(make_down, [["scatter"] + one_way])
    up = begin(make_up, [one_way + clip_bits])
    down = proceed(down)
    up = proceed(up)
    r2, result_pieces, down, up = hold_parts(r2, result_pieces, down, up)
    down, up = depart(down), depart(up)

    grad_packed_two, r2_low, sums_two, *r1_parts = call(
        lambda *refs: time_back_kernel(sub, *refs),
        (places // block,),
        [
            (r2, *row_block(count, width)),
            (h1, *row_block(count, width)),
            (packed_two, *row_block(count, 3 * width)),
            (total_two, *total_block),
            (perm_back, None, None),
            (bias, None, None),
            (vectors, None, None),
            (w_time_out, None, None),
            (w_time_qkv, None, None),
        ],
        [
            ((rows, 3 * width), BF16, *row_block(count, 3 * width)),
            ((rows, width), BF16, *row_block(count, width)),
            ((8, width), F32, None, None),
        ]
        + [((own_frames, places, width), BF16, *slot_block(own_frames))] * group,
        [pltpu.VMEM((count, width), BF16)],
        flops=2 * rows * width * 4 * width + 40 * rows * sub * head_flops,
    )
    grad_packed_two, up = hold_parts(grad_packed_two, up)
    up = depart(arrive(up))
    r1_parts = [r1 if j == 0 else swap(r1, j) for j, r1 in enumerate(r1_parts)]

    def make_time(meta, received, split):
        return columns_grad([([a2], [grad_packed_two]), ([o2], [r2_low])], meta, received, split)

    time = begin(make_time, [["scatter"] + other_way])

    dealt = 1 if p % 16 else n

    def send_back(parts):
        if dealt == 1:
            parts = [parts[0][:, at * p : (at + 1) * p] for at in range(n)]
        return [part if k == 0 else swap(part, k) for k, part in zip(order, parts)]

    def space_back(c):
        packed, _, total = space[c]
        return call(
            lambda *refs: space_back_kernel(len(pieces), group, dealt, *refs),
            (span,),
            [(x, *chunk_block(c * span, *x.shape[1:])) for x in pieces]
            + [(r1, *chunk_block(c * span, places, width)) for r1 in r1_parts]
            + [
                (act_space, *chunk_block(c * span, 1, width)),
                (packed, *frame_block(grid_all, 3 * width)),
                (total, *frame_block(HEADS, grid_all)),
                (vectors, None, None),
                (w_space_out, None, None),
                (w_space_qkv, None, None),
            ],
            [
                ((span, grid_all, 3 * width), BF16, *frame_block(grid_all, 3 * width)),
                ((span, grid_all, width), BF16, *frame_block(grid_all, width)),
                ((span, grid_all, width), BF16, *frame_block(grid_all, width)),
                ((span, 1, width), F32, *frame_block(1, width)),
                ((8, width), F32, None, None),
            ]
            + [((span, grid_all // dealt, width), BF16, *frame_block(grid_all // dealt, width))]
            * dealt,
            [pltpu.VMEM((grid_all, width), BF16)],
            flops=2 * span * grid_all * width * 4 * width
            + 40 * span * grid_all * grid_all * head_flops,
        )

    back = [space_back(0)]
    input_pieces = [send_back(back[0][5:])]
    time, up = hold_parts(time, up)
    up = depart(arrive(up))
    time = proceed(time)
    r1_parts, time, up = hold_parts(r1_parts, time, up)
    time = depart(time)
    up = depart(arrive(up)) if up[0][2] + 1 < len(up[0][0][0]) else up
    for c in range(1, chunks):
        back.append(space_back(c))
        input_pieces.append(send_back(back[c][5:]))
    back[-1], input_pieces[0], up, down = hold_parts(back[-1], input_pieces[0], up, down)
    up = arrive(up)
    while up[2] < len(up[0][0]):
        up = arrive(depart(up))
    up = last_swap(up)
    down = depart(arrive(down))
    grads_one, a1s, r1s, frame_sums, sums_one = list(zip(*back))[:5]

    def flat(values):
        return [value.reshape(-1, value.shape[-1]) for value in values]

    def make_space(meta, received, split):
        return columns_grad(
            [
                (flat(a1s), flat(grads_one)),
                (flat([o1 for _, o1, _ in space]), flat(r1s)),
            ],
            meta,
            received,
            split,
        )

    space_sum = begin(make_space, [one_way + clip_bits, other_way + clip_bits])
    space_sum, down = hold_parts(space_sum, down)
    space_sum = proceed(space_sum)
    down = depart(arrive(down))

    sums_one, frame_sums = sum(sums_one), jnp.concatenate(frame_sums, 0)[:, 0]
    own_hot = lax.dynamic_slice_in_dim(
        lax.dynamic_index_in_dim(onehot, clip, 0, keepdims=False), part * own_frames, own_frames, 0
    )
    grad_table = jnp.einsum("fa,fd->ad", own_hot, frame_sums, precision=lax.Precision.HIGHEST)
    small = jnp.concatenate(
        [
            sums_one[:2],
            sums_two[:2],
            sums_three[:3],
            sums_one[2:3],
            grad_table,
            bias_up.reshape(-1, width),
        ],
        0,
    )
    count_t = 8 + action_table.shape[0]
    small_hops = [("tile", 1 << b) for b in range(n.bit_length() - 1)] + clip_bits

    space_sum, small, up, down = hold_parts(space_sum, small, up, down)
    down = arrive(down)
    while down[2] < len(down[0][0]):
        down = arrive(depart(down))
    down = last_swap(down)
    rounds = max(len(small_hops), len(space_sum[0][0]) + 1)
    for r in range(rounds):
        departed = depart(space_sum) if r < len(space_sum[0][0]) else None
        small_came = swap(small, small_hops[r][1], small_hops[r][0]) if r < len(small_hops) else None
        if r == 0:
            where_clip, space_sum = hold_parts(clip ^ lax.iota(jnp.int32, clips), space_sum)
            result_out = collect_result(result_pieces, where_clip)
            departed, small_came, result_out, down, up = hold_parts(
                departed, small_came, result_out, down, up
            )
        elif r == 1:
            time = depart(arrive(time))
            departed, small_came, input_pieces, time = hold_parts(
                departed, small_came, input_pieces, time
            )
            time = arrive(time)
        elif time[2] < len(time[0][0]):
            time = depart(time)
            departed, small_came, time = hold_parts(departed, small_came, time)
            time = arrive(time)
        else:
            departed, small_came = hold_parts(departed, small_came)
        if departed is not None:
            space_sum = arrive(departed)
        if small_came is not None:
            small = small + small_came
        if r + 1 == len(space_sum[0][0]):
            space_last = last_swap(space_sum)
    while time[2] < len(time[0][0]):
        time = arrive(depart(time))
    time = last_swap(time)

    where_chip = (me // 2) ^ lax.iota(jnp.int32, n // 2)
    by_source = [[pieces_of[at] for pieces_of in input_pieces] for at in range(n)]
    if regular:
        by_slot = [by_source[order.index(k)] for k in range(n)]
        input_grad = collect(by_slot, where_chip, deal_back, tokens.shape)
    else:
        input_grad = jnp.zeros((p, n, own_frames, width), BF16)
        for k, parts in zip(order, by_source):
            piece = jnp.concatenate(parts, 0).transpose(1, 0, 2)[:, None]
            input_grad = lax.dynamic_update_slice_in_dim(input_grad, piece, me ^ k, 1)
        input_grad = input_grad.reshape(tokens.shape)

    (down_out,) = join(*down, [width])
    (up_out,) = join(*up, [hidden])
    time_qkv, time_out = join(*time, [3 * width, width])
    space_qkv, space_out = join(*space_last, [3 * width, width])
    return (
        result_out,
        input_grad,
        small[:8],
        small[8:count_t],
        space_qkv,
        space_out,
        time_qkv,
        time_out,
        up_out,
        small[count_t:].reshape(hidden),
        down_out,
    )


def hold_parts(*values):
    leaves, tree = jax.tree.flatten(values)
    arrays = [i for i, leaf in enumerate(leaves) if isinstance(leaf, jax.Array)]
    held = lax.optimization_barrier([leaves[i] for i in arrays])
    for i, leaf in zip(arrays, held):
        leaves[i] = leaf
    return jax.tree.unflatten(tree, leaves)


def solution(mesh):
    spread = P("tile", "clip", None, None)
    rows = P(("clip", "tile"), None)
    return jax.shard_map(
        body,
        mesh=mesh,
        in_specs=(spread, P("tile", "clip", None), P("clip", None)) + (P(),) * 9 + (spread,),
        out_specs=(spread, spread, P(), P(), rows, rows, rows, rows, rows, P(), rows),
        check_vma=False,
    )
```

```python
import jax
import jax.numpy as jnp
from jax import lax
from jax.experimental import pallas as pl
from jax.experimental.pallas import tpu as pltpu
from jax.sharding import PartitionSpec as P

HEADS = 16
HEAD_DIM = 64
PAIR = 2 * HEAD_DIM
EPSILON = 1e-05
NEGATIVE = -1e30
MASKED = 2.0**100
SEEN = 2.0**99
LOG2E = 1.4426950408889634
SCALE = HEAD_DIM**-0.5
F32 = jnp.float32
BF16 = jnp.bfloat16
VMEM_LIMIT = 60 * 1024 * 1024

NN = (((1,), (0,)), ((), ()))
NT = (((1,), (1,)), ((), ()))
TN = (((0,), (0,)), ((), ()))


def dot(left, right, form=NN):
    return lax.dot_general(left, right, form, preferred_element_type=F32)


def normalise(values):
    centred = values - jnp.mean(values, -1, keepdims=True)
    spread = lax.rsqrt(jnp.mean(centred * centred, -1, keepdims=True) + EPSILON)
    return centred * spread, spread


def norm_back(unit, spread, gain, upstream):
    scaled = upstream * gain
    return spread * (
        scaled
        - jnp.mean(scaled, -1, keepdims=True)
        - unit * jnp.mean(scaled * unit, -1, keepdims=True)
    )


def half_masks():
    lane = lax.broadcasted_iota(jnp.int32, (1, PAIR), 1)
    low = (lane < HEAD_DIM).astype(F32).astype(BF16)
    high = (lane >= HEAD_DIM).astype(F32).astype(BF16)
    return low, high


def pair_slices(packed, rows, width, pair):
    at = pair * PAIR
    return [packed[rows, part * width + at : part * width + at + PAIR] for part in range(3)]


def pair_slices(packed, rows, width, pair):
    at = pair * PAIR
    return [packed[rows, part * width + at : part * width + at + PAIR] for part in range(3)]


def attend_forward(packed, rows, width, out, total, bias, batch):
    masks = half_masks()
    lane = lax.broadcasted_iota(jnp.int32, (1, PAIR), 1)
    pairs = width // PAIR
    for first in range(0, pairs, batch):
        group = range(first, min(first + batch, pairs))
        loaded = [pair_slices(packed, rows, width, pair) for pair in group]
        scores = [
            dot(keys, queries * masks[side], NT) * (SCALE * LOG2E)
            for queries, keys, _ in loaded
            for side in range(2)
        ]
        if bias is not None:
            scores = [value + bias for value in scores]
        highest = [jnp.max(value, 0, keepdims=True) for value in scores]
        shares = [jnp.exp2(value - top) for value, top in zip(scores, highest)]
        weights = [jnp.sum(value, 0, keepdims=True) for value in shares]
        shares = [(value * (1.0 / weight)).astype(BF16) for value, weight in zip(shares, weights)]
        blended = [dot(value, loaded[i // 2][2], TN) for i, value in enumerate(shares)]
        total[2 * first : 2 * group.stop, rows] = jnp.concatenate(
            [top + jnp.log2(weight) for top, weight in zip(highest, weights)], 0
        )
        for i, pair in enumerate(group):
            out[rows, pair * PAIR : (pair + 1) * PAIR] = jnp.where(
                lane < HEAD_DIM, blended[2 * i], blended[2 * i + 1]
            ).astype(BF16)


def attend_forward_rows(packed, rows, width, out, total, batch):
    masks = half_masks()
    lane = lax.broadcasted_iota(jnp.int32, (1, PAIR), 1)
    pairs = width // PAIR
    for first in range(0, pairs, batch):
        group = range(first, min(first + batch, pairs))
        loaded = [pair_slices(packed, rows, width, pair) for pair in group]
        scores = [
            dot(queries * masks[side], keys, NT) * (SCALE * LOG2E)
            for queries, keys, _ in loaded
            for side in range(2)
        ]
        ones = [jnp.concatenate([v, jnp.ones_like(v)], 1) for _, _, v in loaded]
        highest = [jnp.max(value, 1, keepdims=True) for value in scores]
        shares = [jnp.exp2(value - top).astype(BF16) for value, top in zip(scores, highest)]
        blended = [dot(value, ones[i // 2]) for i, value in enumerate(shares)]
        sums = [b[:, PAIR:] for b in blended]
        blended = [b[:, :PAIR] * (1.0 / w) for b, w in zip(blended, sums)]
        logs = [top + jnp.log2(w) for top, w in zip(highest, sums)]
        for i, pair in enumerate(group):
            lg = jnp.where(lane < HEAD_DIM, logs[2*i], logs[2*i+1]).T
            total[2 * pair : 2 * pair + 1, rows] = lg[0:1]
            total[2 * pair + 1: 2 * pair + 2, rows] = lg[HEAD_DIM:HEAD_DIM+1]
            out[rows, pair * PAIR : (pair + 1) * PAIR] = jnp.where(
                lane < HEAD_DIM, blended[2 * i], blended[2 * i + 1]
            ).astype(BF16)


def attend_back(packed, rows, width, grad_out, total, bias, out, batch):
    masks = half_masks()
    pairs = width // PAIR
    for first in range(0, pairs, batch):
        group = range(first, min(first + batch, pairs))
        loaded = [pair_slices(packed, rows, width, pair) for pair in group]
        upstream = [grad_out[rows, pair * PAIR : (pair + 1) * PAIR] for pair in group]
        heads = [(i, side) for i in range(len(group)) for side in range(2)]
        own_q = [loaded[i][0] * masks[side] for i, side in heads]
        own_k = [loaded[i][1] * masks[side] for i, side in heads]
        own_up = [upstream[i] * masks[side] for i, side in heads]
        scores = [dot(loaded[i][1], own, NT) * (SCALE * LOG2E) for (i, _), own in zip(heads, own_q)]
        grad_shares = [dot(loaded[i][2], own, NT) for (i, _), own in zip(heads, own_up)]
        if bias is not None:
            scores = [value + bias for value in scores]
        sums = total[2 * first : 2 * group.stop, rows]
        shares = [jnp.exp2(value - sums[i : i + 1]) for i, value in enumerate(scores)]
        weighted = [value * grad for value, grad in zip(shares, grad_shares)]
        inner = [jnp.sum(value, 0, keepdims=True) for value in weighted]
        grad_scores = [
            (value - share * total_inner).astype(BF16)
            for value, share, total_inner in zip(weighted, shares, inner)
        ]
        grad_q = [dot(value, own, TN) for value, own in zip(grad_scores, own_k)]
        grad_k = [dot(value, own) for value, own in zip(grad_scores, own_q)]
        grad_v = [dot(value.astype(BF16), own) for value, own in zip(shares, own_up)]
        for i, pair in enumerate(group):
            at = pair * PAIR
            for part, (grad, scale) in enumerate(((grad_q, SCALE), (grad_k, SCALE), (grad_v, 1.0))):
                out[rows, part * width + at : part * width + at + PAIR] = (
                    (grad[2 * i] + grad[2 * i + 1]) * scale
                ).astype(BF16)


def embed(raw, vectors, actions):
    raw = raw.astype(F32)
    masked = raw > SEEN
    return jnp.where(masked, vectors[7:8, :], raw) + actions, masked


def space_forward_kernel(group, pieces, *refs):
    xs, (act, vectors, w_qkv, packed, out, total, *parts) = refs[:pieces], refs[pieces:]
    raw = jnp.concatenate([x[0] for x in xs], 0) if pieces > 1 else xs[0][0]
    count, width = raw.shape
    embedded, _ = embed(raw, vectors, act[0])
    unit, _ = normalise(embedded)
    normed = (unit * vectors[0:1, :] + vectors[1:2, :]).astype(BF16)
    packed[0] = dot(normed, w_qkv[...]).astype(BF16)
    attend_forward_rows(packed.at[0], slice(0, count), width, out.at[0], total.at[0], 4)
    share = count // group
    for j in range(group):
        parts[j][0, 0] = raw[j * share : (j + 1) * share]
        parts[j][0, 1] = out[0, j * share : (j + 1) * share]


def time_forward_kernel(sub, pieces, *refs):
    xs, o1s, refs = refs[:pieces], refs[pieces : 2 * pieces], refs[2 * pieces :]
    (act, perm, bias, vectors, w_space_out, w_qkv, w_out, h1, h2, a2, packed, o2, total) = refs
    x = jnp.concatenate([value[...] for value in xs], 0)
    o1 = jnp.concatenate([value[...] for value in o1s], 0)
    frames, places, width = x.shape
    count = frames * places
    raw = dot(perm[...], x.reshape(count, width))
    blended = dot(perm[...], o1.reshape(count, width)).astype(BF16)
    actions = jnp.broadcast_to(act[...][None], (places, frames, width)).reshape(count, width)
    embedded, _ = embed(raw, vectors, actions)
    after_space = embedded + dot(blended, w_space_out[...])
    h1[...] = after_space
    unit, _ = normalise(after_space)
    normed = (unit * vectors[2:3, :] + vectors[3:4, :]).astype(BF16)
    a2[...] = normed
    packed[...] = dot(normed, w_qkv[...]).astype(BF16)
    for start in range(0, count, sub):
        attend_forward(packed, slice(start, start + sub), width, o2, total, bias[...], 8)
    h2[...] = after_space + dot(o2[...], w_out[...])


def feed_kernel(tile, pieces, per, h2, *refs):
    cots, (vectors, b_up, w_up, w_down), refs = refs[:pieces], refs[pieces : pieces + 4], refs[pieces + 4 :]
    results, (cot, z, dur, a3, r2, sums, bias_grad) = refs[:pieces], refs[pieces:]
    piece = pl.program_id(0) // per
    for j in range(pieces):

        @pl.when(piece == j)
        def _(j=j):
            cot[...] = cots[j][...]

    @pl.when(pl.program_id(0) == 0)
    def _():
        sums[...] = jnp.zeros_like(sums)
        bias_grad[...] = jnp.zeros_like(bias_grad)

    after = h2[...]
    unit, spread = normalise(after)
    gain = vectors[4:5, :]
    normed = (unit * gain + vectors[5:6, :]).astype(BF16)
    a3[...] = normed
    upstream_low = cot[...]
    c = 0.7978845608028654
    total = after + vectors[6:7, :]
    grad_normed = jnp.zeros_like(after)
    for at in range(0, w_up.shape[1], tile):
        cols = slice(at, at + tile)
        hidden = dot(normed, w_up[:, cols]) + b_up[:, cols]
        grad_active = dot(upstream_low, w_down[cols, :], NT)
        square = hidden * hidden
        gate = 0.5 * jnp.tanh(hidden * (c + (c * 0.044715) * square)) + 0.5
        active = hidden * gate
        slope = gate + active * (1.0 - gate) * (2.0 * c + (6.0 * c * 0.044715) * square)
        grad_hidden = grad_active * slope
        bias_grad[:, cols] += jnp.sum(grad_hidden, 0, keepdims=True)
        active = active.astype(BF16)
        grad_hidden = grad_hidden.astype(BF16)
        z[:, cols] = active
        dur[:, cols] = grad_hidden
        total = total + dot(active, w_down[cols, :])
        grad_normed = grad_normed + dot(grad_hidden, w_up[:, cols], NT)
    for j in range(pieces):

        @pl.when(piece == j)
        def _(j=j):
            results[j][...] = total.astype(BF16)

    upstream = upstream_low.astype(F32)
    r2[...] = upstream + norm_back(unit, spread, gain, grad_normed)
    sums[0:1, :] += jnp.sum(grad_normed * unit, 0, keepdims=True)
    sums[1:2, :] += jnp.sum(grad_normed, 0, keepdims=True)
    sums[2:3, :] += jnp.sum(upstream, 0, keepdims=True)


def time_back_kernel(
    sub, r2, h1, packed, total, perm, bias, vectors, w_out, w_qkv, grad_packed, r2_low, sums, *rest
):
    *r1s, grad_out = rest

    @pl.when(pl.program_id(0) == 0)
    def _():
        sums[...] = jnp.zeros_like(sums)

    count, width = r2.shape
    stream = r2[...]
    low = stream.astype(BF16)
    r2_low[...] = low
    grad_out[...] = dot(low, w_out[...], NT).astype(BF16)
    for start in range(0, count, sub):
        attend_back(
            packed, slice(start, start + sub), width, grad_out, total, bias[...], grad_packed, 8
        )
    grad_normed = dot(grad_packed[...], w_qkv[...], NT)
    unit, spread = normalise(h1[...])
    stream = stream + norm_back(unit, spread, vectors[2:3, :], grad_normed)
    sums[0:1, :] += jnp.sum(grad_normed * unit, 0, keepdims=True)
    sums[1:2, :] += jnp.sum(grad_normed, 0, keepdims=True)
    r1 = dot(perm[...], stream.astype(BF16)).astype(BF16).reshape(-1, r1s[0].shape[1], width)
    share = r1s[0].shape[0]
    for j, piece in enumerate(r1s):
        piece[...] = r1[j * share : (j + 1) * share]


def space_back_kernel(pieces, group, order, *refs):
    xs, r1s, refs = refs[:pieces], refs[pieces : pieces + group], refs[pieces + group :]
    (act, hot, earlier, packed, total, vectors, w_out, w_qkv) = refs[:8]
    (grad_packed, a1, r1_all, sums), refs = refs[8:12], refs[12:]
    input_grads, (grad_out,) = refs[:-1], refs[-1:]

    @pl.when(pl.program_id(0) == 0)
    def _():
        sums[...] = earlier[...]

    raw = jnp.concatenate([x[0] for x in xs], 0) if pieces > 1 else xs[0][0]
    r1 = jnp.concatenate([value[0] for value in r1s], 0)
    r1_all[0] = r1
    count, width = raw.shape
    grad_out[...] = dot(r1, w_out[...], NT).astype(BF16)
    attend_back(
        packed.at[0], slice(0, count), width, grad_out, total.at[0], None, grad_packed.at[0], 4
    )
    grad_normed = dot(grad_packed[0], w_qkv[...], NT)
    embedded, masked = embed(raw, vectors, act[0])
    unit, spread = normalise(embedded)
    gain = vectors[0:1, :]
    a1[0] = (unit * gain + vectors[1:2, :]).astype(BF16)
    stream = r1.astype(F32) + norm_back(unit, spread, gain, grad_normed)
    kept = jnp.where(masked, 0.0, stream)
    if len(input_grads) == 1:
        input_grads[0][0] = kept.astype(BF16)
    else:
        share = count // len(order)
        for at, k in enumerate(order):
            input_grads[k // 2][k % 2, 0] = kept[at * share : (at + 1) * share].astype(BF16)
    whole_sum = jnp.sum(stream, 0, keepdims=True)
    sums[0:1, :] += jnp.sum(grad_normed * unit, 0, keepdims=True)
    sums[1:2, :] += jnp.sum(grad_normed, 0, keepdims=True)
    sums[2:3, :] += whole_sum - jnp.sum(kept, 0, keepdims=True)
    sums[8:, :] += hot[0] * whole_sum


def whole(array):
    rank = len(array.shape)
    return pl.BlockSpec(array.shape, lambda *_: (0,) * rank, pipeline_mode=pl.Buffered(1))


def struct(shape, kind):
    return jax.ShapeDtypeStruct(shape, kind)


def call(kernel, grid, operands, outs, scratch=(), flops=0, meta=None):
    in_specs = [
        whole(array) if block is None else pl.BlockSpec(block, index)
        for array, block, index in operands
    ]
    out_specs = [
        pl.BlockSpec(shape, lambda *_, rank=len(shape): (0,) * rank)
        if block is None
        else pl.BlockSpec(block, index)
        for shape, _, block, index in outs
    ]
    moved = sum(a.size * a.dtype.itemsize for a, _, _ in operands)
    return pl.pallas_call(
        kernel,
        grid_spec=pltpu.PrefetchScalarGridSpec(
            num_scalar_prefetch=0 if meta is None else 1,
            grid=grid,
            in_specs=in_specs,
            out_specs=out_specs,
            scratch_shapes=scratch,
        ),
        out_shape=[struct(shape, kind) for shape, kind, _, _ in outs],
        cost_estimate=pl.CostEstimate(flops=flops, bytes_accessed=2 * moved, transcendentals=0),
        compiler_params=pltpu.CompilerParams(vmem_limit_bytes=VMEM_LIMIT),
    )(*(() if meta is None else (meta,)), *[a for a, _, _ in operands])


def collect_kernel(parts, meta, *refs):
    *refs, perm, out, held = refs
    chip = pl.program_id(0)
    for i in range(len(refs) // (2 * parts)):

        @pl.when(chip == i)
        def _(i=i):
            found = [ref[...] for ref in refs[2 * parts * i : 2 * parts * (i + 1)]]
            held[...] = jnp.concatenate(found, 0).reshape(held.shape)

    out[...] = dot(perm[...], held[...]).astype(BF16).reshape(out.shape)


def collect(by_slot, chips, perm, shape, operand):
    p, width = shape[0], shape[-1]
    block = 16
    steps = p // block
    parts = len(by_slot[0])
    span = sum(part.shape[-3] for part, _ in by_slot[0])
    count = len(by_slot)
    operands = []
    for k, pieces in enumerate(by_slot):

        def slot_index(i, h, meta, k=k):
            return 0, jnp.where(i == k // 2, h, jnp.where(i < k // 2, 0, steps - 1)), 0

        operands += [
            operand(piece, (piece[0].shape[-3], block, width), slot_index) for piece in pieces
        ]
    operands.append((perm, None, None))
    outs = [
        (
            (p, count * span, width),
            BF16,
            (block, 2 * span, width),
            lambda i, h, meta: (h, meta[i], 0),
        )
    ]
    return call(
        lambda *refs: collect_kernel(parts, *refs),
        (count // 2, steps),
        operands,
        outs,
        [pltpu.VMEM((block * 2 * span, width), BF16)],
        meta=chips,
    )[0].reshape(shape)


def collect_result_kernel(meta, *refs):
    *pieces, out = refs
    for j, piece in enumerate(pieces):

        @pl.when(pl.program_id(0) == j)
        def _(piece=piece):
            out[...] = piece[...]


def collect_result(pieces, where):
    p, _, frames, width = pieces[0].shape
    return call(
        collect_result_kernel,
        (len(pieces),),
        [(piece, None, None) for piece in pieces],
        [
            (
                (p, len(pieces), frames, width),
                BF16,
                (p, 1, frames, width),
                lambda j, meta: (0, meta[j], 0, 0),
            )
        ],
        meta=where,
    )[0]


def put(outs, slot, value):
    share = outs[0].shape[0]
    outs[slot // share][slot % share] = value


def columns_kernel(meta, *refs, counts, firsts, blocks, split):
    step = pl.program_id(0)
    *refs, held = refs
    local = step % firsts[-1]
    for i, count in enumerate(counts):
        lefts, rights, refs = refs[:count], refs[count : 2 * count], refs[2 * count :]

        @pl.when((local >= firsts[i]) & (local < firsts[i + 1]))
        def _(lefts=lefts, rights=rights):
            total = sum(dot(l[...], r[...], TN) for l, r in zip(lefts, rights))
            held[...] = total.astype(BF16)

    shares = len(split)
    size = held.shape[0] // blocks
    per = firsts[-1] // shares
    for part in range(2 * shares):
        two = part >= shares and split[part - shares]
        own, refs = refs[: 1 + two], refs[1 + two :]

        @pl.when(step // per == part)
        def _(first=(part % shares) * blocks, own=own):
            for slot in range(blocks):
                source = pl.multiple_of(meta[first + slot] * size, size)
                put(own, slot, held[pl.ds(source, size), :])


def columns_grad(pairs, meta, split, tile=512):
    shares = len(split)
    blocks = (meta.shape[0] - 1) // shares
    height = pairs[0][0][0].shape[1]
    size = height // blocks
    tile = min([tile] + [rights[0].shape[1] // 2 for _, rights in pairs])
    steps = [rights[0].shape[1] // 2 // tile for _, rights in pairs]
    firsts = [sum(steps[:i]) for i in range(len(steps) + 1)]
    per = firsts[-1] // shares
    operands, flops = [], 0
    for (lefts, rights), first, count in zip(pairs, firsts, steps):
        operands += [(left, None, None) for left in lefts]
        for right in rights:

            def index(i, meta, first=first, count=count):
                core = meta[shares * blocks]
                half = jnp.where(i < firsts[-1], 1 - core, core)
                return 0, half * count + jnp.clip(i % firsts[-1] - first, 0, count - 1)

            operands.append((right, (right.shape[0], tile), index))
            flops += 2 * right.size * height

    def part_out(part, rows):
        block = (rows, size, tile), lambda i, meta: (0, 0, jnp.clip(i - part * per, 0, per - 1))
        return (rows, size, per * tile), BF16, *block

    outs = [part_out(share, blocks) for share in range(shares)]
    for share, two in enumerate(split):
        outs += [part_out(shares + share, blocks // (1 + two))] * (1 + two)
    kernel = lambda *refs: columns_kernel(
        *refs, counts=[len(lefts) for lefts, _ in pairs], firsts=firsts, blocks=blocks, split=split
    )
    scratch = [pltpu.VMEM((height, tile), BF16)]
    return call(kernel, (2 * firsts[-1],), operands, outs, scratch, flops, meta)


def rows_kernel(meta, *refs, step_blocks, steps, blocks):
    step = pl.program_id(0)
    lefts, right, (sent, *outs) = refs[:step_blocks], refs[step_blocks], refs[step_blocks + 1 :]
    value = dot(jnp.concatenate([left[...] for left in lefts], 1), right[...], TN).astype(BF16)
    value = value.reshape(step_blocks, -1, value.shape[-1])
    middle = value.shape[-1] // 2
    halves = value[:, :, :middle], value[:, :, middle:]
    share = steps // len(outs)
    for core in range(2):

        @pl.when(meta[blocks] == core)
        def _(core=core):
            sent[...] = halves[1 - core]

        for i, out in enumerate(outs):

            @pl.when((meta[blocks] == core) & (step >= i * share) & (step < (i + 1) * share))
            def _(core=core, out=out):
                out[...] = halves[core]


def rows_grad(left, right, meta, split, step_blocks=2):
    blocks = meta.shape[0] - 1
    depth, height = left.shape
    size, columns = height // blocks, right.shape[1] // 2
    steps = blocks // step_blocks
    operands = [
        (left, (depth, size), lambda i, meta, j=j: (0, meta[i * step_blocks + j]))
        for j in range(step_blocks)
    ]
    operands.append((right, None, None))
    parts = 1 + split[0]
    share = steps // parts
    block = (step_blocks, size, columns)
    outs = [((blocks, size, columns), BF16, block, lambda i, meta: (i, 0, 0))]
    outs += [
        (
            (blocks // parts, size, columns),
            BF16,
            block,
            lambda i, meta, first=j * share: (jnp.clip(i - first, 0, share - 1), 0, 0),
        )
        for j in range(parts)
    ]
    kernel = lambda *refs: rows_kernel(
        *refs, step_blocks=step_blocks, steps=steps, blocks=blocks
    )
    return call(kernel, (steps,), operands, outs, flops=4 * depth * height * columns, meta=meta)


def body(
    tokens,
    mask_bits,
    action_ids,
    vectors,
    action_table,
    w_space_qkv,
    w_space_out,
    w_time_qkv,
    w_time_out,
    w_up,
    b_up,
    w_down,
    cotangent,
):
    p, clips, frames, width = tokens.shape
    n, layers = lax.axis_size("tile"), lax.axis_size("clip")
    me, layer = lax.axis_index("tile"), lax.axis_index("clip")
    core = me % 2
    group = n // clips
    own_frames = frames // group
    grid_all = n * p
    places = grid_all // group
    clip, part = me // group, me % group
    hidden = w_up.shape[1]
    rows = places * frames

    def swap(value, k, axis="tile"):
        size = lax.axis_size(axis)
        return lax.ppermute(value, axis, [(i, i ^ k) for i in range(size)])

    def row_block(*shape):
        return shape, lambda i: (i,) + (0,) * (len(shape) - 1)

    blocks = n * layers // 2
    tile_bits = [1 << b for b in range(1, n.bit_length() - 1)]

    def orders(hops):
        slots = [(0, None, 0, None)]
        for hop in hops:
            if hop == "scatter":
                choices = [(0, None, 0, c) for c in range(layers)]
            elif hop == "tiles":
                choices = [(0, t, 0, None) for t in range(n // 2)]
            elif hop == "spread":
                choices = [(0, None, c, None) for c in range(layers)]
            else:
                bit = (hop[1], None, 0, None) if hop[0] == "tile" else (0, None, hop[1], None)
                choices = [(0, None, 0, None), bit]
            slots = [
                (a ^ x, t if u is None else u, b ^ y, c if d is None else d)
                for a, t, b, c in slots
                for x, u, y, d in choices
            ]
        where = [
            (layer ^ b if c is None else c) * (n // 2) + ((me ^ a) // 2 if t is None else t)
            for a, t, b, c in slots
        ]
        return jnp.stack([jnp.asarray(w, jnp.int32) for w in where])

    def halves(value, hop):
        if hop is None or isinstance(hop, str):
            return [value]
        middle = value.shape[0] // 2
        return [value[:middle], value[middle:]]

    def meta_of(chains):
        return jnp.concatenate([orders(hops) for hops in chains] + [core.astype(jnp.int32)[None]])

    def begin(make, chains, meta):
        split = [not isinstance(hops[0], str) for hops in chains]
        made = make(meta, split)
        sent, made, parts = list(made[: len(split)]), made[len(split) :], []
        for two in split:
            parts.append(list(made[: 1 + two]))
            made = made[1 + two :]
        return chains, parts, sent

    def cross(begun):
        chains, parts, sent = begun
        return chains, parts, [swap(value, 1) for value in sent]

    def add(values, kind):
        return sum(value.astype(F32) for value in values).astype(kind)

    def land(crossed):
        chains, all_parts, received = crossed
        landed = []
        for hops, parts, came in zip(chains, all_parts, received):
            if isinstance(hops[0], str):
                landed.append([[(add([parts[0], came], BF16), False)]])
            else:
                _, sent = halves(came, hops[0])
                landed.append([[(parts[0], False), (came, True)], add([parts[1], sent], BF16)])
        return chains, landed, 0

    def merge(state):
        chains, parts, at = state
        kept = jnp.concatenate([own[0][0][0] for own in parts], -1)
        return chains[:1], [[[(kept, False)], jnp.concatenate([own[1] for own in parts], -1)]], at

    def depart(state):
        chains, parts, at = state
        coming = []
        for hops, own in zip(chains, parts):
            hop, value = hops[at], own[0][0][0]
            if hop == "scatter":
                coming.append(lax.psum_scatter(value, "clip", scatter_dimension=0, tiled=True))
            elif hop == "tiles":
                same_core = [list(range(c, n, 2)) for c in range(2)]
                coming.append(
                    lax.psum_scatter(
                        value, "tile", scatter_dimension=0, tiled=True, axis_index_groups=same_core
                    )
                )
            elif hop == "spread":
                share = value.shape[0] // layers
                coming.append(
                    [swap(value[j * share : (j + 1) * share], j, "clip") for j in range(1, layers)]
                )
            else:
                coming.append(swap(own[1], hop[1], hop[0]))
        return state, coming

    def arrive(departed):
        (chains, parts, at), coming = departed
        new_parts = []
        for hops, own, came in zip(chains, parts, coming):
            following = hops[at + 1] if at + 1 < len(hops) else None
            kind = F32 if following is None else BF16
            kept = [v[: v.shape[0] // 2] if first else v for v, first in own[0]]
            if hops[at] == "spread":
                values = [kept[0][: kept[0].shape[0] // layers]] + came
            else:
                values = [came] if isinstance(hops[at], str) else kept + [came]
            summed = [add(piece, kind) for piece in zip(*[halves(v, following) for v in values])]
            new_parts.append([[(summed[0], False)]] + summed[1:])
        return chains, new_parts, at + 1

    def last_swap(state):
        own = jnp.concatenate([own[0][0][0][0].astype(F32) for own in state[1]], 1)
        size = own.shape[0] // 2
        mine = lax.dynamic_slice_in_dim(own, core * size, size, 0)
        other = lax.dynamic_slice_in_dim(own, (1 - core) * size, size, 0)
        return mine, swap(other.astype(BF16), 1)

    def join(mine, other, widths):
        whole_parts, at = [], 0
        for w in widths:
            a, b = mine[:, at : at + w // 2], other[:, at : at + w // 2].astype(F32)
            whole_parts.append(
                jnp.where(core == 0, jnp.concatenate([a, b], 1), jnp.concatenate([b, a], 1))
            )
            at += w // 2
        return whole_parts

    one_way = [("tile", bit) for bit in tile_bits]
    other_way = one_way[::-1]
    clip_bits = [("clip", 1 << b) for b in range(layers.bit_length() - 1)]
    up_chains, down_chains = [one_way + clip_bits], [["scatter"] + one_way]
    time_chains, space_chains = [["scatter"] + other_way], [one_way + clip_bits, other_way + clip_bits]

    order = [k for j in range(group) for k in range(j, n, group)]
    onehot = (action_ids[..., None] == lax.iota(jnp.int32, action_table.shape[0])).astype(F32)
    action_rows = jnp.einsum("cfa,ad->cfd", onehot, action_table, precision=lax.Precision.HIGHEST)
    act_time = lax.dynamic_index_in_dim(action_rows, clip, 0, keepdims=False)
    act_space = lax.dynamic_slice_in_dim(act_time, part * own_frames, own_frames, 0)[:, None, :]

    regular = p % 16 == 0 and 2 * own_frames == 16
    deal_back = None
    if regular:
        at = lax.iota(jnp.int32, 16 * 2 * own_frames)
        place, frame = at % 16, at // 16
        source = place * 2 * own_frames + (frame + core * own_frames) % (2 * own_frames)
        deal_back = (at[:, None] == source[None, :]).astype(BF16)
    marked = jnp.where((mask_bits > 0)[..., None], jnp.asarray(MASKED, BF16), tokens)
    marked = marked.reshape(p, n, own_frames, width)
    chunks = 2
    span = own_frames // chunks
    blocks_of = [lax.dynamic_index_in_dim(marked, me ^ k, 1, keepdims=False) for k in order]
    sources = [
        [value[:, c * span : (c + 1) * span].transpose(1, 0, 2) for value in blocks_of]
        for c in range(chunks)
    ]

    def send_out(parts):
        return [part if k == 0 else swap(part, k) for k, part in zip(order, parts)]

    cot_pieces = [
        lax.dynamic_index_in_dim(cotangent, clip ^ j, 1, keepdims=False).reshape(p * frames, width)
        for j in range(n // group)
    ]
    block = 16
    count = block * frames
    sub = min(count, 128)
    index = lax.iota(jnp.int32, count)
    slot, place = index // block, index % block
    frame_of_slot = ((part ^ (slot // own_frames)) * own_frames) + slot % own_frames
    target = place * frames + frame_of_slot
    perm_back = (target[:, None] == index[None, :]).astype(BF16)
    perm = (index[:, None] == target[None, :]).astype(BF16)
    seq = lax.iota(jnp.int32, sub)
    same = (seq[:, None] // frames) == (seq[None, :] // frames)
    bias = jnp.where(same & (seq[:, None] <= seq[None, :]), 0.0, NEGATIVE).astype(F32)
    own_hot = lax.dynamic_slice_in_dim(
        lax.dynamic_index_in_dim(onehot, clip, 0, keepdims=False), part * own_frames, own_frames, 0
    )[..., None]
    where_clip = clip ^ lax.iota(jnp.int32, clips)
    where_chip = (me // 2) ^ lax.iota(jnp.int32, n // 2)
    tables = dict(
        act_time=act_time,
        act_space=act_space,
        perm=perm,
        perm_back=perm_back,
        bias=bias,
        own_hot=own_hot,
        where_clip=where_clip,
        where_chip=where_chip,
        deal_back=deal_back,
        **{
            name: meta_of(chains)
            for name, chains in (
                ("up", up_chains),
                ("down", down_chains),
                ("time", time_chains),
                ("space", space_chains),
            )
        },
    )
    pieces = []
    for c in range(chunks):
        pieces.append(send_out(sources[c]))
        if c == 0:
            pieces[0], sources, cot_pieces, tables = hold_parts(
                pieces[0], sources, cot_pieces, tables
            )
    cot_pieces = [
        piece if j == 0 else swap(piece, j * group) for j, piece in enumerate(cot_pieces)
    ]
    if p % 16:
        pieces = [[jnp.concatenate(parts, 1)] for parts in pieces]
    kinds = len(pieces[0])
    act_time, act_space, own_hot = (tables[name] for name in ("act_time", "act_space", "own_hot"))
    perm, perm_back, bias = (tables[name] for name in ("perm", "perm_back", "bias"))
    where_clip, where_chip, deal_back = (
        tables[name] for name in ("where_clip", "where_chip", "deal_back")
    )

    head_flops = 2 * HEADS * HEAD_DIM

    def frame_block(*shape):
        return (1,) + shape, lambda i: (i, 0, 0)

    def chunk_block(first, *shape):
        return (1,) + shape, lambda i: (first + i, 0, 0)

    space, both = [], []
    for c in range(chunks):
        packed, o1, total, *parts = call(
            lambda *refs: space_forward_kernel(group, kinds, *refs),
            (span,),
            [(x, *frame_block(*x.shape[1:])) for x in pieces[c]]
            + [
                (act_space, *chunk_block(c * span, 1, width)),
                (vectors, None, None),
                (w_space_qkv, None, None),
            ],
            [
                ((span, grid_all, 3 * width), BF16, *frame_block(grid_all, 3 * width)),
                ((span, grid_all, width), BF16, *frame_block(grid_all, width)),
                ((span, HEADS, grid_all), F32, *frame_block(HEADS, grid_all)),
            ]
            + [
                (
                    (span, 2, places, width),
                    BF16,
                    (1, 2, places, width),
                    lambda i: (i, 0, 0, 0),
                )
            ]
            * group,
            flops=2 * span * grid_all * width * 3 * width
            + 16 * span * grid_all * grid_all * head_flops,
        )
        space.append((packed, o1, total))
        both.append([part if j == 0 else swap(part, j) for j, part in enumerate(parts)])
    both = [both[c][j] for j in range(group) for c in range(chunks)]

    def slot_block(size):
        return (size, block, width), lambda i: (0, i, 0)

    total_block = ((HEADS, count), lambda i: (0, i))
    h1, h2, a2, packed_two, o2, total_two = call(
        lambda *refs: time_forward_kernel(sub, len(both), *refs),
        (places // block,),
        [
            (value, (span, None, block, width), lambda i, which=which: (0, which, i, 0))
            for which in range(2)
            for value in both
        ]
        + [
            (act_time, None, None),
            (perm, None, None),
            (bias, None, None),
            (vectors, None, None),
            (w_space_out, None, None),
            (w_time_qkv, None, None),
            (w_time_out, None, None),
        ],
        [
            ((rows, width), F32, *row_block(count, width)),
            ((rows, width), F32, *row_block(count, width)),
            ((rows, width), BF16, *row_block(count, width)),
            ((rows, 3 * width), BF16, *row_block(count, 3 * width)),
            ((rows, width), BF16, *row_block(count, width)),
            ((HEADS, rows), F32, *total_block),
        ],
        flops=2 * rows * width * 5 * width + 16 * rows * sub * head_flops,
    )

    step = min(p * frames, 256)
    per = p * frames // step

    def piece_block(j):
        return (step, width), lambda i, j=j: (jnp.clip(i - j * per, 0, per - 1), 0)

    *result_pieces, cot, z, dur, a3, r2, sums_three, bias_up = call(
        lambda *refs: feed_kernel(1024, len(cot_pieces), per, *refs),
        (rows // step,),
        [(h2, *row_block(step, width))]
        + [(piece, *piece_block(j)) for j, piece in enumerate(cot_pieces)]
        + [
            (vectors, None, None),
            (b_up[None, :], None, None),
            (w_up, None, None),
            (w_down, None, None),
        ],
        [((p * frames, width), BF16, *piece_block(j)) for j in range(len(cot_pieces))]
        + [
            ((rows, width), BF16, *row_block(step, width)),
            ((rows, hidden), BF16, *row_block(step, hidden)),
            ((rows, hidden), BF16, *row_block(step, hidden)),
            ((rows, width), BF16, *row_block(step, width)),
            ((rows, width), F32, *row_block(step, width)),
            ((8, width), F32, None, None),
            ((1, hidden), F32, None, None),
        ],
        flops=8 * rows * width * hidden,
    )

    result_pieces = [
        (piece if j == 0 else swap(piece, j * group)).reshape(p, 1, frames, width)
        for j, piece in enumerate(result_pieces)
    ]

    def make_down(meta, split):
        if hidden // blocks % 128:
            return columns_grad([([z], [cot])], meta, split, 256)
        return rows_grad(z, cot, meta, split)

    def make_up(meta, split):
        return columns_grad([([a3], [dur])], meta, split)

    up = begin(make_up, up_chains, tables["up"])
    cot, up, result_pieces[:-1] = hold_parts(cot, up, result_pieces[:-1])
    up = cross(up)
    down = begin(make_down, down_chains, tables["down"])
    r2, down, up, result_pieces = hold_parts(r2, down, up, result_pieces)
    up, down = depart(land(up)), cross(down)

    grad_packed_two, r2_low, sums_two, *r1_parts = call(
        lambda *refs: time_back_kernel(sub, *refs),
        (places // block,),
        [
            (r2, *row_block(count, width)),
            (h1, *row_block(count, width)),
            (packed_two, *row_block(count, 3 * width)),
            (total_two, *total_block),
            (perm_back, None, None),
            (bias, None, None),
            (vectors, None, None),
            (w_time_out, None, None),
            (w_time_qkv, None, None),
        ],
        [
            ((rows, 3 * width), BF16, *row_block(count, 3 * width)),
            ((rows, width), BF16, *row_block(count, width)),
            ((8, width), F32, None, None),
        ]
        + [((own_frames, places, width), BF16, *slot_block(own_frames))] * group,
        [pltpu.VMEM((count, width), BF16)],
        flops=2 * rows * width * 4 * width + 40 * rows * sub * head_flops,
    )
    grad_packed_two, up, down = hold_parts(grad_packed_two, up, down)
    up, down = depart(arrive(up)), depart(land(down))
    r1_parts = [r1 if j == 0 else swap(r1, j) for j, r1 in enumerate(r1_parts)]

    def make_time(meta, split):
        return columns_grad([([a2], [grad_packed_two]), ([o2], [r2_low])], meta, split)

    time = begin(make_time, time_chains, tables["time"])

    dealt = 1 if p % 16 else n

    def send_back(parts):
        if dealt == 1:
            parts = [parts[0][:, at * p : (at + 1) * p] for at in range(n)]
            parts = [parts[order.index(k)] for k in range(n)]
            parts = [jnp.stack(parts[2 * j : 2 * j + 2]) for j in range(n // 2)]
        return [part if j == 0 else swap(part, 2 * j) for j, part in enumerate(parts)]

    def pass_on(came):
        crossed = swap(jnp.stack([value[1] for value in came]), 1)
        return [found for j, value in enumerate(came) for found in ((value, 0), (crossed, j))]

    def operand(found, block, index):
        return found[0], (None,) + block, lambda *i: (found[1],) + index(*i)

    def space_back(c, earlier):
        packed, _, total = space[c]
        return call(
            lambda *refs: space_back_kernel(kinds, group, order, *refs),
            (span,),
            [(x, *frame_block(*x.shape[1:])) for x in pieces[c]]
            + [(r1, *chunk_block(c * span, places, width)) for r1 in r1_parts]
            + [
                (act_space, *chunk_block(c * span, 1, width)),
                (own_hot, *chunk_block(c * span, action_table.shape[0], 1)),
                (earlier, None, None),
                (packed, *frame_block(grid_all, 3 * width)),
                (total, *frame_block(HEADS, grid_all)),
                (vectors, None, None),
                (w_space_out, None, None),
                (w_space_qkv, None, None),
            ],
            [
                ((span, grid_all, 3 * width), BF16, *frame_block(grid_all, 3 * width)),
                ((span, grid_all, width), BF16, *frame_block(grid_all, width)),
                ((span, grid_all, width), BF16, *frame_block(grid_all, width)),
                ((8 + action_table.shape[0], width), F32, None, None),
            ]
            + (
                [((span, grid_all, width), BF16, *frame_block(grid_all, width))]
                if dealt == 1
                else [
                    ((2, span, p, width), BF16, (2, 1, p, width), lambda i: (0, i, 0, 0))
                ]
                * (n // 2)
            ),
            [pltpu.VMEM((grid_all, width), BF16)],
            flops=2 * span * grid_all * width * 4 * width
            + 40 * span * grid_all * grid_all * head_flops,
        )

    r1_parts, time, up = hold_parts(r1_parts, time, up)
    up, time = depart(arrive(up)), cross(time)
    early = jnp.concatenate([sums_two, sums_three, bias_up.reshape(-1, width)], 0)
    back = [space_back(0, jnp.zeros((8 + action_table.shape[0], width), F32))]
    back[0], r1_parts, time, up = hold_parts(back[0], r1_parts, time, up)
    input_pieces = [send_back(back[0][4:])]
    up, time = depart(arrive(up)), depart(land(time))
    for c in range(1, chunks):
        back.append(space_back(c, back[-1][3]))
    back, input_pieces, up, down = hold_parts(back, input_pieces, up, down)
    input_pieces[0] = pass_on(input_pieces[0])
    for c in range(1, chunks):
        input_pieces.append(send_back(back[c][4:]))
    up = arrive(up)
    while up[2] < len(up[0][0]):
        up = arrive(depart(up))
    up, down = last_swap(up), depart(arrive(down))
    grads_one, a1s, r1s = list(zip(*back))[:3]

    def flat(values):
        return [value.reshape(-1, value.shape[-1]) for value in values]

    def make_space(meta, split):
        return columns_grad(
            [
                (flat(a1s), flat(grads_one)),
                (flat([o1 for _, o1, _ in space]), flat(r1s)),
            ],
            meta,
            split,
        )

    small = jnp.concatenate([back[-1][3], early], 0)
    small_hops = [("tile", 1 << b) for b in range(n.bit_length() - 1)] + clip_bits

    space_sum = begin(make_space, space_chains, tables["space"])
    where_clip, space_sum, up, down, input_pieces = hold_parts(
        where_clip, space_sum, up, down, input_pieces
    )
    space_sum = cross(space_sum)
    small_came = swap(small, small_hops[0][1], small_hops[0][0])
    down = depart(arrive(down))
    result_out = collect_result(result_pieces, where_clip)
    space_sum, result_out, small_came = hold_parts(space_sum, result_out, small_came)
    space_sum, small = land(space_sum), small + small_came
    input_pieces[1:] = [pass_on(came) for came in input_pieces[1:]]
    time = arrive(time)

    def collect_input(input_pieces, where_chip):
        by_slot = [[pieces_of[k] for pieces_of in input_pieces] for k in range(n)]
        if regular:
            input_grad = collect(by_slot, where_chip, deal_back, tokens.shape, operand)
        else:
            input_grad = jnp.zeros((p, n, own_frames, width), BF16)
            for k, parts in enumerate(by_slot):
                piece = jnp.concatenate([value[at] for value, at in parts], 0)
                input_grad = lax.dynamic_update_slice_in_dim(
                    input_grad, piece.transpose(1, 0, 2)[:, None], me ^ k, 1
                )
            input_grad = input_grad.reshape(tokens.shape)
        return input_grad

    rounds = max(len(small_hops) - 1, len(space_sum[0][0]) + 1, 2 * len(one_way))
    for r in range(rounds):
        departed = small_came = time_moves = None
        if r < len(space_sum[0][0]):
            if r == len(one_way):
                space_sum = merge(space_sum)
            departed = depart(space_sum)
        if r + 1 < len(small_hops):
            small_came = swap(small, small_hops[r + 1][1], small_hops[r + 1][0])
        if r >= len(one_way) and time[2] < len(time[0][0]):
            time_moves = depart(time)
        others = [down, input_pieces] if r == 0 else []
        if r == 1:
            input_grad = collect_input(input_pieces, where_chip)
            others = [input_grad]
        departed, small_came, time_moves, *others = hold_parts(
            departed, small_came, time_moves, *others
        )
        if r == 0:
            down, input_pieces = others
            down = arrive(down)
            while down[2] < len(down[0][0]):
                down = arrive(depart(down))
            down = last_swap(down)
        if r == 1:
            (input_grad,) = others
        if time_moves is not None:
            time = arrive(time_moves)
            if time[2] == len(time[0][0]):
                time_last = last_swap(time)
        if departed is not None:
            space_sum = arrive(departed)
        if small_came is not None:
            small = small + small_came
        if r + 1 == len(space_sum[0][0]):
            space_last = last_swap(space_sum)
    at = 8 + action_table.shape[0]
    sums = small[at:]
    (down_out,) = join(*down, [width])
    (up_out,) = join(*up, [hidden])
    time_qkv, time_out = join(*time_last, [3 * width, width])
    space_qkv, space_out = join(*space_last, [3 * width, width])
    return (
        result_out,
        input_grad,
        jnp.concatenate([small[:2], sums[:2], sums[8:11], small[2:3]], 0),
        small[8:at],
        space_qkv,
        space_out,
        time_qkv,
        time_out,
        up_out,
        sums[16:].reshape(hidden),
        down_out,
    )


def hold_parts(*values):
    leaves, tree = jax.tree.flatten(values)
    arrays = [i for i, leaf in enumerate(leaves) if isinstance(leaf, jax.Array)]
    held = lax.optimization_barrier([leaves[i] for i in arrays])
    for i, leaf in zip(arrays, held):
        leaves[i] = leaf
    return jax.tree.unflatten(tree, leaves)


def solution(mesh):
    spread = P("tile", "clip", None, None)
    rows = P(("clip", "tile"), None)
    return jax.shard_map(
        body,
        mesh=mesh,
        in_specs=(spread, P("tile", "clip", None), P("clip", None)) + (P(),) * 9 + (spread,),
        out_specs=(spread, spread, P(), P(), rows, rows, rows, rows, rows, P(), rows),
        check_vma=False,
    )
```

```python
import jax
import jax.numpy as jnp
from jax import lax
from jax.experimental import pallas as pl
from jax.experimental.pallas import tpu as pltpu
from jax.sharding import PartitionSpec as P

HEADS = 16
HEAD_DIM = 64
PAIR = 2 * HEAD_DIM
EPSILON = 1e-05
NEGATIVE = -1e30
MASKED = 2.0**100
SEEN = 2.0**99
LOG2E = 1.4426950408889634
SCALE = HEAD_DIM**-0.5
F32 = jnp.float32
BF16 = jnp.bfloat16
VMEM_LIMIT = 60 * 1024 * 1024

NN = (((1,), (0,)), ((), ()))
NT = (((1,), (1,)), ((), ()))
TN = (((0,), (0,)), ((), ()))


def dot(left, right, form=NN):
    return lax.dot_general(left, right, form, preferred_element_type=F32)


def normalise(values):
    centred = values - jnp.mean(values, -1, keepdims=True)
    spread = lax.rsqrt(jnp.mean(centred * centred, -1, keepdims=True) + EPSILON)
    return centred * spread, spread


def norm_back(unit, spread, gain, upstream):
    scaled = upstream * gain
    return spread * (
        scaled
        - jnp.mean(scaled, -1, keepdims=True)
        - unit * jnp.mean(scaled * unit, -1, keepdims=True)
    )


def half_masks():
    lane = lax.broadcasted_iota(jnp.int32, (1, PAIR), 1)
    low = (lane < HEAD_DIM).astype(F32).astype(BF16)
    high = (lane >= HEAD_DIM).astype(F32).astype(BF16)
    return low, high


def pair_slices(packed, rows, width, pair):
    at = pair * PAIR
    return [packed[rows, part * width + at : part * width + at + PAIR] for part in range(3)]


def pair_slices(packed, rows, width, pair):
    at = pair * PAIR
    return [packed[rows, part * width + at : part * width + at + PAIR] for part in range(3)]


def attend_forward(packed, rows, width, out, total, bias, batch):
    masks = half_masks()
    lane = lax.broadcasted_iota(jnp.int32, (1, PAIR), 1)
    pairs = width // PAIR
    for first in range(0, pairs, batch):
        group = range(first, min(first + batch, pairs))
        loaded = [pair_slices(packed, rows, width, pair) for pair in group]
        scores = [
            dot(keys, queries * masks[side], NT) * (SCALE * LOG2E)
            for queries, keys, _ in loaded
            for side in range(2)
        ]
        if bias is not None:
            scores = [value + bias for value in scores]
        highest = [jnp.max(value, 0, keepdims=True) for value in scores]
        shares = [jnp.exp2(value - top) for value, top in zip(scores, highest)]
        weights = [jnp.sum(value, 0, keepdims=True) for value in shares]
        shares = [(value * (1.0 / weight)).astype(BF16) for value, weight in zip(shares, weights)]
        blended = [dot(value, loaded[i // 2][2], TN) for i, value in enumerate(shares)]
        total[2 * first : 2 * group.stop, rows] = jnp.concatenate(
            [top + jnp.log2(weight) for top, weight in zip(highest, weights)], 0
        )
        for i, pair in enumerate(group):
            out[rows, pair * PAIR : (pair + 1) * PAIR] = jnp.where(
                lane < HEAD_DIM, blended[2 * i], blended[2 * i + 1]
            ).astype(BF16)


def attend_forward_rows(packed, rows, width, out, total, batch):
    masks = half_masks()
    lane = lax.broadcasted_iota(jnp.int32, (1, PAIR), 1)
    pairs = width // PAIR
    for first in range(0, pairs, batch):
        group = range(first, min(first + batch, pairs))
        loaded = [pair_slices(packed, rows, width, pair) for pair in group]
        scores = [
            dot(queries * masks[side], keys, NT) * (SCALE * LOG2E)
            for queries, keys, _ in loaded
            for side in range(2)
        ]
        ones = [jnp.concatenate([v, jnp.ones_like(v)], 1) for _, _, v in loaded]
        highest = [jnp.max(value, 1, keepdims=True) for value in scores]
        shares = [jnp.exp2(value - top).astype(BF16) for value, top in zip(scores, highest)]
        blended = [dot(value, ones[i // 2]) for i, value in enumerate(shares)]
        sums = [b[:, PAIR:] for b in blended]
        blended = [b[:, :PAIR] * (1.0 / w) for b, w in zip(blended, sums)]
        logs = [top + jnp.log2(w) for top, w in zip(highest, sums)]
        for i, pair in enumerate(group):
            lg = jnp.where(lane < HEAD_DIM, logs[2*i], logs[2*i+1]).T
            total[2 * pair : 2 * pair + 1, rows] = lg[0:1]
            total[2 * pair + 1: 2 * pair + 2, rows] = lg[HEAD_DIM:HEAD_DIM+1]
            out[rows, pair * PAIR : (pair + 1) * PAIR] = jnp.where(
                lane < HEAD_DIM, blended[2 * i], blended[2 * i + 1]
            ).astype(BF16)


def attend_back(packed, rows, width, grad_out, total, bias, out, batch):
    masks = half_masks()
    pairs = width // PAIR
    for first in range(0, pairs, batch):
        group = range(first, min(first + batch, pairs))
        loaded = [pair_slices(packed, rows, width, pair) for pair in group]
        upstream = [grad_out[rows, pair * PAIR : (pair + 1) * PAIR] for pair in group]
        heads = [(i, side) for i in range(len(group)) for side in range(2)]
        own_q = [loaded[i][0] * masks[side] for i, side in heads]
        own_k = [loaded[i][1] * masks[side] for i, side in heads]
        own_up = [upstream[i] * masks[side] for i, side in heads]
        scores = [dot(loaded[i][1], own, NT) * (SCALE * LOG2E) for (i, _), own in zip(heads, own_q)]
        grad_shares = [dot(loaded[i][2], own, NT) for (i, _), own in zip(heads, own_up)]
        if bias is not None:
            scores = [value + bias for value in scores]
        sums = total[2 * first : 2 * group.stop, rows]
        shares = [jnp.exp2(value - sums[i : i + 1]) for i, value in enumerate(scores)]
        weighted = [value * grad for value, grad in zip(shares, grad_shares)]
        inner = [jnp.sum(value, 0, keepdims=True) for value in weighted]
        grad_scores = [
            (value - share * total_inner).astype(BF16)
            for value, share, total_inner in zip(weighted, shares, inner)
        ]
        grad_q = [dot(value, own, TN) for value, own in zip(grad_scores, own_k)]
        grad_k = [dot(value, own) for value, own in zip(grad_scores, own_q)]
        grad_v = [dot(value.astype(BF16), own) for value, own in zip(shares, own_up)]
        for i, pair in enumerate(group):
            at = pair * PAIR
            for part, (grad, scale) in enumerate(((grad_q, SCALE), (grad_k, SCALE), (grad_v, 1.0))):
                out[rows, part * width + at : part * width + at + PAIR] = (
                    (grad[2 * i] + grad[2 * i + 1]) * scale
                ).astype(BF16)


def embed(raw, vectors, actions):
    raw = raw.astype(F32)
    masked = raw > SEEN
    return jnp.where(masked, vectors[7:8, :], raw) + actions, masked


def space_forward_kernel(group, pieces, *refs):
    xs, (act, vectors, w_qkv, packed, out, total, *parts) = refs[:pieces], refs[pieces:]
    raw = jnp.concatenate([x[0] for x in xs], 0) if pieces > 1 else xs[0][0]
    count, width = raw.shape
    embedded, _ = embed(raw, vectors, act[0])
    unit, _ = normalise(embedded)
    normed = (unit * vectors[0:1, :] + vectors[1:2, :]).astype(BF16)
    packed[0] = dot(normed, w_qkv[...]).astype(BF16)
    attend_forward_rows(packed.at[0], slice(0, count), width, out.at[0], total.at[0], 4)
    share = count // group
    for j in range(group):
        parts[j][0, 0] = raw[j * share : (j + 1) * share]
        parts[j][0, 1] = out[0, j * share : (j + 1) * share]


def time_forward_kernel(sub, pieces, *refs):
    xs, o1s, refs = refs[:pieces], refs[pieces : 2 * pieces], refs[2 * pieces :]
    (act, perm, bias, vectors, w_space_out, w_qkv, w_out, h1, h2, a2, packed, o2, total) = refs
    x = jnp.concatenate([value[...] for value in xs], 0)
    o1 = jnp.concatenate([value[...] for value in o1s], 0)
    frames, places, width = x.shape
    count = frames * places
    raw = dot(perm[...], x.reshape(count, width))
    blended = dot(perm[...], o1.reshape(count, width)).astype(BF16)
    actions = jnp.broadcast_to(act[...][None], (places, frames, width)).reshape(count, width)
    embedded, _ = embed(raw, vectors, actions)
    after_space = embedded + dot(blended, w_space_out[...])
    h1[...] = after_space
    unit, _ = normalise(after_space)
    normed = (unit * vectors[2:3, :] + vectors[3:4, :]).astype(BF16)
    a2[...] = normed
    packed[...] = dot(normed, w_qkv[...]).astype(BF16)
    for start in range(0, count, sub):
        attend_forward(packed, slice(start, start + sub), width, o2, total, bias[...], 8)
    h2[...] = after_space + dot(o2[...], w_out[...])


def feed_kernel(tile, pieces, per, h2, *refs):
    cots, (vectors, b_up, w_up, w_down), refs = refs[:pieces], refs[pieces : pieces + 4], refs[pieces + 4 :]
    results, (cot, z, dur, a3, r2, sums, bias_grad) = refs[:pieces], refs[pieces:]
    piece = pl.program_id(0) // per
    for j in range(pieces):

        @pl.when(piece == j)
        def _(j=j):
            cot[...] = cots[j][...]

    @pl.when(pl.program_id(0) == 0)
    def _():
        sums[...] = jnp.zeros_like(sums)
        bias_grad[...] = jnp.zeros_like(bias_grad)

    after = h2[...]
    unit, spread = normalise(after)
    gain = vectors[4:5, :]
    normed = (unit * gain + vectors[5:6, :]).astype(BF16)
    a3[...] = normed
    upstream_low = cot[...]
    c = 0.7978845608028654
    total = after + vectors[6:7, :]
    grad_normed = jnp.zeros_like(after)
    for at in range(0, w_up.shape[1], tile):
        cols = slice(at, at + tile)
        hidden = dot(normed, w_up[:, cols]) + b_up[:, cols]
        grad_active = dot(upstream_low, w_down[cols, :], NT)
        square = hidden * hidden
        gate = 0.5 * jnp.tanh(hidden * (c + (c * 0.044715) * square)) + 0.5
        active = hidden * gate
        slope = gate + active * (1.0 - gate) * (2.0 * c + (6.0 * c * 0.044715) * square)
        grad_hidden = grad_active * slope
        bias_grad[:, cols] += jnp.sum(grad_hidden, 0, keepdims=True)
        active = active.astype(BF16)
        grad_hidden = grad_hidden.astype(BF16)
        z[:, cols] = active
        dur[:, cols] = grad_hidden
        total = total + dot(active, w_down[cols, :])
        grad_normed = grad_normed + dot(grad_hidden, w_up[:, cols], NT)
    for j in range(pieces):

        @pl.when(piece == j)
        def _(j=j):
            results[j][...] = total.astype(BF16)

    upstream = upstream_low.astype(F32)
    r2[...] = upstream + norm_back(unit, spread, gain, grad_normed)
    sums[0:1, :] += jnp.sum(grad_normed * unit, 0, keepdims=True)
    sums[1:2, :] += jnp.sum(grad_normed, 0, keepdims=True)
    sums[2:3, :] += jnp.sum(upstream, 0, keepdims=True)


def time_back_kernel(
    sub, r2, h1, packed, total, perm, bias, vectors, w_out, w_qkv, grad_packed, r2_low, sums, *rest
):
    *r1s, grad_out = rest

    @pl.when(pl.program_id(0) == 0)
    def _():
        sums[...] = jnp.zeros_like(sums)

    count, width = r2.shape
    stream = r2[...]
    low = stream.astype(BF16)
    r2_low[...] = low
    grad_out[...] = dot(low, w_out[...], NT).astype(BF16)
    for start in range(0, count, sub):
        attend_back(
            packed, slice(start, start + sub), width, grad_out, total, bias[...], grad_packed, 8
        )
    grad_normed = dot(grad_packed[...], w_qkv[...], NT)
    unit, spread = normalise(h1[...])
    stream = stream + norm_back(unit, spread, vectors[2:3, :], grad_normed)
    sums[0:1, :] += jnp.sum(grad_normed * unit, 0, keepdims=True)
    sums[1:2, :] += jnp.sum(grad_normed, 0, keepdims=True)
    r1 = dot(perm[...], stream.astype(BF16)).astype(BF16).reshape(-1, r1s[0].shape[1], width)
    share = r1s[0].shape[0]
    for j, piece in enumerate(r1s):
        piece[...] = r1[j * share : (j + 1) * share]


def space_back_kernel(pieces, group, order, *refs):
    xs, r1s, refs = refs[:pieces], refs[pieces : pieces + group], refs[pieces + group :]
    (act, hot, earlier, packed, total, vectors, w_out, w_qkv) = refs[:8]
    (grad_packed, a1, r1_all, sums), refs = refs[8:12], refs[12:]
    input_grads, (grad_out,) = refs[:-1], refs[-1:]

    @pl.when(pl.program_id(0) == 0)
    def _():
        sums[...] = earlier[...]

    raw = jnp.concatenate([x[0] for x in xs], 0) if pieces > 1 else xs[0][0]
    r1 = jnp.concatenate([value[0] for value in r1s], 0)
    r1_all[0] = r1
    count, width = raw.shape
    grad_out[...] = dot(r1, w_out[...], NT).astype(BF16)
    attend_back(
        packed.at[0], slice(0, count), width, grad_out, total.at[0], None, grad_packed.at[0], 4
    )
    grad_normed = dot(grad_packed[0], w_qkv[...], NT)
    embedded, masked = embed(raw, vectors, act[0])
    unit, spread = normalise(embedded)
    gain = vectors[0:1, :]
    a1[0] = (unit * gain + vectors[1:2, :]).astype(BF16)
    stream = r1.astype(F32) + norm_back(unit, spread, gain, grad_normed)
    kept = jnp.where(masked, 0.0, stream)
    if len(input_grads) == 1:
        input_grads[0][0] = kept.astype(BF16)
    else:
        share = count // len(order)
        for at, k in enumerate(order):
            input_grads[k // 2][k % 2, 0] = kept[at * share : (at + 1) * share].astype(BF16)
    whole_sum = jnp.sum(stream, 0, keepdims=True)
    sums[0:1, :] += jnp.sum(grad_normed * unit, 0, keepdims=True)
    sums[1:2, :] += jnp.sum(grad_normed, 0, keepdims=True)
    sums[2:3, :] += whole_sum - jnp.sum(kept, 0, keepdims=True)
    sums[8:, :] += hot[0] * whole_sum


def whole(array):
    rank = len(array.shape)
    return pl.BlockSpec(array.shape, lambda *_: (0,) * rank, pipeline_mode=pl.Buffered(1))


def struct(shape, kind):
    return jax.ShapeDtypeStruct(shape, kind)


def call(kernel, grid, operands, outs, scratch=(), flops=0, meta=None, sums=()):
    if sums:
        own, reads, makes, lead = kernel, len(operands), len(outs), meta is not None
        operands, outs = list(operands), list(outs)
        for arrays in sums:
            length = min(array.shape[0] for array in arrays)
            block = (length // grid[0],) + arrays[0].shape[1:]
            index = lambda i, *_, rank=arrays[0].ndim: (i,) + (0,) * (rank - 1)
            operands += [(array, block, index) for array in arrays]
            outs.append(((length,) + arrays[0].shape[1:], BF16, block, index))
        ends = lead + len(operands), lead + len(operands) + len(outs)

        def kernel(*refs):
            made = refs[ends[0] : ends[1]]
            own(*refs[: lead + reads], *made[:makes], *refs[ends[1] :])
            terms = refs[lead + reads : ends[0]]
            for arrays, out in zip(sums, made[makes:]):
                out[...] = sum(term[...].astype(F32) for term in terms[: len(arrays)]).astype(BF16)
                terms = terms[len(arrays) :]

    in_specs = [
        whole(array) if block is None else pl.BlockSpec(block, index)
        for array, block, index in operands
    ]
    out_specs = [
        pl.BlockSpec(shape, lambda *_, rank=len(shape): (0,) * rank)
        if block is None
        else pl.BlockSpec(block, index)
        for shape, _, block, index in outs
    ]
    moved = sum(a.size * a.dtype.itemsize for a, _, _ in operands)
    return pl.pallas_call(
        kernel,
        grid_spec=pltpu.PrefetchScalarGridSpec(
            num_scalar_prefetch=0 if meta is None else 1,
            grid=grid,
            in_specs=in_specs,
            out_specs=out_specs,
            scratch_shapes=scratch,
        ),
        out_shape=[struct(shape, kind) for shape, kind, _, _ in outs],
        cost_estimate=pl.CostEstimate(flops=flops, bytes_accessed=2 * moved, transcendentals=0),
        compiler_params=pltpu.CompilerParams(vmem_limit_bytes=VMEM_LIMIT),
    )(*(() if meta is None else (meta,)), *[a for a, _, _ in operands])


def collect_kernel(parts, meta, *refs):
    *refs, perm, out, held = refs
    chip = pl.program_id(0)
    for i in range(len(refs) // (2 * parts)):

        @pl.when(chip == i)
        def _(i=i):
            found = [ref[...] for ref in refs[2 * parts * i : 2 * parts * (i + 1)]]
            held[...] = jnp.concatenate(found, 0).reshape(held.shape)

    out[...] = dot(perm[...], held[...]).astype(BF16).reshape(out.shape)


def collect(by_slot, chips, perm, shape, operand):
    p, width = shape[0], shape[-1]
    block = 16
    steps = p // block
    parts = len(by_slot[0])
    span = sum(part.shape[-3] for part, _ in by_slot[0])
    count = len(by_slot)
    operands = []
    for k, pieces in enumerate(by_slot):

        def slot_index(i, h, meta, k=k):
            return 0, jnp.where(i == k // 2, h, jnp.where(i < k // 2, 0, steps - 1)), 0

        operands += [
            operand(piece, (piece[0].shape[-3], block, width), slot_index) for piece in pieces
        ]
    operands.append((perm, None, None))
    outs = [
        (
            (p, count * span, width),
            BF16,
            (block, 2 * span, width),
            lambda i, h, meta: (h, meta[i], 0),
        )
    ]
    return call(
        lambda *refs: collect_kernel(parts, *refs),
        (count // 2, steps),
        operands,
        outs,
        [pltpu.VMEM((block * 2 * span, width), BF16)],
        meta=chips,
    )[0].reshape(shape)


def collect_result_kernel(meta, *refs):
    *pieces, out = refs
    for j, piece in enumerate(pieces):

        @pl.when(pl.program_id(0) == j)
        def _(piece=piece):
            out[...] = piece[...]


def collect_result(pieces, where):
    p, _, frames, width = pieces[0].shape
    return call(
        collect_result_kernel,
        (len(pieces),),
        [(piece, None, None) for piece in pieces],
        [
            (
                (p, len(pieces), frames, width),
                BF16,
                (p, 1, frames, width),
                lambda j, meta: (0, meta[j], 0, 0),
            )
        ],
        meta=where,
    )[0]


def put(outs, slot, value):
    share = outs[0].shape[0]
    outs[slot // share][slot % share] = value


def columns_kernel(meta, *refs, counts, firsts, blocks, split):
    step = pl.program_id(0)
    *refs, held = refs
    local = step % firsts[-1]
    for i, count in enumerate(counts):
        lefts, rights, refs = refs[:count], refs[count : 2 * count], refs[2 * count :]

        @pl.when((local >= firsts[i]) & (local < firsts[i + 1]))
        def _(lefts=lefts, rights=rights):
            total = sum(dot(l[...], r[...], TN) for l, r in zip(lefts, rights))
            held[...] = total.astype(BF16)

    shares = len(split)
    size = held.shape[0] // blocks
    per = firsts[-1] // shares
    for part in range(2 * shares):
        two = part >= shares and split[part - shares]
        own, refs = refs[: 1 + two], refs[1 + two :]

        @pl.when(step // per == part)
        def _(first=(part % shares) * blocks, own=own):
            for slot in range(blocks):
                source = pl.multiple_of(meta[first + slot] * size, size)
                put(own, slot, held[pl.ds(source, size), :])


def columns_grad(pairs, meta, split, tile=512, sums=()):
    shares = len(split)
    blocks = (meta.shape[0] - 1) // shares
    height = pairs[0][0][0].shape[1]
    size = height // blocks
    tile = min([tile] + [rights[0].shape[1] // 2 for _, rights in pairs])
    steps = [rights[0].shape[1] // 2 // tile for _, rights in pairs]
    firsts = [sum(steps[:i]) for i in range(len(steps) + 1)]
    per = firsts[-1] // shares
    operands, flops = [], 0
    for (lefts, rights), first, count in zip(pairs, firsts, steps):
        operands += [(left, None, None) for left in lefts]
        for right in rights:

            def index(i, meta, first=first, count=count):
                core = meta[shares * blocks]
                half = jnp.where(i < firsts[-1], 1 - core, core)
                return 0, half * count + jnp.clip(i % firsts[-1] - first, 0, count - 1)

            operands.append((right, (right.shape[0], tile), index))
            flops += 2 * right.size * height

    def part_out(part, rows):
        block = (rows, size, tile), lambda i, meta: (0, 0, jnp.clip(i - part * per, 0, per - 1))
        return (rows, size, per * tile), BF16, *block

    outs = [part_out(share, blocks) for share in range(shares)]
    for share, two in enumerate(split):
        outs += [part_out(shares + share, blocks // (1 + two))] * (1 + two)
    kernel = lambda *refs: columns_kernel(
        *refs, counts=[len(lefts) for lefts, _ in pairs], firsts=firsts, blocks=blocks, split=split
    )
    scratch = [pltpu.VMEM((height, tile), BF16)]
    return call(kernel, (2 * firsts[-1],), operands, outs, scratch, flops, meta, sums)


def rows_kernel(meta, *refs, step_blocks, steps, blocks):
    step = pl.program_id(0)
    lefts, right, (sent, *outs) = refs[:step_blocks], refs[step_blocks], refs[step_blocks + 1 :]
    value = dot(jnp.concatenate([left[...] for left in lefts], 1), right[...], TN).astype(BF16)
    value = value.reshape(step_blocks, -1, value.shape[-1])
    middle = value.shape[-1] // 2
    halves = value[:, :, :middle], value[:, :, middle:]
    share = steps // len(outs)
    for core in range(2):

        @pl.when(meta[blocks] == core)
        def _(core=core):
            sent[...] = halves[1 - core]

        for i, out in enumerate(outs):

            @pl.when((meta[blocks] == core) & (step >= i * share) & (step < (i + 1) * share))
            def _(core=core, out=out):
                out[...] = halves[core]


def rows_grad(left, right, meta, split, step_blocks=2):
    blocks = meta.shape[0] - 1
    depth, height = left.shape
    size, columns = height // blocks, right.shape[1] // 2
    steps = blocks // step_blocks
    operands = [
        (left, (depth, size), lambda i, meta, j=j: (0, meta[i * step_blocks + j]))
        for j in range(step_blocks)
    ]
    operands.append((right, None, None))
    parts = 1 + split[0]
    share = steps // parts
    block = (step_blocks, size, columns)
    outs = [((blocks, size, columns), BF16, block, lambda i, meta: (i, 0, 0))]
    outs += [
        (
            (blocks // parts, size, columns),
            BF16,
            block,
            lambda i, meta, first=j * share: (jnp.clip(i - first, 0, share - 1), 0, 0),
        )
        for j in range(parts)
    ]
    kernel = lambda *refs: rows_kernel(
        *refs, step_blocks=step_blocks, steps=steps, blocks=blocks
    )
    return call(kernel, (steps,), operands, outs, flops=4 * depth * height * columns, meta=meta)


def body(
    tokens,
    mask_bits,
    action_ids,
    vectors,
    action_table,
    w_space_qkv,
    w_space_out,
    w_time_qkv,
    w_time_out,
    w_up,
    b_up,
    w_down,
    cotangent,
):
    p, clips, frames, width = tokens.shape
    n, layers = lax.axis_size("tile"), lax.axis_size("clip")
    me, layer = lax.axis_index("tile"), lax.axis_index("clip")
    core = me % 2
    group = n // clips
    own_frames = frames // group
    grid_all = n * p
    places = grid_all // group
    clip, part = me // group, me % group
    hidden = w_up.shape[1]
    rows = places * frames

    def swap(value, k, axis="tile"):
        size = lax.axis_size(axis)
        return lax.ppermute(value, axis, [(i, i ^ k) for i in range(size)])

    def row_block(*shape):
        return shape, lambda i: (i,) + (0,) * (len(shape) - 1)

    blocks = n * layers // 2
    tile_bits = [1 << b for b in range(1, n.bit_length() - 1)]

    def orders(hops):
        slots = [(0, None, 0, None)]
        for hop in hops:
            if hop == "scatter":
                choices = [(0, None, 0, c) for c in range(layers)]
            elif hop == "tiles":
                choices = [(0, t, 0, None) for t in range(n // 2)]
            elif hop == "spread":
                choices = [(0, None, c, None) for c in range(layers)]
            else:
                bit = (hop[1], None, 0, None) if hop[0] == "tile" else (0, None, hop[1], None)
                choices = [(0, None, 0, None), bit]
            slots = [
                (a ^ x, t if u is None else u, b ^ y, c if d is None else d)
                for a, t, b, c in slots
                for x, u, y, d in choices
            ]
        where = [
            (layer ^ b if c is None else c) * (n // 2) + ((me ^ a) // 2 if t is None else t)
            for a, t, b, c in slots
        ]
        return jnp.stack([jnp.asarray(w, jnp.int32) for w in where])

    def halves(value, hop):
        if hop is None or isinstance(hop, str):
            return [value]
        middle = value.shape[0] // 2
        return [value[:middle], value[middle:]]

    def meta_of(chains):
        return jnp.concatenate([orders(hops) for hops in chains] + [core.astype(jnp.int32)[None]])

    def begin(make, chains, meta):
        split = [not isinstance(hops[0], str) for hops in chains]
        made = make(meta, split)
        sent, made, parts = list(made[: len(split)]), made[len(split) :], []
        for two in split:
            parts.append(list(made[: 1 + two]))
            made = made[1 + two :]
        return chains, parts, sent

    def cross(begun):
        chains, parts, sent = begun
        return chains, parts, [swap(value, 1) for value in sent]

    def add(values, kind):
        return sum(value.astype(F32) for value in values).astype(kind)

    def land(crossed):
        chains, all_parts, received = crossed
        landed = []
        for hops, parts, came in zip(chains, all_parts, received):
            if isinstance(hops[0], str):
                landed.append([[(add([parts[0], came], BF16), False)]])
            else:
                _, sent = halves(came, hops[0])
                landed.append([[(parts[0], False), (came, True)], add([parts[1], sent], BF16)])
        return chains, landed, 0

    def addends(departed):
        (chains, parts, at), coming = departed
        return [value for value, _ in parts[0][0]] + coming

    def arrived(departed, total):
        chains, parts, at = departed[0]
        hops = chains[0]
        pieces = halves(total, hops[at + 1] if at + 1 < len(hops) else None)
        return chains, [[[(total, len(pieces) == 2)]] + pieces[1:]], at + 1

    def merge(state):
        chains, parts, at = state
        kept = jnp.concatenate([own[0][0][0] for own in parts], -1)
        return chains[:1], [[[(kept, False)]]], at

    def depart(state):
        chains, parts, at = state
        coming = []
        for hops, own in zip(chains, parts):
            hop, value = hops[at], own[0][0][0]
            if hop == "scatter":
                coming.append(lax.psum_scatter(value, "clip", scatter_dimension=0, tiled=True))
            elif hop == "tiles":
                same_core = [list(range(c, n, 2)) for c in range(2)]
                coming.append(
                    lax.psum_scatter(
                        value, "tile", scatter_dimension=0, tiled=True, axis_index_groups=same_core
                    )
                )
            elif hop == "spread":
                share = value.shape[0] // layers
                coming.append(
                    [swap(value[j * share : (j + 1) * share], j, "clip") for j in range(1, layers)]
                )
            else:
                coming.append(swap(own[1], hop[1], hop[0]))
        return state, coming

    def arrive(departed):
        (chains, parts, at), coming = departed
        new_parts = []
        for hops, own, came in zip(chains, parts, coming):
            following = hops[at + 1] if at + 1 < len(hops) else None
            kind = F32 if following is None else BF16
            kept = [v[: v.shape[0] // 2] if first else v for v, first in own[0]]
            if hops[at] == "spread":
                values = [kept[0][: kept[0].shape[0] // layers]] + came
            else:
                values = [came] if isinstance(hops[at], str) else kept + [came]
            summed = [add(piece, kind) for piece in zip(*[halves(v, following) for v in values])]
            new_parts.append([[(summed[0], False)]] + summed[1:])
        return chains, new_parts, at + 1

    def last_swap(state):
        own = jnp.concatenate([own[0][0][0][0].astype(F32) for own in state[1]], 1)
        size = own.shape[0] // 2
        mine = lax.dynamic_slice_in_dim(own, core * size, size, 0)
        other = lax.dynamic_slice_in_dim(own, (1 - core) * size, size, 0)
        return mine, swap(other.astype(BF16), 1)

    def join(mine, other, widths):
        whole_parts, at = [], 0
        for w in widths:
            a, b = mine[:, at : at + w // 2], other[:, at : at + w // 2].astype(F32)
            whole_parts.append(
                jnp.where(core == 0, jnp.concatenate([a, b], 1), jnp.concatenate([b, a], 1))
            )
            at += w // 2
        return whole_parts

    one_way = [("tile", bit) for bit in tile_bits]
    other_way = one_way[::-1]
    clip_bits = [("clip", 1 << b) for b in range(layers.bit_length() - 1)]
    up_chains, down_chains = [one_way + clip_bits], [["scatter"] + one_way]
    time_chains = [["scatter"] + other_way]
    space_chains = [one_way + ["spread"], other_way + ["spread"]]

    order = [k for j in range(group) for k in range(j, n, group)]
    onehot = (action_ids[..., None] == lax.iota(jnp.int32, action_table.shape[0])).astype(F32)
    action_rows = jnp.einsum("cfa,ad->cfd", onehot, action_table, precision=lax.Precision.HIGHEST)
    act_time = lax.dynamic_index_in_dim(action_rows, clip, 0, keepdims=False)
    act_space = lax.dynamic_slice_in_dim(act_time, part * own_frames, own_frames, 0)[:, None, :]

    regular = p % 16 == 0 and 2 * own_frames == 16
    deal_back = None
    if regular:
        at = lax.iota(jnp.int32, 16 * 2 * own_frames)
        place, frame = at % 16, at // 16
        source = place * 2 * own_frames + (frame + core * own_frames) % (2 * own_frames)
        deal_back = (at[:, None] == source[None, :]).astype(BF16)
    marked = jnp.where((mask_bits > 0)[..., None], jnp.asarray(MASKED, BF16), tokens)
    marked = marked.reshape(p, n, own_frames, width)
    chunks = 2
    span = own_frames // chunks
    blocks_of = [lax.dynamic_index_in_dim(marked, me ^ k, 1, keepdims=False) for k in order]
    sources = [
        [value[:, c * span : (c + 1) * span].transpose(1, 0, 2) for value in blocks_of]
        for c in range(chunks)
    ]

    def send_out(parts):
        return [part if k == 0 else swap(part, k) for k, part in zip(order, parts)]

    cot_pieces = [
        lax.dynamic_index_in_dim(cotangent, clip ^ j, 1, keepdims=False).reshape(p * frames, width)
        for j in range(n // group)
    ]
    block = 16
    count = block * frames
    sub = min(count, 128)
    index = lax.iota(jnp.int32, count)
    slot, place = index // block, index % block
    frame_of_slot = ((part ^ (slot // own_frames)) * own_frames) + slot % own_frames
    target = place * frames + frame_of_slot
    perm_back = (target[:, None] == index[None, :]).astype(BF16)
    perm = (index[:, None] == target[None, :]).astype(BF16)
    seq = lax.iota(jnp.int32, sub)
    same = (seq[:, None] // frames) == (seq[None, :] // frames)
    bias = jnp.where(same & (seq[:, None] <= seq[None, :]), 0.0, NEGATIVE).astype(F32)
    own_hot = lax.dynamic_slice_in_dim(
        lax.dynamic_index_in_dim(onehot, clip, 0, keepdims=False), part * own_frames, own_frames, 0
    )[..., None]
    where_clip = clip ^ lax.iota(jnp.int32, clips)
    where_chip = (me // 2) ^ lax.iota(jnp.int32, n // 2)
    tables = dict(
        act_time=act_time,
        act_space=act_space,
        perm=perm,
        perm_back=perm_back,
        bias=bias,
        own_hot=own_hot,
        where_clip=where_clip,
        where_chip=where_chip,
        deal_back=deal_back,
        **{
            name: meta_of(chains)
            for name, chains in (
                ("up", up_chains),
                ("down", down_chains),
                ("time", time_chains),
                ("space", space_chains),
            )
        },
    )
    pieces = []
    for c in range(chunks):
        pieces.append(send_out(sources[c]))
        if c == 0:
            pieces[0], sources, cot_pieces, tables = hold_parts(
                pieces[0], sources, cot_pieces, tables
            )
    cot_pieces = [
        piece if j == 0 else swap(piece, j * group) for j, piece in enumerate(cot_pieces)
    ]
    if p % 16:
        pieces = [[jnp.concatenate(parts, 1)] for parts in pieces]
    kinds = len(pieces[0])
    act_time, act_space, own_hot = (tables[name] for name in ("act_time", "act_space", "own_hot"))
    perm, perm_back, bias = (tables[name] for name in ("perm", "perm_back", "bias"))
    where_clip, where_chip, deal_back = (
        tables[name] for name in ("where_clip", "where_chip", "deal_back")
    )

    head_flops = 2 * HEADS * HEAD_DIM

    def frame_block(*shape):
        return (1,) + shape, lambda i: (i, 0, 0)

    def chunk_block(first, *shape):
        return (1,) + shape, lambda i: (first + i, 0, 0)

    space, both = [], []
    for c in range(chunks):
        packed, o1, total, *parts = call(
            lambda *refs: space_forward_kernel(group, kinds, *refs),
            (span,),
            [(x, *frame_block(*x.shape[1:])) for x in pieces[c]]
            + [
                (act_space, *chunk_block(c * span, 1, width)),
                (vectors, None, None),
                (w_space_qkv, None, None),
            ],
            [
                ((span, grid_all, 3 * width), BF16, *frame_block(grid_all, 3 * width)),
                ((span, grid_all, width), BF16, *frame_block(grid_all, width)),
                ((span, HEADS, grid_all), F32, *frame_block(HEADS, grid_all)),
            ]
            + [
                (
                    (span, 2, places, width),
                    BF16,
                    (1, 2, places, width),
                    lambda i: (i, 0, 0, 0),
                )
            ]
            * group,
            flops=2 * span * grid_all * width * 3 * width
            + 16 * span * grid_all * grid_all * head_flops,
        )
        space.append((packed, o1, total))
        both.append([part if j == 0 else swap(part, j) for j, part in enumerate(parts)])
    both = [both[c][j] for j in range(group) for c in range(chunks)]

    def slot_block(size):
        return (size, block, width), lambda i: (0, i, 0)

    total_block = ((HEADS, count), lambda i: (0, i))
    h1, h2, a2, packed_two, o2, total_two = call(
        lambda *refs: time_forward_kernel(sub, len(both), *refs),
        (places // block,),
        [
            (value, (span, None, block, width), lambda i, which=which: (0, which, i, 0))
            for which in range(2)
            for value in both
        ]
        + [
            (act_time, None, None),
            (perm, None, None),
            (bias, None, None),
            (vectors, None, None),
            (w_space_out, None, None),
            (w_time_qkv, None, None),
            (w_time_out, None, None),
        ],
        [
            ((rows, width), F32, *row_block(count, width)),
            ((rows, width), F32, *row_block(count, width)),
            ((rows, width), BF16, *row_block(count, width)),
            ((rows, 3 * width), BF16, *row_block(count, 3 * width)),
            ((rows, width), BF16, *row_block(count, width)),
            ((HEADS, rows), F32, *total_block),
        ],
        flops=2 * rows * width * 5 * width + 16 * rows * sub * head_flops,
    )

    step = min(p * frames, 256)
    per = p * frames // step

    def piece_block(j):
        return (step, width), lambda i, j=j: (jnp.clip(i - j * per, 0, per - 1), 0)

    *result_pieces, cot, z, dur, a3, r2, sums_three, bias_up = call(
        lambda *refs: feed_kernel(1024, len(cot_pieces), per, *refs),
        (rows // step,),
        [(h2, *row_block(step, width))]
        + [(piece, *piece_block(j)) for j, piece in enumerate(cot_pieces)]
        + [
            (vectors, None, None),
            (b_up[None, :], None, None),
            (w_up, None, None),
            (w_down, None, None),
        ],
        [((p * frames, width), BF16, *piece_block(j)) for j in range(len(cot_pieces))]
        + [
            ((rows, width), BF16, *row_block(step, width)),
            ((rows, hidden), BF16, *row_block(step, hidden)),
            ((rows, hidden), BF16, *row_block(step, hidden)),
            ((rows, width), BF16, *row_block(step, width)),
            ((rows, width), F32, *row_block(step, width)),
            ((8, width), F32, None, None),
            ((1, hidden), F32, None, None),
        ],
        flops=8 * rows * width * hidden,
    )

    result_pieces = [
        (piece if j == 0 else swap(piece, j * group)).reshape(p, 1, frames, width)
        for j, piece in enumerate(result_pieces)
    ]

    def make_down(meta, split):
        if hidden // blocks % 128:
            return columns_grad([([z], [cot])], meta, split, 256)
        return rows_grad(z, cot, meta, split)

    def make_up(meta, split):
        return columns_grad([([a3], [dur])], meta, split)

    up = begin(make_up, up_chains, tables["up"])
    cot, up, result_pieces[:-1] = hold_parts(cot, up, result_pieces[:-1])
    up = cross(up)
    down = begin(make_down, down_chains, tables["down"])
    r2, down, up, result_pieces = hold_parts(r2, down, up, result_pieces)
    up, down = depart(land(up)), cross(down)

    grad_packed_two, r2_low, sums_two, *r1_parts = call(
        lambda *refs: time_back_kernel(sub, *refs),
        (places // block,),
        [
            (r2, *row_block(count, width)),
            (h1, *row_block(count, width)),
            (packed_two, *row_block(count, 3 * width)),
            (total_two, *total_block),
            (perm_back, None, None),
            (bias, None, None),
            (vectors, None, None),
            (w_time_out, None, None),
            (w_time_qkv, None, None),
        ],
        [
            ((rows, 3 * width), BF16, *row_block(count, 3 * width)),
            ((rows, width), BF16, *row_block(count, width)),
            ((8, width), F32, None, None),
        ]
        + [((own_frames, places, width), BF16, *slot_block(own_frames))] * group,
        [pltpu.VMEM((count, width), BF16)],
        flops=2 * rows * width * 4 * width + 40 * rows * sub * head_flops,
    )
    grad_packed_two, up, down = hold_parts(grad_packed_two, up, down)
    r1_parts = [r1 if j == 0 else swap(r1, j) for j, r1 in enumerate(r1_parts)]
    extra = []

    def make_time(meta, split):
        pairs = [([a2], [grad_packed_two]), ([o2], [r2_low])]
        beside = [[down[1][0][0], down[2][0]], addends(up)]
        *made, down_total, up_total = columns_grad(pairs, meta, split, sums=beside)
        extra.extend((down_total, up_total))
        return made

    time = begin(make_time, time_chains, tables["time"])
    down = down[0], [[[(extra[0], False)]]], 0
    up = arrived(up, extra[1])

    dealt = 1 if p % 16 else n

    def send_back(parts):
        if dealt == 1:
            parts = [parts[0][:, at * p : (at + 1) * p] for at in range(n)]
            parts = [parts[order.index(k)] for k in range(n)]
            parts = [jnp.stack(parts[2 * j : 2 * j + 2]) for j in range(n // 2)]
        return [part if j == 0 else swap(part, 2 * j) for j, part in enumerate(parts)]

    def pass_on(came):
        crossed = swap(jnp.stack([value[1] for value in came]), 1)
        return [found for j, value in enumerate(came) for found in ((value, 0), (crossed, j))]

    def operand(found, block, index):
        return found[0], (None,) + block, lambda *i: (found[1],) + index(*i)

    def space_back(c, earlier, sums=()):
        packed, _, total = space[c]
        return call(
            lambda *refs: space_back_kernel(kinds, group, order, *refs),
            (span,),
            [(x, *frame_block(*x.shape[1:])) for x in pieces[c]]
            + [(r1, *chunk_block(c * span, places, width)) for r1 in r1_parts]
            + [
                (act_space, *chunk_block(c * span, 1, width)),
                (own_hot, *chunk_block(c * span, action_table.shape[0], 1)),
                (earlier, None, None),
                (packed, *frame_block(grid_all, 3 * width)),
                (total, *frame_block(HEADS, grid_all)),
                (vectors, None, None),
                (w_space_out, None, None),
                (w_space_qkv, None, None),
            ],
            [
                ((span, grid_all, 3 * width), BF16, *frame_block(grid_all, 3 * width)),
                ((span, grid_all, width), BF16, *frame_block(grid_all, width)),
                ((span, grid_all, width), BF16, *frame_block(grid_all, width)),
                ((8 + action_table.shape[0], width), F32, None, None),
            ]
            + (
                [((span, grid_all, width), BF16, *frame_block(grid_all, width))]
                if dealt == 1
                else [
                    ((2, span, p, width), BF16, (2, 1, p, width), lambda i: (0, i, 0, 0))
                ]
                * (n // 2)
            ),
            [pltpu.VMEM((grid_all, width), BF16)],
            flops=2 * span * grid_all * width * 4 * width
            + 40 * span * grid_all * grid_all * head_flops,
            sums=sums,
        )

    r1_parts, time, up, down = hold_parts(r1_parts, time, up, down)
    up, down, time = depart(up), depart(down), cross(time)
    early = jnp.concatenate([sums_two, sums_three, bias_up.reshape(-1, width)], 0)
    back = [space_back(0, jnp.zeros((8 + action_table.shape[0], width), F32))]
    back[0], r1_parts, time, up = hold_parts(back[0], r1_parts, time, up)
    input_pieces = [send_back(back[0][4:])]
    up = depart(arrive(up))
    for c in range(1, chunks):
        beside = [[time[1][0][0], time[2][0]]] if c == 1 else []
        back.append(space_back(c, back[-1][3], beside))
        if c == 1:
            *back[c], time_total = back[c]
    time = time[0], [[[(time_total, False)]]], 0
    back, input_pieces, up, time = hold_parts(back, input_pieces, up, time)
    input_pieces[0] = pass_on(input_pieces[0])
    for c in range(1, chunks):
        input_pieces.append(send_back(back[c][4:]))
    up, time = depart(arrive(up)), depart(time)
    grads_one, a1s, r1s = list(zip(*back))[:3]

    def flat(values):
        return [value.reshape(-1, value.shape[-1]) for value in values]

    def make_space(meta, split):
        return columns_grad(
            [
                (flat(a1s), flat(grads_one)),
                (flat([o1 for _, o1, _ in space]), flat(r1s)),
            ],
            meta,
            split,
        )

    small = jnp.concatenate([back[-1][3], early], 0)
    small_hops = [("tile", 1 << b) for b in range(n.bit_length() - 1)] + clip_bits

    space_sum = begin(make_space, space_chains, tables["space"])
    where_clip, space_sum, up, down, input_pieces = hold_parts(
        where_clip, space_sum, up, down, input_pieces
    )
    space_sum = cross(space_sum)
    small_came = swap(small, small_hops[0][1], small_hops[0][0])
    up = arrive(up)
    while up[2] < len(up[0][0]):
        up = arrive(depart(up))
    up, down = last_swap(up), depart(arrive(down))
    result_out = collect_result(result_pieces, where_clip)
    space_sum, result_out, small_came = hold_parts(space_sum, result_out, small_came)
    space_sum, small = land(space_sum), small + small_came
    input_pieces[1:] = [pass_on(came) for came in input_pieces[1:]]
    time = arrive(time)

    def collect_input(input_pieces, where_chip):
        by_slot = [[pieces_of[k] for pieces_of in input_pieces] for k in range(n)]
        if regular:
            input_grad = collect(by_slot, where_chip, deal_back, tokens.shape, operand)
        else:
            input_grad = jnp.zeros((p, n, own_frames, width), BF16)
            for k, parts in enumerate(by_slot):
                piece = jnp.concatenate([value[at] for value, at in parts], 0)
                input_grad = lax.dynamic_update_slice_in_dim(
                    input_grad, piece.transpose(1, 0, 2)[:, None], me ^ k, 1
                )
            input_grad = input_grad.reshape(tokens.shape)
        return input_grad

    rounds = max(len(small_hops) - 1, len(space_sum[0][0]) + 1, 2 * len(one_way) + 1)
    for r in range(rounds):
        departed = small_came = time_moves = down_moves = None
        if r < len(space_sum[0][0]):
            if r == len(one_way):
                space_sum = merge(space_sum)
            departed = depart(space_sum)
        if r + 1 < len(small_hops):
            small_came = swap(small, small_hops[r + 1][1], small_hops[r + 1][0])
        if r >= len(one_way) and time[2] < len(time[0][0]):
            time_moves = depart(time)
        if r > len(one_way) and down[2] < len(down[0][0]):
            down_moves = depart(down)
        others = [down, input_pieces, up] if r == 0 else []
        if r == 1:
            input_grad = collect_input(input_pieces, where_chip)
            others = [input_grad]
        departed, small_came, time_moves, down_moves, *others = hold_parts(
            departed, small_came, time_moves, down_moves, *others
        )
        if r == 0:
            down, input_pieces, up = others
            down = arrive(down)
        if r == 1:
            (input_grad,) = others
        if time_moves is not None:
            time = arrive(time_moves)
            if time[2] == len(time[0][0]):
                time_last = last_swap(time)
        if down_moves is not None:
            down = arrive(down_moves)
            if down[2] == len(down[0][0]):
                down_last = last_swap(down)
        if departed is not None:
            space_sum = arrive(departed)
        if small_came is not None:
            small = small + small_came
        if r + 1 == len(space_sum[0][0]):
            space_last = last_swap(space_sum)
    at = 8 + action_table.shape[0]
    sums = small[at:]
    (down_out,) = join(*down_last, [width])
    (up_out,) = join(*up, [hidden])
    time_qkv, time_out = join(*time_last, [3 * width, width])
    space_qkv, space_out = join(*space_last, [3 * width, width])
    return (
        result_out,
        input_grad,
        jnp.concatenate([small[:2], sums[:2], sums[8:11], small[2:3]], 0),
        small[8:at],
        space_qkv,
        space_out,
        time_qkv,
        time_out,
        up_out,
        sums[16:].reshape(hidden),
        down_out,
    )


def hold_parts(*values):
    leaves, tree = jax.tree.flatten(values)
    arrays = [i for i, leaf in enumerate(leaves) if isinstance(leaf, jax.Array)]
    held = lax.optimization_barrier([leaves[i] for i in arrays])
    for i, leaf in zip(arrays, held):
        leaves[i] = leaf
    return jax.tree.unflatten(tree, leaves)


def solution(mesh):
    spread = P("tile", "clip", None, None)
    rows = P(("clip", "tile"), None)
    return jax.shard_map(
        body,
        mesh=mesh,
        in_specs=(spread, P("tile", "clip", None), P("clip", None)) + (P(),) * 9 + (spread,),
        out_specs=(spread, spread, P(), P(), rows, rows, rows, rows, rows, P(), rows),
        check_vma=False,
    )
```

```python
import jax
import jax.numpy as jnp
from jax import lax
from jax.experimental import pallas as pl
from jax.experimental.pallas import tpu as pltpu
from jax.sharding import PartitionSpec as P

HEADS = 16
HEAD_DIM = 64
PAIR = 2 * HEAD_DIM
EPSILON = 1e-05
NEGATIVE = -1e30
MASKED = 2.0**100
SEEN = 2.0**99
LOG2E = 1.4426950408889634
SCALE = HEAD_DIM**-0.5
F32 = jnp.float32
BF16 = jnp.bfloat16
VMEM_LIMIT = 60 * 1024 * 1024

NN = (((1,), (0,)), ((), ()))
NT = (((1,), (1,)), ((), ()))
TN = (((0,), (0,)), ((), ()))


def dot(left, right, form=NN):
    return lax.dot_general(left, right, form, preferred_element_type=F32)


def normalise(values):
    centred = values - jnp.mean(values, -1, keepdims=True)
    spread = lax.rsqrt(jnp.mean(centred * centred, -1, keepdims=True) + EPSILON)
    return centred * spread, spread


def norm_back(unit, spread, gain, upstream):
    scaled = upstream * gain
    return spread * (
        scaled
        - jnp.mean(scaled, -1, keepdims=True)
        - unit * jnp.mean(scaled * unit, -1, keepdims=True)
    )


def half_masks():
    lane = lax.broadcasted_iota(jnp.int32, (1, PAIR), 1)
    low = (lane < HEAD_DIM).astype(F32).astype(BF16)
    high = (lane >= HEAD_DIM).astype(F32).astype(BF16)
    return low, high


def pair_slices(packed, rows, width, pair):
    at = pair * PAIR
    return [packed[rows, part * width + at : part * width + at + PAIR] for part in range(3)]


def pair_slices(packed, rows, width, pair):
    at = pair * PAIR
    return [packed[rows, part * width + at : part * width + at + PAIR] for part in range(3)]


def attend_forward(packed, rows, width, out, total, bias, batch):
    masks = half_masks()
    lane = lax.broadcasted_iota(jnp.int32, (1, PAIR), 1)
    pairs = width // PAIR
    for first in range(0, pairs, batch):
        group = range(first, min(first + batch, pairs))
        loaded = [pair_slices(packed, rows, width, pair) for pair in group]
        scores = [
            dot(keys, queries * masks[side], NT) * (SCALE * LOG2E)
            for queries, keys, _ in loaded
            for side in range(2)
        ]
        if bias is not None:
            scores = [value + bias for value in scores]
        highest = [jnp.max(value, 0, keepdims=True) for value in scores]
        shares = [jnp.exp2(value - top) for value, top in zip(scores, highest)]
        weights = [jnp.sum(value, 0, keepdims=True) for value in shares]
        shares = [(value * (1.0 / weight)).astype(BF16) for value, weight in zip(shares, weights)]
        blended = [dot(value, loaded[i // 2][2], TN) for i, value in enumerate(shares)]
        total[2 * first : 2 * group.stop, rows] = jnp.concatenate(
            [top + jnp.log2(weight) for top, weight in zip(highest, weights)], 0
        )
        for i, pair in enumerate(group):
            out[rows, pair * PAIR : (pair + 1) * PAIR] = jnp.where(
                lane < HEAD_DIM, blended[2 * i], blended[2 * i + 1]
            ).astype(BF16)


def attend_forward_rows(packed, rows, width, out, total, batch):
    masks = half_masks()
    lane = lax.broadcasted_iota(jnp.int32, (1, PAIR), 1)
    pairs = width // PAIR
    for first in range(0, pairs, batch):
        group = range(first, min(first + batch, pairs))
        loaded = [pair_slices(packed, rows, width, pair) for pair in group]
        scores = [
            dot(queries * masks[side], keys, NT) * (SCALE * LOG2E)
            for queries, keys, _ in loaded
            for side in range(2)
        ]
        ones = [jnp.concatenate([v, jnp.ones_like(v)], 1) for _, _, v in loaded]
        highest = [jnp.max(value, 1, keepdims=True) for value in scores]
        shares = [jnp.exp2(value - top).astype(BF16) for value, top in zip(scores, highest)]
        blended = [dot(value, ones[i // 2]) for i, value in enumerate(shares)]
        sums = [b[:, PAIR:] for b in blended]
        blended = [b[:, :PAIR] * (1.0 / w) for b, w in zip(blended, sums)]
        logs = [top + jnp.log2(w) for top, w in zip(highest, sums)]
        for i, pair in enumerate(group):
            lg = jnp.where(lane < HEAD_DIM, logs[2*i], logs[2*i+1]).T
            total[2 * pair : 2 * pair + 1, rows] = lg[0:1]
            total[2 * pair + 1: 2 * pair + 2, rows] = lg[HEAD_DIM:HEAD_DIM+1]
            out[rows, pair * PAIR : (pair + 1) * PAIR] = jnp.where(
                lane < HEAD_DIM, blended[2 * i], blended[2 * i + 1]
            ).astype(BF16)


def attend_back(packed, rows, width, grad_out, total, bias, out, batch):
    masks = half_masks()
    pairs = width // PAIR
    for first in range(0, pairs, batch):
        group = range(first, min(first + batch, pairs))
        loaded = [pair_slices(packed, rows, width, pair) for pair in group]
        upstream = [grad_out[rows, pair * PAIR : (pair + 1) * PAIR] for pair in group]
        heads = [(i, side) for i in range(len(group)) for side in range(2)]
        own_q = [loaded[i][0] * masks[side] for i, side in heads]
        own_k = [loaded[i][1] * masks[side] for i, side in heads]
        own_up = [upstream[i] * masks[side] for i, side in heads]
        scores = [dot(loaded[i][1], own, NT) * (SCALE * LOG2E) for (i, _), own in zip(heads, own_q)]
        grad_shares = [dot(loaded[i][2], own, NT) for (i, _), own in zip(heads, own_up)]
        if bias is not None:
            scores = [value + bias for value in scores]
        sums = total[2 * first : 2 * group.stop, rows]
        shares = [jnp.exp2(value - sums[i : i + 1]) for i, value in enumerate(scores)]
        weighted = [value * grad for value, grad in zip(shares, grad_shares)]
        inner = [jnp.sum(value, 0, keepdims=True) for value in weighted]
        grad_scores = [
            (value - share * total_inner).astype(BF16)
            for value, share, total_inner in zip(weighted, shares, inner)
        ]
        grad_q = [dot(value, own, TN) for value, own in zip(grad_scores, own_k)]
        grad_k = [dot(value, own) for value, own in zip(grad_scores, own_q)]
        grad_v = [dot(value.astype(BF16), own) for value, own in zip(shares, own_up)]
        for i, pair in enumerate(group):
            at = pair * PAIR
            for part, (grad, scale) in enumerate(((grad_q, SCALE), (grad_k, SCALE), (grad_v, 1.0))):
                out[rows, part * width + at : part * width + at + PAIR] = (
                    (grad[2 * i] + grad[2 * i + 1]) * scale
                ).astype(BF16)


def embed(raw, vectors, actions):
    raw = raw.astype(F32)
    masked = raw > SEEN
    return jnp.where(masked, vectors[7:8, :], raw) + actions, masked


def space_forward_kernel(group, pieces, *refs):
    xs, (act, vectors, w_qkv, packed, out, total, *parts) = refs[:pieces], refs[pieces:]
    raw = jnp.concatenate([x[0] for x in xs], 0) if pieces > 1 else xs[0][0]
    count, width = raw.shape
    embedded, _ = embed(raw, vectors, act[0])
    unit, _ = normalise(embedded)
    normed = (unit * vectors[0:1, :] + vectors[1:2, :]).astype(BF16)
    packed[0] = dot(normed, w_qkv[...]).astype(BF16)
    attend_forward_rows(packed.at[0], slice(0, count), width, out.at[0], total.at[0], 4)
    share = count // group
    for j in range(group):
        parts[j][0, 0] = raw[j * share : (j + 1) * share]
        parts[j][0, 1] = out[0, j * share : (j + 1) * share]


def time_forward_kernel(sub, pieces, *refs):
    xs, o1s, refs = refs[:pieces], refs[pieces : 2 * pieces], refs[2 * pieces :]
    (act, perm, bias, vectors, w_space_out, w_qkv, w_out, h1, h2, a2, packed, o2, total) = refs
    x = jnp.concatenate([value[...] for value in xs], 0)
    o1 = jnp.concatenate([value[...] for value in o1s], 0)
    frames, places, width = x.shape
    count = frames * places
    raw = dot(perm[...], x.reshape(count, width))
    blended = dot(perm[...], o1.reshape(count, width)).astype(BF16)
    actions = jnp.broadcast_to(act[...][None], (places, frames, width)).reshape(count, width)
    embedded, _ = embed(raw, vectors, actions)
    after_space = embedded + dot(blended, w_space_out[...])
    h1[...] = after_space
    unit, _ = normalise(after_space)
    normed = (unit * vectors[2:3, :] + vectors[3:4, :]).astype(BF16)
    a2[...] = normed
    packed[...] = dot(normed, w_qkv[...]).astype(BF16)
    for start in range(0, count, sub):
        attend_forward(packed, slice(start, start + sub), width, o2, total, bias[...], 8)
    h2[...] = after_space + dot(o2[...], w_out[...])


def feed_kernel(tile, pieces, per, h2, *refs):
    cots, (vectors, b_up, w_up, w_down), refs = refs[:pieces], refs[pieces : pieces + 4], refs[pieces + 4 :]
    results, (cot, z, dur, a3, r2, sums, bias_grad) = refs[:pieces], refs[pieces:]
    piece = pl.program_id(0) // per
    for j in range(pieces):

        @pl.when(piece == j)
        def _(j=j):
            cot[...] = cots[j][...]

    @pl.when(pl.program_id(0) == 0)
    def _():
        sums[...] = jnp.zeros_like(sums)
        bias_grad[...] = jnp.zeros_like(bias_grad)

    after = h2[...]
    unit, spread = normalise(after)
    gain = vectors[4:5, :]
    normed = (unit * gain + vectors[5:6, :]).astype(BF16)
    a3[...] = normed
    upstream_low = cot[...]
    c = 0.7978845608028654
    total = after + vectors[6:7, :]
    grad_normed = jnp.zeros_like(after)
    for at in range(0, w_up.shape[1], tile):
        cols = slice(at, at + tile)
        hidden = dot(normed, w_up[:, cols]) + b_up[:, cols]
        grad_active = dot(upstream_low, w_down[cols, :], NT)
        square = hidden * hidden
        gate = 0.5 * jnp.tanh(hidden * (c + (c * 0.044715) * square)) + 0.5
        active = hidden * gate
        slope = gate + active * (1.0 - gate) * (2.0 * c + (6.0 * c * 0.044715) * square)
        grad_hidden = grad_active * slope
        bias_grad[:, cols] += jnp.sum(grad_hidden, 0, keepdims=True)
        active = active.astype(BF16)
        grad_hidden = grad_hidden.astype(BF16)
        z[:, cols] = active
        dur[:, cols] = grad_hidden
        total = total + dot(active, w_down[cols, :])
        grad_normed = grad_normed + dot(grad_hidden, w_up[:, cols], NT)
    for j in range(pieces):

        @pl.when(piece == j)
        def _(j=j):
            results[j][...] = total.astype(BF16)

    upstream = upstream_low.astype(F32)
    r2[...] = upstream + norm_back(unit, spread, gain, grad_normed)
    sums[0:1, :] += jnp.sum(grad_normed * unit, 0, keepdims=True)
    sums[1:2, :] += jnp.sum(grad_normed, 0, keepdims=True)
    sums[2:3, :] += jnp.sum(upstream, 0, keepdims=True)


def time_back_kernel(
    sub, r2, h1, packed, total, perm, bias, vectors, w_out, w_qkv, grad_packed, r2_low, sums, *rest
):
    *r1s, grad_out = rest

    @pl.when(pl.program_id(0) == 0)
    def _():
        sums[...] = jnp.zeros_like(sums)

    count, width = r2.shape
    stream = r2[...]
    low = stream.astype(BF16)
    r2_low[...] = low
    grad_out[...] = dot(low, w_out[...], NT).astype(BF16)
    for start in range(0, count, sub):
        attend_back(
            packed, slice(start, start + sub), width, grad_out, total, bias[...], grad_packed, 8
        )
    grad_normed = dot(grad_packed[...], w_qkv[...], NT)
    unit, spread = normalise(h1[...])
    stream = stream + norm_back(unit, spread, vectors[2:3, :], grad_normed)
    sums[0:1, :] += jnp.sum(grad_normed * unit, 0, keepdims=True)
    sums[1:2, :] += jnp.sum(grad_normed, 0, keepdims=True)
    r1 = dot(perm[...], stream.astype(BF16)).astype(BF16).reshape(-1, r1s[0].shape[1], width)
    share = r1s[0].shape[0]
    for j, piece in enumerate(r1s):
        piece[...] = r1[j * share : (j + 1) * share]


def space_back_kernel(pieces, group, order, *refs):
    xs, r1s, refs = refs[:pieces], refs[pieces : pieces + group], refs[pieces + group :]
    (act, hot, earlier, packed, total, vectors, w_out, w_qkv) = refs[:8]
    (grad_packed, a1, r1_all, sums), refs = refs[8:12], refs[12:]
    input_grads, (grad_out,) = refs[:-1], refs[-1:]

    @pl.when(pl.program_id(0) == 0)
    def _():
        sums[...] = earlier[...]

    raw = jnp.concatenate([x[0] for x in xs], 0) if pieces > 1 else xs[0][0]
    r1 = jnp.concatenate([value[0] for value in r1s], 0)
    r1_all[0] = r1
    count, width = raw.shape
    grad_out[...] = dot(r1, w_out[...], NT).astype(BF16)
    attend_back(
        packed.at[0], slice(0, count), width, grad_out, total.at[0], None, grad_packed.at[0], 4
    )
    grad_normed = dot(grad_packed[0], w_qkv[...], NT)
    embedded, masked = embed(raw, vectors, act[0])
    unit, spread = normalise(embedded)
    gain = vectors[0:1, :]
    a1[0] = (unit * gain + vectors[1:2, :]).astype(BF16)
    stream = r1.astype(F32) + norm_back(unit, spread, gain, grad_normed)
    kept = jnp.where(masked, 0.0, stream)
    if len(input_grads) == 1:
        input_grads[0][0] = kept.astype(BF16)
    else:
        share = count // len(order)
        for at, k in enumerate(order):
            input_grads[k // 2][k % 2, 0] = kept[at * share : (at + 1) * share].astype(BF16)
    whole_sum = jnp.sum(stream, 0, keepdims=True)
    sums[0:1, :] += jnp.sum(grad_normed * unit, 0, keepdims=True)
    sums[1:2, :] += jnp.sum(grad_normed, 0, keepdims=True)
    sums[2:3, :] += whole_sum - jnp.sum(kept, 0, keepdims=True)
    sums[8:, :] += hot[0] * whole_sum


def whole(array):
    rank = len(array.shape)
    return pl.BlockSpec(array.shape, lambda *_: (0,) * rank, pipeline_mode=pl.Buffered(1))


def struct(shape, kind):
    return jax.ShapeDtypeStruct(shape, kind)


def call(kernel, grid, operands, outs, scratch=(), flops=0, meta=None, sums=()):
    if sums:
        own, reads, makes, lead = kernel, len(operands), len(outs), meta is not None
        operands, outs = list(operands), list(outs)
        for arrays in sums:
            length = min(array.shape[0] for array in arrays)
            block = (length // grid[0],) + arrays[0].shape[1:]
            index = lambda i, *_, rank=arrays[0].ndim: (i,) + (0,) * (rank - 1)
            operands += [(array, block, index) for array in arrays]
            outs.append(((length,) + arrays[0].shape[1:], BF16, block, index))
        ends = lead + len(operands), lead + len(operands) + len(outs)

        def kernel(*refs):
            made = refs[ends[0] : ends[1]]
            own(*refs[: lead + reads], *made[:makes], *refs[ends[1] :])
            terms = refs[lead + reads : ends[0]]
            for arrays, out in zip(sums, made[makes:]):
                out[...] = sum(term[...].astype(F32) for term in terms[: len(arrays)]).astype(BF16)
                terms = terms[len(arrays) :]

    in_specs = [
        whole(array) if block is None else pl.BlockSpec(block, index)
        for array, block, index in operands
    ]
    out_specs = [
        pl.BlockSpec(shape, lambda *_, rank=len(shape): (0,) * rank)
        if block is None
        else pl.BlockSpec(block, index)
        for shape, _, block, index in outs
    ]
    moved = sum(a.size * a.dtype.itemsize for a, _, _ in operands)
    return pl.pallas_call(
        kernel,
        grid_spec=pltpu.PrefetchScalarGridSpec(
            num_scalar_prefetch=0 if meta is None else 1,
            grid=grid,
            in_specs=in_specs,
            out_specs=out_specs,
            scratch_shapes=scratch,
        ),
        out_shape=[struct(shape, kind) for shape, kind, _, _ in outs],
        cost_estimate=pl.CostEstimate(flops=flops, bytes_accessed=2 * moved, transcendentals=0),
        compiler_params=pltpu.CompilerParams(vmem_limit_bytes=VMEM_LIMIT),
    )(*(() if meta is None else (meta,)), *[a for a, _, _ in operands])


def collect_kernel(parts, meta, *refs):
    *refs, perm, out, held = refs
    chip = pl.program_id(0)
    for i in range(len(refs) // (2 * parts)):

        @pl.when(chip == i)
        def _(i=i):
            found = [ref[...] for ref in refs[2 * parts * i : 2 * parts * (i + 1)]]
            held[...] = jnp.concatenate(found, 0).reshape(held.shape)

    out[...] = dot(perm[...], held[...]).astype(BF16).reshape(out.shape)


def collect(by_slot, chips, perm, shape, operand):
    p, width = shape[0], shape[-1]
    block = 16
    steps = p // block
    parts = len(by_slot[0])
    span = sum(part.shape[-3] for part, _ in by_slot[0])
    count = len(by_slot)
    operands = []
    for k, pieces in enumerate(by_slot):

        def slot_index(i, h, meta, k=k):
            return 0, jnp.where(i == k // 2, h, jnp.where(i < k // 2, 0, steps - 1)), 0

        operands += [
            operand(piece, (piece[0].shape[-3], block, width), slot_index) for piece in pieces
        ]
    operands.append((perm, None, None))
    outs = [
        (
            (p, count * span, width),
            BF16,
            (block, 2 * span, width),
            lambda i, h, meta: (h, meta[i], 0),
        )
    ]
    return call(
        lambda *refs: collect_kernel(parts, *refs),
        (count // 2, steps),
        operands,
        outs,
        [pltpu.VMEM((block * 2 * span, width), BF16)],
        meta=chips,
    )[0].reshape(shape)


def collect_result_kernel(meta, *refs):
    *pieces, out = refs
    for j, piece in enumerate(pieces):

        @pl.when(pl.program_id(0) == j)
        def _(piece=piece):
            out[...] = piece[...]


def collect_result(pieces, where):
    p, _, frames, width = pieces[0].shape
    return call(
        collect_result_kernel,
        (len(pieces),),
        [(piece, None, None) for piece in pieces],
        [
            (
                (p, len(pieces), frames, width),
                BF16,
                (p, 1, frames, width),
                lambda j, meta: (0, meta[j], 0, 0),
            )
        ],
        meta=where,
    )[0]


def put(outs, slot, value):
    share = outs[0].shape[0]
    outs[slot // share][slot % share] = value


def columns_kernel(meta, *refs, counts, firsts, blocks, split):
    step = pl.program_id(0)
    *refs, held = refs
    local = step % firsts[-1]
    for i, count in enumerate(counts):
        lefts, rights, refs = refs[:count], refs[count : 2 * count], refs[2 * count :]

        @pl.when((local >= firsts[i]) & (local < firsts[i + 1]))
        def _(lefts=lefts, rights=rights):
            total = sum(dot(l[...], r[...], TN) for l, r in zip(lefts, rights))
            held[...] = total.astype(BF16)

    shares = len(split)
    size = held.shape[0] // blocks
    per = firsts[-1] // shares
    for part in range(2 * shares):
        two = part >= shares and split[part - shares]
        own, refs = refs[: 1 + two], refs[1 + two :]

        @pl.when(step // per == part)
        def _(first=(part % shares) * blocks, own=own):
            for slot in range(blocks):
                source = pl.multiple_of(meta[first + slot] * size, size)
                put(own, slot, held[pl.ds(source, size), :])


def columns_grad(pairs, meta, split, tile=512, sums=()):
    shares = len(split)
    blocks = (meta.shape[0] - 1) // shares
    height = pairs[0][0][0].shape[1]
    size = height // blocks
    tile = min([tile] + [rights[0].shape[1] // 2 for _, rights in pairs])
    steps = [rights[0].shape[1] // 2 // tile for _, rights in pairs]
    firsts = [sum(steps[:i]) for i in range(len(steps) + 1)]
    per = firsts[-1] // shares
    operands, flops = [], 0
    for (lefts, rights), first, count in zip(pairs, firsts, steps):
        operands += [(left, None, None) for left in lefts]
        for right in rights:

            def index(i, meta, first=first, count=count):
                core = meta[shares * blocks]
                half = jnp.where(i < firsts[-1], 1 - core, core)
                return 0, half * count + jnp.clip(i % firsts[-1] - first, 0, count - 1)

            operands.append((right, (right.shape[0], tile), index))
            flops += 2 * right.size * height

    def part_out(part, rows):
        block = (rows, size, tile), lambda i, meta: (0, 0, jnp.clip(i - part * per, 0, per - 1))
        return (rows, size, per * tile), BF16, *block

    outs = [part_out(share, blocks) for share in range(shares)]
    for share, two in enumerate(split):
        outs += [part_out(shares + share, blocks // (1 + two))] * (1 + two)
    kernel = lambda *refs: columns_kernel(
        *refs, counts=[len(lefts) for lefts, _ in pairs], firsts=firsts, blocks=blocks, split=split
    )
    scratch = [pltpu.VMEM((height, tile), BF16)]
    return call(kernel, (2 * firsts[-1],), operands, outs, scratch, flops, meta, sums)


def rows_kernel(meta, *refs, step_blocks, steps, blocks):
    step = pl.program_id(0)
    lefts, right, (sent, *outs) = refs[:step_blocks], refs[step_blocks], refs[step_blocks + 1 :]
    value = dot(jnp.concatenate([left[...] for left in lefts], 1), right[...], TN).astype(BF16)
    value = value.reshape(step_blocks, -1, value.shape[-1])
    middle = value.shape[-1] // 2
    halves = value[:, :, :middle], value[:, :, middle:]
    share = steps // len(outs)
    for core in range(2):

        @pl.when(meta[blocks] == core)
        def _(core=core):
            sent[...] = halves[1 - core]

        for i, out in enumerate(outs):

            @pl.when((meta[blocks] == core) & (step >= i * share) & (step < (i + 1) * share))
            def _(core=core, out=out):
                out[...] = halves[core]


def rows_grad(left, right, meta, split, step_blocks=2):
    blocks = meta.shape[0] - 1
    depth, height = left.shape
    size, columns = height // blocks, right.shape[1] // 2
    steps = blocks // step_blocks
    operands = [
        (left, (depth, size), lambda i, meta, j=j: (0, meta[i * step_blocks + j]))
        for j in range(step_blocks)
    ]
    operands.append((right, None, None))
    parts = 1 + split[0]
    share = steps // parts
    block = (step_blocks, size, columns)
    outs = [((blocks, size, columns), BF16, block, lambda i, meta: (i, 0, 0))]
    outs += [
        (
            (blocks // parts, size, columns),
            BF16,
            block,
            lambda i, meta, first=j * share: (jnp.clip(i - first, 0, share - 1), 0, 0),
        )
        for j in range(parts)
    ]
    kernel = lambda *refs: rows_kernel(
        *refs, step_blocks=step_blocks, steps=steps, blocks=blocks
    )
    return call(kernel, (steps,), operands, outs, flops=4 * depth * height * columns, meta=meta)


def body(
    tokens,
    mask_bits,
    action_ids,
    vectors,
    action_table,
    w_space_qkv,
    w_space_out,
    w_time_qkv,
    w_time_out,
    w_up,
    b_up,
    w_down,
    cotangent,
):
    p, clips, frames, width = tokens.shape
    n, layers = lax.axis_size("tile"), lax.axis_size("clip")
    me, layer = lax.axis_index("tile"), lax.axis_index("clip")
    core = me % 2
    group = n // clips
    own_frames = frames // group
    grid_all = n * p
    places = grid_all // group
    clip, part = me // group, me % group
    hidden = w_up.shape[1]
    rows = places * frames

    def swap(value, k, axis="tile"):
        size = lax.axis_size(axis)
        return lax.ppermute(value, axis, [(i, i ^ k) for i in range(size)])

    def row_block(*shape):
        return shape, lambda i: (i,) + (0,) * (len(shape) - 1)

    blocks = n * layers // 2
    tile_bits = [1 << b for b in range(1, n.bit_length() - 1)]

    def orders(hops):
        slots = [(0, None, 0, None)]
        for hop in hops:
            if hop == "scatter":
                choices = [(0, None, 0, c) for c in range(layers)]
            elif hop == "tiles":
                choices = [(0, t, 0, None) for t in range(n // 2)]
            elif hop == "spread":
                choices = [(0, None, c, None) for c in range(layers)]
            else:
                bit = (hop[1], None, 0, None) if hop[0] == "tile" else (0, None, hop[1], None)
                choices = [(0, None, 0, None), bit]
            slots = [
                (a ^ x, t if u is None else u, b ^ y, c if d is None else d)
                for a, t, b, c in slots
                for x, u, y, d in choices
            ]
        where = [
            (layer ^ b if c is None else c) * (n // 2) + ((me ^ a) // 2 if t is None else t)
            for a, t, b, c in slots
        ]
        return jnp.stack([jnp.asarray(w, jnp.int32) for w in where])

    def halves(value, hop):
        if hop is None or isinstance(hop, str):
            return [value]
        middle = value.shape[0] // 2
        return [value[:middle], value[middle:]]

    def meta_of(chains):
        return jnp.concatenate([orders(hops) for hops in chains] + [core.astype(jnp.int32)[None]])

    def begin(make, chains, meta):
        split = [not isinstance(hops[0], str) for hops in chains]
        made = make(meta, split)
        sent, made, parts = list(made[: len(split)]), made[len(split) :], []
        for two in split:
            parts.append(list(made[: 1 + two]))
            made = made[1 + two :]
        return chains, parts, sent

    def cross(begun):
        chains, parts, sent = begun
        return chains, parts, [swap(value, 1) for value in sent]

    def add(values, kind):
        if len(values) == 2 and all(value.dtype == kind for value in values):
            return values[0] + values[1]
        return sum(value.astype(F32) for value in values).astype(kind)

    def land(crossed):
        chains, all_parts, received = crossed
        landed = []
        for hops, parts, came in zip(chains, all_parts, received):
            if isinstance(hops[0], str):
                landed.append([[(add([parts[0], came], BF16), False)]])
            else:
                _, sent = halves(came, hops[0])
                landed.append([[(parts[0], False), (came, True)], add([parts[1], sent], BF16)])
        return chains, landed, 0

    def addends(departed):
        (chains, parts, at), coming = departed
        return [value for value, _ in parts[0][0]] + coming

    def arrived(departed, total):
        chains, parts, at = departed[0]
        hops = chains[0]
        pieces = halves(total, hops[at + 1] if at + 1 < len(hops) else None)
        return chains, [[[(total, len(pieces) == 2)]] + pieces[1:]], at + 1

    def merge(state):
        chains, parts, at = state
        kept = jnp.concatenate([own[0][0][0] for own in parts], -1)
        return chains[:1], [[[(kept, False)]]], at

    def depart(state):
        chains, parts, at = state
        coming = []
        for hops, own in zip(chains, parts):
            hop, value = hops[at], own[0][0][0]
            if hop == "scatter":
                coming.append(lax.psum_scatter(value, "clip", scatter_dimension=0, tiled=True))
            elif hop == "tiles":
                same_core = [list(range(c, n, 2)) for c in range(2)]
                coming.append(
                    lax.psum_scatter(
                        value, "tile", scatter_dimension=0, tiled=True, axis_index_groups=same_core
                    )
                )
            elif hop == "spread":
                share = value.shape[0] // layers
                coming.append(
                    [swap(value[j * share : (j + 1) * share], j, "clip") for j in range(1, layers)]
                )
            else:
                coming.append(swap(own[1], hop[1], hop[0]))
        return state, coming

    def arrive(departed):
        (chains, parts, at), coming = departed
        new_parts = []
        for hops, own, came in zip(chains, parts, coming):
            following = hops[at + 1] if at + 1 < len(hops) else None
            kind = F32 if following is None else BF16
            kept = [v[: v.shape[0] // 2] if first else v for v, first in own[0]]
            if hops[at] == "spread":
                values = [kept[0][: kept[0].shape[0] // layers]] + came
            else:
                values = [came] if isinstance(hops[at], str) else kept + [came]
            summed = [add(piece, kind) for piece in zip(*[halves(v, following) for v in values])]
            new_parts.append([[(summed[0], False)]] + summed[1:])
        return chains, new_parts, at + 1

    def last_swap(state):
        own = jnp.concatenate([own[0][0][0][0].astype(F32) for own in state[1]], 1)
        size = own.shape[0] // 2
        mine = lax.dynamic_slice_in_dim(own, core * size, size, 0)
        other = lax.dynamic_slice_in_dim(own, (1 - core) * size, size, 0)
        return mine, swap(other.astype(BF16), 1)

    def join(mine, other, widths):
        whole_parts, at = [], 0
        for w in widths:
            a, b = mine[:, at : at + w // 2], other[:, at : at + w // 2].astype(F32)
            whole_parts.append(
                jnp.where(core == 0, jnp.concatenate([a, b], 1), jnp.concatenate([b, a], 1))
            )
            at += w // 2
        return whole_parts

    one_way = [("tile", bit) for bit in tile_bits]
    other_way = one_way[::-1]
    clip_bits = [("clip", 1 << b) for b in range(layers.bit_length() - 1)]
    up_chains, down_chains = [one_way + clip_bits], [["scatter"] + one_way]
    time_chains = [["scatter"] + other_way]
    space_chains = [one_way + ["spread"], other_way + ["spread"]]

    order = [k for j in range(group) for k in range(j, n, group)]
    onehot = (action_ids[..., None] == lax.iota(jnp.int32, action_table.shape[0])).astype(F32)
    action_rows = jnp.einsum("cfa,ad->cfd", onehot, action_table, precision=lax.Precision.HIGHEST)
    act_time = lax.dynamic_index_in_dim(action_rows, clip, 0, keepdims=False)
    act_space = lax.dynamic_slice_in_dim(act_time, part * own_frames, own_frames, 0)[:, None, :]

    regular = p % 16 == 0 and 2 * own_frames == 16
    deal_back = None
    if regular:
        at = lax.iota(jnp.int32, 16 * 2 * own_frames)
        place, frame = at % 16, at // 16
        source = place * 2 * own_frames + (frame + core * own_frames) % (2 * own_frames)
        deal_back = (at[:, None] == source[None, :]).astype(BF16)
    marked = jnp.where((mask_bits > 0)[..., None], jnp.asarray(MASKED, BF16), tokens)
    marked = marked.reshape(p, n, own_frames, width)
    chunks = 2
    span = own_frames // chunks
    blocks_of = [lax.dynamic_index_in_dim(marked, me ^ k, 1, keepdims=False) for k in order]
    sources = [
        [value[:, c * span : (c + 1) * span].transpose(1, 0, 2) for value in blocks_of]
        for c in range(chunks)
    ]

    def send_out(parts):
        return [part if k == 0 else swap(part, k) for k, part in zip(order, parts)]

    cot_pieces = [
        lax.dynamic_index_in_dim(cotangent, clip ^ j, 1, keepdims=False).reshape(p * frames, width)
        for j in range(n // group)
    ]
    block = 16
    count = block * frames
    sub = min(count, 128)
    index = lax.iota(jnp.int32, count)
    slot, place = index // block, index % block
    frame_of_slot = ((part ^ (slot // own_frames)) * own_frames) + slot % own_frames
    target = place * frames + frame_of_slot
    perm_back = (target[:, None] == index[None, :]).astype(BF16)
    perm = (index[:, None] == target[None, :]).astype(BF16)
    seq = lax.iota(jnp.int32, sub)
    same = (seq[:, None] // frames) == (seq[None, :] // frames)
    bias = jnp.where(same & (seq[:, None] <= seq[None, :]), 0.0, NEGATIVE).astype(F32)
    own_hot = lax.dynamic_slice_in_dim(
        lax.dynamic_index_in_dim(onehot, clip, 0, keepdims=False), part * own_frames, own_frames, 0
    )[..., None]
    where_clip = clip ^ lax.iota(jnp.int32, clips)
    where_chip = (me // 2) ^ lax.iota(jnp.int32, n // 2)
    tables = dict(
        act_time=act_time,
        act_space=act_space,
        perm=perm,
        perm_back=perm_back,
        bias=bias,
        own_hot=own_hot,
        where_clip=where_clip,
        where_chip=where_chip,
        deal_back=deal_back,
        **{
            name: meta_of(chains)
            for name, chains in (
                ("up", up_chains),
                ("down", down_chains),
                ("time", time_chains),
                ("space", space_chains),
            )
        },
    )
    ahead = [at for at, k in enumerate(order) if k in (1, n - 1)]
    started = [swap(sources[1][at], order[at]) for at in ahead]
    pieces = [send_out(sources[0])]
    pieces[0], sources, cot_pieces, tables, started = hold_parts(
        pieces[0], sources, cot_pieces, tables, started
    )
    for c in range(1, chunks):
        came = dict(zip(ahead, started)) if c == 1 else {}
        pieces.append(
            [
                came[at] if at in came else part if k == 0 else swap(part, k)
                for at, (k, part) in enumerate(zip(order, sources[c]))
            ]
        )
    cot_pieces = [
        piece if j == 0 else swap(piece, j * group) for j, piece in enumerate(cot_pieces)
    ]
    if p % 16:
        pieces = [[jnp.concatenate(parts, 1)] for parts in pieces]
    kinds = len(pieces[0])
    act_time, act_space, own_hot = (tables[name] for name in ("act_time", "act_space", "own_hot"))
    perm, perm_back, bias = (tables[name] for name in ("perm", "perm_back", "bias"))
    where_clip, where_chip, deal_back = (
        tables[name] for name in ("where_clip", "where_chip", "deal_back")
    )

    head_flops = 2 * HEADS * HEAD_DIM

    def frame_block(*shape):
        return (1,) + shape, lambda i: (i, 0, 0)

    def chunk_block(first, *shape):
        return (1,) + shape, lambda i: (first + i, 0, 0)

    space, both = [], []
    for c in range(chunks):
        packed, o1, total, *parts = call(
            lambda *refs: space_forward_kernel(group, kinds, *refs),
            (span,),
            [(x, *frame_block(*x.shape[1:])) for x in pieces[c]]
            + [
                (act_space, *chunk_block(c * span, 1, width)),
                (vectors, None, None),
                (w_space_qkv, None, None),
            ],
            [
                ((span, grid_all, 3 * width), BF16, *frame_block(grid_all, 3 * width)),
                ((span, grid_all, width), BF16, *frame_block(grid_all, width)),
                ((span, HEADS, grid_all), F32, *frame_block(HEADS, grid_all)),
            ]
            + [
                (
                    (span, 2, places, width),
                    BF16,
                    (1, 2, places, width),
                    lambda i: (i, 0, 0, 0),
                )
            ]
            * group,
            flops=2 * span * grid_all * width * 3 * width
            + 16 * span * grid_all * grid_all * head_flops,
        )
        space.append((packed, o1, total))
        both.append([part if j == 0 else swap(part, j) for j, part in enumerate(parts)])
    both = [both[c][j] for j in range(group) for c in range(chunks)]

    def slot_block(size):
        return (size, block, width), lambda i: (0, i, 0)

    total_block = ((HEADS, count), lambda i: (0, i))
    h1, h2, a2, packed_two, o2, total_two = call(
        lambda *refs: time_forward_kernel(sub, len(both), *refs),
        (places // block,),
        [
            (value, (span, None, block, width), lambda i, which=which: (0, which, i, 0))
            for which in range(2)
            for value in both
        ]
        + [
            (act_time, None, None),
            (perm, None, None),
            (bias, None, None),
            (vectors, None, None),
            (w_space_out, None, None),
            (w_time_qkv, None, None),
            (w_time_out, None, None),
        ],
        [
            ((rows, width), F32, *row_block(count, width)),
            ((rows, width), F32, *row_block(count, width)),
            ((rows, width), BF16, *row_block(count, width)),
            ((rows, 3 * width), BF16, *row_block(count, 3 * width)),
            ((rows, width), BF16, *row_block(count, width)),
            ((HEADS, rows), F32, *total_block),
        ],
        flops=2 * rows * width * 5 * width + 16 * rows * sub * head_flops,
    )

    step = min(p * frames, 256)
    per = p * frames // step

    def piece_block(j):
        return (step, width), lambda i, j=j: (jnp.clip(i - j * per, 0, per - 1), 0)

    *result_pieces, cot, z, dur, a3, r2, sums_three, bias_up = call(
        lambda *refs: feed_kernel(1024, len(cot_pieces), per, *refs),
        (rows // step,),
        [(h2, *row_block(step, width))]
        + [(piece, *piece_block(j)) for j, piece in enumerate(cot_pieces)]
        + [
            (vectors, None, None),
            (b_up[None, :], None, None),
            (w_up, None, None),
            (w_down, None, None),
        ],
        [((p * frames, width), BF16, *piece_block(j)) for j in range(len(cot_pieces))]
        + [
            ((rows, width), BF16, *row_block(step, width)),
            ((rows, hidden), BF16, *row_block(step, hidden)),
            ((rows, hidden), BF16, *row_block(step, hidden)),
            ((rows, width), BF16, *row_block(step, width)),
            ((rows, width), F32, *row_block(step, width)),
            ((8, width), F32, None, None),
            ((1, hidden), F32, None, None),
        ],
        flops=8 * rows * width * hidden,
    )

    result_pieces = [
        (piece if j == 0 else swap(piece, j * group)).reshape(p, 1, frames, width)
        for j, piece in enumerate(result_pieces)
    ]

    def make_down(meta, split):
        if hidden // blocks % 128:
            return columns_grad([([z], [cot])], meta, split, 256)
        return rows_grad(z, cot, meta, split)

    def make_up(meta, split):
        return columns_grad([([a3], [dur])], meta, split)

    up = begin(make_up, up_chains, tables["up"])
    cot, up, result_pieces[:-1] = hold_parts(cot, up, result_pieces[:-1])
    up = cross(up)
    down = begin(make_down, down_chains, tables["down"])
    r2, down, up, result_pieces = hold_parts(r2, down, up, result_pieces)
    up, down = depart(land(up)), cross(down)

    grad_packed_two, r2_low, sums_two, *r1_parts = call(
        lambda *refs: time_back_kernel(sub, *refs),
        (places // block,),
        [
            (r2, *row_block(count, width)),
            (h1, *row_block(count, width)),
            (packed_two, *row_block(count, 3 * width)),
            (total_two, *total_block),
            (perm_back, None, None),
            (bias, None, None),
            (vectors, None, None),
            (w_time_out, None, None),
            (w_time_qkv, None, None),
        ],
        [
            ((rows, 3 * width), BF16, *row_block(count, 3 * width)),
            ((rows, width), BF16, *row_block(count, width)),
            ((8, width), F32, None, None),
        ]
        + [((own_frames, places, width), BF16, *slot_block(own_frames))] * group,
        [pltpu.VMEM((count, width), BF16)],
        flops=2 * rows * width * 4 * width + 40 * rows * sub * head_flops,
    )
    grad_packed_two, up, down = hold_parts(grad_packed_two, up, down)
    r1_parts = [r1 if j == 0 else swap(r1, j) for j, r1 in enumerate(r1_parts)]
    extra = []

    def make_time(meta, split):
        pairs = [([a2], [grad_packed_two]), ([o2], [r2_low])]
        beside = [[down[1][0][0], down[2][0]], addends(up)]
        *made, down_total, up_total = columns_grad(pairs, meta, split, sums=beside)
        extra.extend((down_total, up_total))
        return made

    time = begin(make_time, time_chains, tables["time"])
    down = down[0], [[[(extra[0], False)]]], 0
    up = arrived(up, extra[1])

    dealt = 1 if p % 16 else n

    def send_back(parts):
        if dealt == 1:
            parts = [parts[0][:, at * p : (at + 1) * p] for at in range(n)]
            parts = [parts[order.index(k)] for k in range(n)]
            parts = [jnp.stack(parts[2 * j : 2 * j + 2]) for j in range(n // 2)]
        return [part if j == 0 else swap(part, 2 * j) for j, part in enumerate(parts)]

    def pass_on(came):
        crossed = swap(jnp.stack([value[1] for value in came]), 1)
        return [found for j, value in enumerate(came) for found in ((value, 0), (crossed, j))]

    def operand(found, block, index):
        return found[0], (None,) + block, lambda *i: (found[1],) + index(*i)

    def space_back(c, earlier, sums=()):
        packed, _, total = space[c]
        return call(
            lambda *refs: space_back_kernel(kinds, group, order, *refs),
            (span,),
            [(x, *frame_block(*x.shape[1:])) for x in pieces[c]]
            + [(r1, *chunk_block(c * span, places, width)) for r1 in r1_parts]
            + [
                (act_space, *chunk_block(c * span, 1, width)),
                (own_hot, *chunk_block(c * span, action_table.shape[0], 1)),
                (earlier, None, None),
                (packed, *frame_block(grid_all, 3 * width)),
                (total, *frame_block(HEADS, grid_all)),
                (vectors, None, None),
                (w_space_out, None, None),
                (w_space_qkv, None, None),
            ],
            [
                ((span, grid_all, 3 * width), BF16, *frame_block(grid_all, 3 * width)),
                ((span, grid_all, width), BF16, *frame_block(grid_all, width)),
                ((span, grid_all, width), BF16, *frame_block(grid_all, width)),
                ((8 + action_table.shape[0], width), F32, None, None),
            ]
            + (
                [((span, grid_all, width), BF16, *frame_block(grid_all, width))]
                if dealt == 1
                else [
                    ((2, span, p, width), BF16, (2, 1, p, width), lambda i: (0, i, 0, 0))
                ]
                * (n // 2)
            ),
            [pltpu.VMEM((grid_all, width), BF16)],
            flops=2 * span * grid_all * width * 4 * width
            + 40 * span * grid_all * grid_all * head_flops,
            sums=sums,
        )

    r1_parts, time, up, down = hold_parts(r1_parts, time, up, down)
    up, down, time = depart(up), depart(down), cross(time)
    early = jnp.concatenate([sums_two, sums_three, bias_up.reshape(-1, width)], 0)
    back = [space_back(0, jnp.zeros((8 + action_table.shape[0], width), F32))]
    back[0], r1_parts, time, up = hold_parts(back[0], r1_parts, time, up)
    input_pieces = [send_back(back[0][4:])]
    up = depart(arrive(up))
    for c in range(1, chunks):
        beside = [[time[1][0][0], time[2][0]]] if c == 1 else []
        back.append(space_back(c, back[-1][3], beside))
        if c == 1:
            *back[c], time_total = back[c]
    time = time[0], [[[(time_total, False)]]], 0
    back, input_pieces, up, time = hold_parts(back, input_pieces, up, time)
    input_pieces[0] = pass_on(input_pieces[0])
    for c in range(1, chunks):
        input_pieces.append(send_back(back[c][4:]))
    up, time = depart(arrive(up)), depart(time)
    grads_one, a1s, r1s = list(zip(*back))[:3]

    def flat(values):
        return [value.reshape(-1, value.shape[-1]) for value in values]

    def make_space(meta, split):
        return columns_grad(
            [
                (flat(a1s), flat(grads_one)),
                (flat([o1 for _, o1, _ in space]), flat(r1s)),
            ],
            meta,
            split,
        )

    small = jnp.concatenate([back[-1][3], early], 0)
    small_hops = [("tile", 1 << b) for b in range(n.bit_length() - 1)] + clip_bits

    space_sum = begin(make_space, space_chains, tables["space"])
    where_clip, space_sum, up, down, input_pieces = hold_parts(
        where_clip, space_sum, up, down, input_pieces
    )
    space_sum = cross(space_sum)
    small_came = swap(small, small_hops[0][1], small_hops[0][0])
    up = arrive(up)
    while up[2] < len(up[0][0]):
        up = arrive(depart(up))
    up, down = last_swap(up), depart(arrive(down))
    result_out = collect_result(result_pieces, where_clip)
    space_sum, result_out, small_came = hold_parts(space_sum, result_out, small_came)
    space_sum, small = land(space_sum), small + small_came
    input_pieces[1:] = [pass_on(came) for came in input_pieces[1:]]
    time = arrive(time)

    def collect_input(input_pieces, where_chip):
        by_slot = [[pieces_of[k] for pieces_of in input_pieces] for k in range(n)]
        if regular:
            input_grad = collect(by_slot, where_chip, deal_back, tokens.shape, operand)
        else:
            input_grad = jnp.zeros((p, n, own_frames, width), BF16)
            for k, parts in enumerate(by_slot):
                piece = jnp.concatenate([value[at] for value, at in parts], 0)
                input_grad = lax.dynamic_update_slice_in_dim(
                    input_grad, piece.transpose(1, 0, 2)[:, None], me ^ k, 1
                )
            input_grad = input_grad.reshape(tokens.shape)
        return input_grad

    rounds = max(len(small_hops) - 1, len(space_sum[0][0]) + 1, 2 * len(one_way) + 1)
    for r in range(rounds):
        departed = small_came = time_moves = down_moves = None
        if r < len(space_sum[0][0]):
            if r == len(one_way):
                space_sum = merge(space_sum)
            departed = depart(space_sum)
        if r + 1 < len(small_hops):
            small_came = swap(small, small_hops[r + 1][1], small_hops[r + 1][0])
        if r >= len(one_way) and time[2] < len(time[0][0]):
            time_moves = depart(time)
        if r > len(one_way) and down[2] < len(down[0][0]):
            down_moves = depart(down)
        others = [down, input_pieces, up] if r == 0 else []
        if r == 1:
            input_grad = collect_input(input_pieces, where_chip)
            others = [input_grad]
        departed, small_came, time_moves, down_moves, *others = hold_parts(
            departed, small_came, time_moves, down_moves, *others
        )
        if r == 0:
            down, input_pieces, up = others
            down = arrive(down)
        if r == 1:
            (input_grad,) = others
        if time_moves is not None:
            time = arrive(time_moves)
            if time[2] == len(time[0][0]):
                time_last = last_swap(time)
        if down_moves is not None:
            down = arrive(down_moves)
            if down[2] == len(down[0][0]):
                down_last = last_swap(down)
        if departed is not None:
            space_sum = arrive(departed)
        if small_came is not None:
            small = small + small_came
        if r + 1 == len(space_sum[0][0]):
            space_last = last_swap(space_sum)
    at = 8 + action_table.shape[0]
    sums = small[at:]
    (down_out,) = join(*down_last, [width])
    (up_out,) = join(*up, [hidden])
    time_qkv, time_out = join(*time_last, [3 * width, width])
    space_qkv, space_out = join(*space_last, [3 * width, width])
    return (
        result_out,
        input_grad,
        jnp.concatenate([small[:2], sums[:2], sums[8:11], small[2:3]], 0),
        small[8:at],
        space_qkv,
        space_out,
        time_qkv,
        time_out,
        up_out,
        sums[16:].reshape(hidden),
        down_out,
    )


def hold_parts(*values):
    leaves, tree = jax.tree.flatten(values)
    arrays = [i for i, leaf in enumerate(leaves) if isinstance(leaf, jax.Array)]
    held = lax.optimization_barrier([leaves[i] for i in arrays])
    for i, leaf in zip(arrays, held):
        leaves[i] = leaf
    return jax.tree.unflatten(tree, leaves)


def solution(mesh):
    spread = P("tile", "clip", None, None)
    rows = P(("clip", "tile"), None)
    return jax.shard_map(
        body,
        mesh=mesh,
        in_specs=(spread, P("tile", "clip", None), P("clip", None)) + (P(),) * 9 + (spread,),
        out_specs=(spread, spread, P(), P(), rows, rows, rows, rows, rows, P(), rows),
        check_vma=False,
    )
```

```python
import jax
import jax.numpy as jnp
from jax import lax
from jax.experimental import pallas as pl
from jax.experimental.pallas import tpu as pltpu
from jax.sharding import PartitionSpec as P

HEADS = 16
HEAD_DIM = 64
PAIR = 2 * HEAD_DIM
EPSILON = 1e-05
NEGATIVE = -1e30
MASKED = 2.0**100
SEEN = 2.0**99
LOG2E = 1.4426950408889634
SCALE = HEAD_DIM**-0.5
F32 = jnp.float32
BF16 = jnp.bfloat16
VMEM_LIMIT = 60 * 1024 * 1024

NN = (((1,), (0,)), ((), ()))
NT = (((1,), (1,)), ((), ()))
TN = (((0,), (0,)), ((), ()))


def dot(left, right, form=NN):
    return lax.dot_general(left, right, form, preferred_element_type=F32)


def normalise(values):
    centred = values - jnp.mean(values, -1, keepdims=True)
    spread = lax.rsqrt(jnp.mean(centred * centred, -1, keepdims=True) + EPSILON)
    return centred * spread, spread


def norm_back(unit, spread, gain, upstream):
    scaled = upstream * gain
    return spread * (
        scaled
        - jnp.mean(scaled, -1, keepdims=True)
        - unit * jnp.mean(scaled * unit, -1, keepdims=True)
    )


def half_masks():
    lane = lax.broadcasted_iota(jnp.int32, (1, PAIR), 1)
    low = (lane < HEAD_DIM).astype(F32).astype(BF16)
    high = (lane >= HEAD_DIM).astype(F32).astype(BF16)
    return low, high


def pair_slices(packed, rows, width, pair):
    at = pair * PAIR
    return [packed[rows, part * width + at : part * width + at + PAIR] for part in range(3)]


def pair_slices(packed, rows, width, pair):
    at = pair * PAIR
    return [packed[rows, part * width + at : part * width + at + PAIR] for part in range(3)]


def attend_forward(packed, rows, width, out, total, bias, batch):
    masks = half_masks()
    lane = lax.broadcasted_iota(jnp.int32, (1, PAIR), 1)
    pairs = width // PAIR
    for first in range(0, pairs, batch):
        group = range(first, min(first + batch, pairs))
        loaded = [pair_slices(packed, rows, width, pair) for pair in group]
        scores = [
            dot(keys, queries * masks[side], NT) * (SCALE * LOG2E)
            for queries, keys, _ in loaded
            for side in range(2)
        ]
        if bias is not None:
            scores = [value + bias for value in scores]
        highest = [jnp.max(value, 0, keepdims=True) for value in scores]
        shares = [jnp.exp2(value - top) for value, top in zip(scores, highest)]
        weights = [jnp.sum(value, 0, keepdims=True) for value in shares]
        shares = [(value * (1.0 / weight)).astype(BF16) for value, weight in zip(shares, weights)]
        blended = [dot(value, loaded[i // 2][2], TN) for i, value in enumerate(shares)]
        total[2 * first : 2 * group.stop, rows] = jnp.concatenate(
            [top + jnp.log2(weight) for top, weight in zip(highest, weights)], 0
        )
        for i, pair in enumerate(group):
            out[rows, pair * PAIR : (pair + 1) * PAIR] = jnp.where(
                lane < HEAD_DIM, blended[2 * i], blended[2 * i + 1]
            ).astype(BF16)


def attend_forward_rows(packed, rows, width, out, total, batch):
    masks = half_masks()
    lane = lax.broadcasted_iota(jnp.int32, (1, PAIR), 1)
    pairs = width // PAIR
    for first in range(0, pairs, batch):
        group = range(first, min(first + batch, pairs))
        loaded = [pair_slices(packed, rows, width, pair) for pair in group]
        scores = [
            dot(queries * masks[side], keys, NT) * (SCALE * LOG2E)
            for queries, keys, _ in loaded
            for side in range(2)
        ]
        ones = [jnp.concatenate([v, jnp.ones_like(v)], 1) for _, _, v in loaded]
        highest = [jnp.max(value, 1, keepdims=True) for value in scores]
        shares = [jnp.exp2(value - top).astype(BF16) for value, top in zip(scores, highest)]
        blended = [dot(value, ones[i // 2]) for i, value in enumerate(shares)]
        sums = [b[:, PAIR:] for b in blended]
        blended = [b[:, :PAIR] * (1.0 / w) for b, w in zip(blended, sums)]
        logs = [top + jnp.log2(w) for top, w in zip(highest, sums)]
        for i, pair in enumerate(group):
            lg = jnp.where(lane < HEAD_DIM, logs[2*i], logs[2*i+1]).T
            total[2 * pair : 2 * pair + 1, rows] = lg[0:1]
            total[2 * pair + 1: 2 * pair + 2, rows] = lg[HEAD_DIM:HEAD_DIM+1]
            out[rows, pair * PAIR : (pair + 1) * PAIR] = jnp.where(
                lane < HEAD_DIM, blended[2 * i], blended[2 * i + 1]
            ).astype(BF16)


def attend_back(packed, rows, width, grad_out, total, bias, out, batch):
    masks = half_masks()
    pairs = width // PAIR
    for first in range(0, pairs, batch):
        group = range(first, min(first + batch, pairs))
        loaded = [pair_slices(packed, rows, width, pair) for pair in group]
        upstream = [grad_out[rows, pair * PAIR : (pair + 1) * PAIR] for pair in group]
        heads = [(i, side) for i in range(len(group)) for side in range(2)]
        own_q = [loaded[i][0] * masks[side] for i, side in heads]
        own_k = [loaded[i][1] * masks[side] for i, side in heads]
        own_up = [upstream[i] * masks[side] for i, side in heads]
        scores = [dot(loaded[i][1], own, NT) * (SCALE * LOG2E) for (i, _), own in zip(heads, own_q)]
        grad_shares = [dot(loaded[i][2], own, NT) for (i, _), own in zip(heads, own_up)]
        if bias is not None:
            scores = [value + bias for value in scores]
        sums = total[2 * first : 2 * group.stop, rows]
        shares = [jnp.exp2(value - sums[i : i + 1]) for i, value in enumerate(scores)]
        weighted = [value * grad for value, grad in zip(shares, grad_shares)]
        inner = [jnp.sum(value, 0, keepdims=True) for value in weighted]
        grad_scores = [
            (value - share * total_inner).astype(BF16)
            for value, share, total_inner in zip(weighted, shares, inner)
        ]
        grad_q = [dot(value, own, TN) for value, own in zip(grad_scores, own_k)]
        grad_k = [dot(value, own) for value, own in zip(grad_scores, own_q)]
        grad_v = [dot(value.astype(BF16), own) for value, own in zip(shares, own_up)]
        for i, pair in enumerate(group):
            at = pair * PAIR
            for part, (grad, scale) in enumerate(((grad_q, SCALE), (grad_k, SCALE), (grad_v, 1.0))):
                out[rows, part * width + at : part * width + at + PAIR] = (
                    (grad[2 * i] + grad[2 * i + 1]) * scale
                ).astype(BF16)


def embed(raw, vectors, actions):
    raw = raw.astype(F32)
    masked = raw > SEEN
    return jnp.where(masked, vectors[7:8, :], raw) + actions, masked


def space_forward_kernel(group, pieces, *refs):
    xs, (act, vectors, w_qkv, packed, out, total, *parts) = refs[:pieces], refs[pieces:]
    raw = jnp.concatenate([x[0] for x in xs], 0) if pieces > 1 else xs[0][0]
    count, width = raw.shape
    embedded, _ = embed(raw, vectors, act[0])
    unit, _ = normalise(embedded)
    normed = (unit * vectors[0:1, :] + vectors[1:2, :]).astype(BF16)
    packed[0] = dot(normed, w_qkv[...]).astype(BF16)
    attend_forward_rows(packed.at[0], slice(0, count), width, out.at[0], total.at[0], 4)
    share = count // group
    for j in range(group):
        parts[j][0, 0] = raw[j * share : (j + 1) * share]
        parts[j][0, 1] = out[0, j * share : (j + 1) * share]


def time_forward_kernel(sub, pieces, *refs):
    xs, o1s, refs = refs[:pieces], refs[pieces : 2 * pieces], refs[2 * pieces :]
    (act, perm, bias, vectors, w_space_out, w_qkv, w_out, h1, h2, a2, packed, o2, total) = refs
    x = jnp.concatenate([value[...] for value in xs], 0)
    o1 = jnp.concatenate([value[...] for value in o1s], 0)
    frames, places, width = x.shape
    count = frames * places
    raw = dot(perm[...], x.reshape(count, width))
    blended = dot(perm[...], o1.reshape(count, width)).astype(BF16)
    actions = jnp.broadcast_to(act[...][None], (places, frames, width)).reshape(count, width)
    embedded, _ = embed(raw, vectors, actions)
    after_space = embedded + dot(blended, w_space_out[...])
    h1[...] = after_space
    unit, _ = normalise(after_space)
    normed = (unit * vectors[2:3, :] + vectors[3:4, :]).astype(BF16)
    a2[...] = normed
    packed[...] = dot(normed, w_qkv[...]).astype(BF16)
    for start in range(0, count, sub):
        attend_forward(packed, slice(start, start + sub), width, o2, total, bias[...], 8)
    h2[...] = after_space + dot(o2[...], w_out[...])


def feed_kernel(tile, pieces, per, h2, *refs):
    cots, (vectors, b_up, w_up, w_down), refs = refs[:pieces], refs[pieces : pieces + 4], refs[pieces + 4 :]
    results, (cot, z, dur, a3, r2, sums, bias_grad) = refs[:pieces], refs[pieces:]
    piece = pl.program_id(0) // per
    for j in range(pieces):

        @pl.when(piece == j)
        def _(j=j):
            cot[...] = cots[j][...]

    @pl.when(pl.program_id(0) == 0)
    def _():
        sums[...] = jnp.zeros_like(sums)
        bias_grad[...] = jnp.zeros_like(bias_grad)

    after = h2[...]
    unit, spread = normalise(after)
    gain = vectors[4:5, :]
    normed = (unit * gain + vectors[5:6, :]).astype(BF16)
    a3[...] = normed
    upstream_low = cot[...]
    c = 0.7978845608028654
    total = after + vectors[6:7, :]
    grad_normed = jnp.zeros_like(after)
    for at in range(0, w_up.shape[1], tile):
        cols = slice(at, at + tile)
        hidden = dot(normed, w_up[:, cols]) + b_up[:, cols]
        grad_active = dot(upstream_low, w_down[cols, :], NT)
        square = hidden * hidden
        gate = 0.5 * jnp.tanh(hidden * (c + (c * 0.044715) * square)) + 0.5
        active = hidden * gate
        slope = gate + active * (1.0 - gate) * (2.0 * c + (6.0 * c * 0.044715) * square)
        grad_hidden = grad_active * slope
        bias_grad[:, cols] += jnp.sum(grad_hidden, 0, keepdims=True)
        active = active.astype(BF16)
        grad_hidden = grad_hidden.astype(BF16)
        z[:, cols] = active
        dur[:, cols] = grad_hidden
        total = total + dot(active, w_down[cols, :])
        grad_normed = grad_normed + dot(grad_hidden, w_up[:, cols], NT)
    for j in range(pieces):

        @pl.when(piece == j)
        def _(j=j):
            results[j][...] = total.astype(BF16)

    upstream = upstream_low.astype(F32)
    r2[...] = upstream + norm_back(unit, spread, gain, grad_normed)
    sums[0:1, :] += jnp.sum(grad_normed * unit, 0, keepdims=True)
    sums[1:2, :] += jnp.sum(grad_normed, 0, keepdims=True)
    sums[2:3, :] += jnp.sum(upstream, 0, keepdims=True)


def time_back_kernel(
    sub, r2, h1, packed, total, perm, bias, vectors, w_out, w_qkv, grad_packed, r2_low, sums, *rest
):
    *r1s, grad_out = rest

    @pl.when(pl.program_id(0) == 0)
    def _():
        sums[...] = jnp.zeros_like(sums)

    count, width = r2.shape
    stream = r2[...]
    low = stream.astype(BF16)
    r2_low[...] = low
    grad_out[...] = dot(low, w_out[...], NT).astype(BF16)
    for start in range(0, count, sub):
        attend_back(
            packed, slice(start, start + sub), width, grad_out, total, bias[...], grad_packed, 8
        )
    grad_normed = dot(grad_packed[...], w_qkv[...], NT)
    unit, spread = normalise(h1[...])
    stream = stream + norm_back(unit, spread, vectors[2:3, :], grad_normed)
    sums[0:1, :] += jnp.sum(grad_normed * unit, 0, keepdims=True)
    sums[1:2, :] += jnp.sum(grad_normed, 0, keepdims=True)
    r1 = dot(perm[...], stream.astype(BF16)).astype(BF16).reshape(-1, r1s[0].shape[1], width)
    share = r1s[0].shape[0]
    for j, piece in enumerate(r1s):
        piece[...] = r1[j * share : (j + 1) * share]


def space_back_kernel(pieces, group, order, *refs):
    xs, r1s, refs = refs[:pieces], refs[pieces : pieces + group], refs[pieces + group :]
    (act, hot, earlier, packed, total, vectors, w_out, w_qkv) = refs[:8]
    (grad_packed, a1, r1_all, sums), refs = refs[8:12], refs[12:]
    input_grads, (grad_out,) = refs[:-1], refs[-1:]

    @pl.when(pl.program_id(0) == 0)
    def _():
        sums[...] = earlier[...]

    raw = jnp.concatenate([x[0] for x in xs], 0) if pieces > 1 else xs[0][0]
    r1 = jnp.concatenate([value[0] for value in r1s], 0)
    r1_all[0] = r1
    count, width = raw.shape
    grad_out[...] = dot(r1, w_out[...], NT).astype(BF16)
    attend_back(
        packed.at[0], slice(0, count), width, grad_out, total.at[0], None, grad_packed.at[0], 4
    )
    grad_normed = dot(grad_packed[0], w_qkv[...], NT)
    embedded, masked = embed(raw, vectors, act[0])
    unit, spread = normalise(embedded)
    gain = vectors[0:1, :]
    a1[0] = (unit * gain + vectors[1:2, :]).astype(BF16)
    stream = r1.astype(F32) + norm_back(unit, spread, gain, grad_normed)
    kept = jnp.where(masked, 0.0, stream)
    if len(input_grads) == 1:
        input_grads[0][0] = kept.astype(BF16)
    else:
        share = count // len(order)
        for at, k in enumerate(order):
            input_grads[k // 2][k % 2, 0] = kept[at * share : (at + 1) * share].astype(BF16)
    whole_sum = jnp.sum(stream, 0, keepdims=True)
    sums[0:1, :] += jnp.sum(grad_normed * unit, 0, keepdims=True)
    sums[1:2, :] += jnp.sum(grad_normed, 0, keepdims=True)
    sums[2:3, :] += whole_sum - jnp.sum(kept, 0, keepdims=True)
    sums[8:, :] += hot[0] * whole_sum


def whole(array):
    rank = len(array.shape)
    return pl.BlockSpec(array.shape, lambda *_: (0,) * rank, pipeline_mode=pl.Buffered(1))


def struct(shape, kind):
    return jax.ShapeDtypeStruct(shape, kind)


def call(kernel, grid, operands, outs, scratch=(), flops=0, meta=None, sums=()):
    if sums:
        own, reads, makes, lead = kernel, len(operands), len(outs), meta is not None
        operands, outs = list(operands), list(outs)
        for arrays in sums:
            length = min(array.shape[0] for array in arrays)
            block = (length // grid[0],) + arrays[0].shape[1:]
            index = lambda i, *_, rank=arrays[0].ndim: (i,) + (0,) * (rank - 1)
            operands += [(array, block, index) for array in arrays]
            outs.append(((length,) + arrays[0].shape[1:], BF16, block, index))
        ends = lead + len(operands), lead + len(operands) + len(outs)

        def kernel(*refs):
            made = refs[ends[0] : ends[1]]
            own(*refs[: lead + reads], *made[:makes], *refs[ends[1] :])
            terms = refs[lead + reads : ends[0]]
            for arrays, out in zip(sums, made[makes:]):
                out[...] = sum(term[...].astype(F32) for term in terms[: len(arrays)]).astype(BF16)
                terms = terms[len(arrays) :]

    in_specs = [
        whole(array) if block is None else pl.BlockSpec(block, index)
        for array, block, index in operands
    ]
    out_specs = [
        pl.BlockSpec(shape, lambda *_, rank=len(shape): (0,) * rank)
        if block is None
        else pl.BlockSpec(block, index)
        for shape, _, block, index in outs
    ]
    moved = sum(a.size * a.dtype.itemsize for a, _, _ in operands)
    return pl.pallas_call(
        kernel,
        grid_spec=pltpu.PrefetchScalarGridSpec(
            num_scalar_prefetch=0 if meta is None else 1,
            grid=grid,
            in_specs=in_specs,
            out_specs=out_specs,
            scratch_shapes=scratch,
        ),
        out_shape=[struct(shape, kind) for shape, kind, _, _ in outs],
        cost_estimate=pl.CostEstimate(flops=flops, bytes_accessed=2 * moved, transcendentals=0),
        compiler_params=pltpu.CompilerParams(vmem_limit_bytes=VMEM_LIMIT),
    )(*(() if meta is None else (meta,)), *[a for a, _, _ in operands])


def collect_kernel(parts, meta, *refs):
    *refs, perm, out, held = refs
    chip = pl.program_id(0)
    for i in range(len(refs) // (2 * parts)):

        @pl.when(chip == i)
        def _(i=i):
            found = [ref[...] for ref in refs[2 * parts * i : 2 * parts * (i + 1)]]
            held[...] = jnp.concatenate(found, 0).reshape(held.shape)

    out[...] = dot(perm[...], held[...]).astype(BF16).reshape(out.shape)


def collect(by_slot, chips, perm, shape, operand):
    p, width = shape[0], shape[-1]
    block = 16
    steps = p // block
    parts = len(by_slot[0])
    span = sum(part.shape[-3] for part, _ in by_slot[0])
    count = len(by_slot)
    operands = []
    for k, pieces in enumerate(by_slot):

        def slot_index(i, h, meta, k=k):
            return 0, jnp.where(i == k // 2, h, jnp.where(i < k // 2, 0, steps - 1)), 0

        operands += [
            operand(piece, (piece[0].shape[-3], block, width), slot_index) for piece in pieces
        ]
    operands.append((perm, None, None))
    outs = [
        (
            (p, count * span, width),
            BF16,
            (block, 2 * span, width),
            lambda i, h, meta: (h, meta[i], 0),
        )
    ]
    return call(
        lambda *refs: collect_kernel(parts, *refs),
        (count // 2, steps),
        operands,
        outs,
        [pltpu.VMEM((block * 2 * span, width), BF16)],
        meta=chips,
    )[0].reshape(shape)


def collect_result_kernel(meta, *refs):
    *pieces, out = refs
    for j, piece in enumerate(pieces):

        @pl.when(pl.program_id(0) == j)
        def _(piece=piece):
            out[...] = piece[...]


def collect_result(pieces, where):
    p, _, frames, width = pieces[0].shape
    return call(
        collect_result_kernel,
        (len(pieces),),
        [(piece, None, None) for piece in pieces],
        [
            (
                (p, len(pieces), frames, width),
                BF16,
                (p, 1, frames, width),
                lambda j, meta: (0, meta[j], 0, 0),
            )
        ],
        meta=where,
    )[0]


def put(outs, slot, value):
    share = outs[0].shape[0]
    outs[slot // share][slot % share] = value


def columns_kernel(meta, *refs, counts, firsts, blocks, split):
    step = pl.program_id(0)
    *refs, held = refs
    local = step % firsts[-1]
    for i, count in enumerate(counts):
        lefts, rights, refs = refs[:count], refs[count : 2 * count], refs[2 * count :]

        @pl.when((local >= firsts[i]) & (local < firsts[i + 1]))
        def _(lefts=lefts, rights=rights):
            total = sum(dot(l[...], r[...], TN) for l, r in zip(lefts, rights))
            held[...] = total.astype(BF16)

    shares = len(split)
    size = held.shape[0] // blocks
    per = firsts[-1] // shares
    for part in range(2 * shares):
        two = part >= shares and split[part - shares]
        own, refs = refs[: 1 + two], refs[1 + two :]

        @pl.when(step // per == part)
        def _(first=(part % shares) * blocks, own=own):
            for slot in range(blocks):
                source = pl.multiple_of(meta[first + slot] * size, size)
                put(own, slot, held[pl.ds(source, size), :])


def columns_grad(pairs, meta, split, tile=512, sums=()):
    shares = len(split)
    blocks = (meta.shape[0] - 1) // shares
    height = pairs[0][0][0].shape[1]
    size = height // blocks
    tile = min([tile] + [rights[0].shape[1] // 2 for _, rights in pairs])
    steps = [rights[0].shape[1] // 2 // tile for _, rights in pairs]
    firsts = [sum(steps[:i]) for i in range(len(steps) + 1)]
    per = firsts[-1] // shares
    operands, flops = [], 0
    for (lefts, rights), first, count in zip(pairs, firsts, steps):
        operands += [(left, None, None) for left in lefts]
        for right in rights:

            def index(i, meta, first=first, count=count):
                core = meta[shares * blocks]
                half = jnp.where(i < firsts[-1], 1 - core, core)
                return 0, half * count + jnp.clip(i % firsts[-1] - first, 0, count - 1)

            operands.append((right, (right.shape[0], tile), index))
            flops += 2 * right.size * height

    def part_out(part, rows):
        block = (rows, size, tile), lambda i, meta: (0, 0, jnp.clip(i - part * per, 0, per - 1))
        return (rows, size, per * tile), BF16, *block

    outs = [part_out(share, blocks) for share in range(shares)]
    for share, two in enumerate(split):
        outs += [part_out(shares + share, blocks // (1 + two))] * (1 + two)
    kernel = lambda *refs: columns_kernel(
        *refs, counts=[len(lefts) for lefts, _ in pairs], firsts=firsts, blocks=blocks, split=split
    )
    scratch = [pltpu.VMEM((height, tile), BF16)]
    return call(kernel, (2 * firsts[-1],), operands, outs, scratch, flops, meta, sums)


def rows_kernel(meta, *refs, step_blocks, steps, blocks):
    step = pl.program_id(0)
    lefts, right, (sent, *outs) = refs[:step_blocks], refs[step_blocks], refs[step_blocks + 1 :]
    value = dot(jnp.concatenate([left[...] for left in lefts], 1), right[...], TN).astype(BF16)
    value = value.reshape(step_blocks, -1, value.shape[-1])
    middle = value.shape[-1] // 2
    halves = value[:, :, :middle], value[:, :, middle:]
    share = steps // len(outs)
    for core in range(2):

        @pl.when(meta[blocks] == core)
        def _(core=core):
            sent[...] = halves[1 - core]

        for i, out in enumerate(outs):

            @pl.when((meta[blocks] == core) & (step >= i * share) & (step < (i + 1) * share))
            def _(core=core, out=out):
                out[...] = halves[core]


def rows_grad(left, right, meta, split, step_blocks=2):
    blocks = meta.shape[0] - 1
    depth, height = left.shape
    size, columns = height // blocks, right.shape[1] // 2
    steps = blocks // step_blocks
    operands = [
        (left, (depth, size), lambda i, meta, j=j: (0, meta[i * step_blocks + j]))
        for j in range(step_blocks)
    ]
    operands.append((right, None, None))
    parts = 1 + split[0]
    share = steps // parts
    block = (step_blocks, size, columns)
    outs = [((blocks, size, columns), BF16, block, lambda i, meta: (i, 0, 0))]
    outs += [
        (
            (blocks // parts, size, columns),
            BF16,
            block,
            lambda i, meta, first=j * share: (jnp.clip(i - first, 0, share - 1), 0, 0),
        )
        for j in range(parts)
    ]
    kernel = lambda *refs: rows_kernel(
        *refs, step_blocks=step_blocks, steps=steps, blocks=blocks
    )
    return call(kernel, (steps,), operands, outs, flops=4 * depth * height * columns, meta=meta)


def body(
    tokens,
    mask_bits,
    action_ids,
    vectors,
    action_table,
    w_space_qkv,
    w_space_out,
    w_time_qkv,
    w_time_out,
    w_up,
    b_up,
    w_down,
    cotangent,
):
    p, clips, frames, width = tokens.shape
    n, layers = lax.axis_size("tile"), lax.axis_size("clip")
    me, layer = lax.axis_index("tile"), lax.axis_index("clip")
    core = me % 2
    group = n // clips
    own_frames = frames // group
    grid_all = n * p
    places = grid_all // group
    clip, part = me // group, me % group
    hidden = w_up.shape[1]
    rows = places * frames

    def swap(value, k, axis="tile"):
        size = lax.axis_size(axis)
        return lax.ppermute(value, axis, [(i, i ^ k) for i in range(size)])

    def row_block(*shape):
        return shape, lambda i: (i,) + (0,) * (len(shape) - 1)

    blocks = n * layers // 2
    tile_bits = [1 << b for b in range(1, n.bit_length() - 1)]

    def orders(hops):
        slots = [(0, None, 0, None)]
        for hop in hops:
            if hop == "scatter":
                choices = [(0, None, 0, c) for c in range(layers)]
            elif hop == "tiles":
                choices = [(0, t, 0, None) for t in range(n // 2)]
            elif hop == "spread":
                choices = [(0, None, c, None) for c in range(layers)]
            else:
                bit = (hop[1], None, 0, None) if hop[0] == "tile" else (0, None, hop[1], None)
                choices = [(0, None, 0, None), bit]
            slots = [
                (a ^ x, t if u is None else u, b ^ y, c if d is None else d)
                for a, t, b, c in slots
                for x, u, y, d in choices
            ]
        where = [
            (layer ^ b if c is None else c) * (n // 2) + ((me ^ a) // 2 if t is None else t)
            for a, t, b, c in slots
        ]
        return jnp.stack([jnp.asarray(w, jnp.int32) for w in where])

    def halves(value, hop):
        if hop is None or isinstance(hop, str):
            return [value]
        middle = value.shape[0] // 2
        return [value[:middle], value[middle:]]

    def meta_of(chains):
        return jnp.concatenate([orders(hops) for hops in chains] + [core.astype(jnp.int32)[None]])

    def begin(make, chains, meta):
        split = [not isinstance(hops[0], str) for hops in chains]
        made = make(meta, split)
        sent, made, parts = list(made[: len(split)]), made[len(split) :], []
        for two in split:
            parts.append(list(made[: 1 + two]))
            made = made[1 + two :]
        return chains, parts, sent

    def cross(begun):
        chains, parts, sent = begun
        return chains, parts, [swap(value, 1) for value in sent]

    def add(values, kind):
        if len(values) == 2 and all(value.dtype == kind for value in values):
            return values[0] + values[1]
        return sum(value.astype(F32) for value in values).astype(kind)

    def land(crossed):
        chains, all_parts, received = crossed
        landed = []
        for hops, parts, came in zip(chains, all_parts, received):
            if isinstance(hops[0], str):
                landed.append([[(add([parts[0], came], BF16), False)]])
            else:
                _, sent = halves(came, hops[0])
                landed.append([[(parts[0], False), (came, True)], add([parts[1], sent], BF16)])
        return chains, landed, 0

    def addends(departed):
        (chains, parts, at), coming = departed
        return [value for value, _ in parts[0][0]] + coming

    def arrived(departed, total):
        chains, parts, at = departed[0]
        hops = chains[0]
        pieces = halves(total, hops[at + 1] if at + 1 < len(hops) else None)
        return chains, [[[(total, len(pieces) == 2)]] + pieces[1:]], at + 1

    def merge(state):
        chains, parts, at = state
        kept = jnp.concatenate([own[0][0][0] for own in parts], -1)
        return chains[:1], [[[(kept, False)]]], at

    def depart(state):
        chains, parts, at = state
        coming = []
        for hops, own in zip(chains, parts):
            hop, value = hops[at], own[0][0][0]
            if hop == "scatter":
                coming.append(lax.psum_scatter(value, "clip", scatter_dimension=0, tiled=True))
            elif hop == "tiles":
                same_core = [list(range(c, n, 2)) for c in range(2)]
                coming.append(
                    lax.psum_scatter(
                        value, "tile", scatter_dimension=0, tiled=True, axis_index_groups=same_core
                    )
                )
            elif hop == "spread":
                share = value.shape[0] // layers
                coming.append(
                    [swap(value[j * share : (j + 1) * share], j, "clip") for j in range(1, layers)]
                )
            else:
                coming.append(swap(own[1], hop[1], hop[0]))
        return state, coming

    def arrive(departed):
        (chains, parts, at), coming = departed
        new_parts = []
        for hops, own, came in zip(chains, parts, coming):
            following = hops[at + 1] if at + 1 < len(hops) else None
            kind = F32 if following is None else BF16
            kept = [v[: v.shape[0] // 2] if first else v for v, first in own[0]]
            if hops[at] == "spread":
                values = [kept[0][: kept[0].shape[0] // layers]] + came
            else:
                values = [came] if isinstance(hops[at], str) else kept + [came]
            summed = [add(piece, kind) for piece in zip(*[halves(v, following) for v in values])]
            new_parts.append([[(summed[0], False)]] + summed[1:])
        return chains, new_parts, at + 1

    def last_swap(state):
        own = jnp.concatenate([own[0][0][0][0].astype(F32) for own in state[1]], 1)
        size = own.shape[0] // 2
        mine = lax.dynamic_slice_in_dim(own, core * size, size, 0)
        other = lax.dynamic_slice_in_dim(own, (1 - core) * size, size, 0)
        return mine, swap(other.astype(BF16), 1)

    def join(mine, other, widths):
        whole_parts, at = [], 0
        for w in widths:
            a, b = mine[:, at : at + w // 2], other[:, at : at + w // 2].astype(F32)
            whole_parts.append(
                jnp.where(core == 0, jnp.concatenate([a, b], 1), jnp.concatenate([b, a], 1))
            )
            at += w // 2
        return whole_parts

    one_way = [("tile", bit) for bit in tile_bits]
    other_way = one_way[::-1]
    clip_bits = [("clip", 1 << b) for b in range(layers.bit_length() - 1)]
    up_chains, down_chains = [one_way + clip_bits], [["scatter"] + one_way]
    time_chains = [["scatter"] + other_way]
    space_chains = [one_way + ["spread"], other_way + ["spread"]]

    order = [k for j in range(group) for k in range(j, n, group)]
    onehot = (action_ids[..., None] == lax.iota(jnp.int32, action_table.shape[0])).astype(F32)
    action_rows = jnp.einsum("cfa,ad->cfd", onehot, action_table, precision=lax.Precision.HIGHEST)
    act_time = lax.dynamic_index_in_dim(action_rows, clip, 0, keepdims=False)
    act_space = lax.dynamic_slice_in_dim(act_time, part * own_frames, own_frames, 0)[:, None, :]

    regular = p % 16 == 0 and 2 * own_frames == 16
    deal_back = None
    if regular:
        at = lax.iota(jnp.int32, 16 * 2 * own_frames)
        place, frame = at % 16, at // 16
        source = place * 2 * own_frames + (frame + core * own_frames) % (2 * own_frames)
        deal_back = (at[:, None] == source[None, :]).astype(BF16)
    marked = jnp.where((mask_bits > 0)[..., None], jnp.asarray(MASKED, BF16), tokens)
    marked = marked.reshape(p, n, own_frames, width)
    chunks = 2
    span = own_frames // chunks
    blocks_of = [lax.dynamic_index_in_dim(marked, me ^ k, 1, keepdims=False) for k in order]
    sources = [
        [value[:, c * span : (c + 1) * span].transpose(1, 0, 2) for value in blocks_of]
        for c in range(chunks)
    ]

    def send_out(parts):
        return [part if k == 0 else swap(part, k) for k, part in zip(order, parts)]

    cot_pieces = [
        lax.dynamic_index_in_dim(cotangent, clip ^ j, 1, keepdims=False).reshape(p * frames, width)
        for j in range(n // group)
    ]
    block = 16
    count = block * frames
    sub = min(count, 128)
    index = lax.iota(jnp.int32, count)
    slot, place = index // block, index % block
    frame_of_slot = ((part ^ (slot // own_frames)) * own_frames) + slot % own_frames
    target = place * frames + frame_of_slot
    perm_back = (target[:, None] == index[None, :]).astype(BF16)
    perm = (index[:, None] == target[None, :]).astype(BF16)
    seq = lax.iota(jnp.int32, sub)
    same = (seq[:, None] // frames) == (seq[None, :] // frames)
    bias = jnp.where(same & (seq[:, None] <= seq[None, :]), 0.0, NEGATIVE).astype(F32)
    own_hot = lax.dynamic_slice_in_dim(
        lax.dynamic_index_in_dim(onehot, clip, 0, keepdims=False), part * own_frames, own_frames, 0
    )[..., None]
    where_clip = clip ^ lax.iota(jnp.int32, clips)
    where_chip = (me // 2) ^ lax.iota(jnp.int32, n // 2)
    tables = dict(
        act_time=act_time,
        act_space=act_space,
        perm=perm,
        perm_back=perm_back,
        bias=bias,
        own_hot=own_hot,
        where_clip=where_clip,
        where_chip=where_chip,
        deal_back=deal_back,
        **{
            name: meta_of(chains)
            for name, chains in (
                ("up", up_chains),
                ("down", down_chains),
                ("time", time_chains),
                ("space", space_chains),
            )
        },
    )
    whole_at = [at for at, k in enumerate(order) if k in (0, 1, n - 1)]
    sources = [
        [blocks_of[at].transpose(1, 0, 2) if at in whole_at else part for at, part in enumerate(parts)]
        for parts in sources
    ]
    pieces = [send_out(sources[0])]
    pieces[0], sources, cot_pieces, tables = hold_parts(pieces[0], sources, cot_pieces, tables)
    for c in range(1, chunks):
        pieces.append(
            [
                pieces[0][at] if at in whole_at else swap(part, order[at])
                for at, part in enumerate(sources[c])
            ]
        )
    cot_pieces = [
        piece if j == 0 else swap(piece, j * group) for j, piece in enumerate(cot_pieces)
    ]
    if p % 16:
        pieces = [
            [
                jnp.concatenate(
                    [
                        part[c * span : (c + 1) * span] if at in whole_at else part
                        for at, part in enumerate(parts)
                    ],
                    1,
                )
            ]
            for c, parts in enumerate(pieces)
        ]

    def piece_blocks(c):
        return [
            (x, (1,) + x.shape[1:], lambda i, first=c * span * (x.shape[0] > span): (first + i, 0, 0))
            for x in pieces[c]
        ]

    kinds = len(pieces[0])
    act_time, act_space, own_hot = (tables[name] for name in ("act_time", "act_space", "own_hot"))
    perm, perm_back, bias = (tables[name] for name in ("perm", "perm_back", "bias"))
    where_clip, where_chip, deal_back = (
        tables[name] for name in ("where_clip", "where_chip", "deal_back")
    )

    head_flops = 2 * HEADS * HEAD_DIM

    def frame_block(*shape):
        return (1,) + shape, lambda i: (i, 0, 0)

    def chunk_block(first, *shape):
        return (1,) + shape, lambda i: (first + i, 0, 0)

    space, both = [], []
    for c in range(chunks):
        packed, o1, total, *parts = call(
            lambda *refs: space_forward_kernel(group, kinds, *refs),
            (span,),
            piece_blocks(c)
            + [
                (act_space, *chunk_block(c * span, 1, width)),
                (vectors, None, None),
                (w_space_qkv, None, None),
            ],
            [
                ((span, grid_all, 3 * width), BF16, *frame_block(grid_all, 3 * width)),
                ((span, grid_all, width), BF16, *frame_block(grid_all, width)),
                ((span, HEADS, grid_all), F32, *frame_block(HEADS, grid_all)),
            ]
            + [
                (
                    (span, 2, places, width),
                    BF16,
                    (1, 2, places, width),
                    lambda i: (i, 0, 0, 0),
                )
            ]
            * group,
            flops=2 * span * grid_all * width * 3 * width
            + 16 * span * grid_all * grid_all * head_flops,
        )
        space.append((packed, o1, total))
        both.append([part if j == 0 else swap(part, j) for j, part in enumerate(parts)])
    both = [both[c][j] for j in range(group) for c in range(chunks)]

    def slot_block(size):
        return (size, block, width), lambda i: (0, i, 0)

    total_block = ((HEADS, count), lambda i: (0, i))
    h1, h2, a2, packed_two, o2, total_two = call(
        lambda *refs: time_forward_kernel(sub, len(both), *refs),
        (places // block,),
        [
            (value, (span, None, block, width), lambda i, which=which: (0, which, i, 0))
            for which in range(2)
            for value in both
        ]
        + [
            (act_time, None, None),
            (perm, None, None),
            (bias, None, None),
            (vectors, None, None),
            (w_space_out, None, None),
            (w_time_qkv, None, None),
            (w_time_out, None, None),
        ],
        [
            ((rows, width), F32, *row_block(count, width)),
            ((rows, width), F32, *row_block(count, width)),
            ((rows, width), BF16, *row_block(count, width)),
            ((rows, 3 * width), BF16, *row_block(count, 3 * width)),
            ((rows, width), BF16, *row_block(count, width)),
            ((HEADS, rows), F32, *total_block),
        ],
        flops=2 * rows * width * 5 * width + 16 * rows * sub * head_flops,
    )

    step = min(p * frames, 256)
    per = p * frames // step

    def piece_block(j):
        return (step, width), lambda i, j=j: (jnp.clip(i - j * per, 0, per - 1), 0)

    *result_pieces, cot, z, dur, a3, r2, sums_three, bias_up = call(
        lambda *refs: feed_kernel(1024, len(cot_pieces), per, *refs),
        (rows // step,),
        [(h2, *row_block(step, width))]
        + [(piece, *piece_block(j)) for j, piece in enumerate(cot_pieces)]
        + [
            (vectors, None, None),
            (b_up[None, :], None, None),
            (w_up, None, None),
            (w_down, None, None),
        ],
        [((p * frames, width), BF16, *piece_block(j)) for j in range(len(cot_pieces))]
        + [
            ((rows, width), BF16, *row_block(step, width)),
            ((rows, hidden), BF16, *row_block(step, hidden)),
            ((rows, hidden), BF16, *row_block(step, hidden)),
            ((rows, width), BF16, *row_block(step, width)),
            ((rows, width), F32, *row_block(step, width)),
            ((8, width), F32, None, None),
            ((1, hidden), F32, None, None),
        ],
        flops=8 * rows * width * hidden,
    )

    result_pieces = [
        (piece if j == 0 else swap(piece, j * group)).reshape(p, 1, frames, width)
        for j, piece in enumerate(result_pieces)
    ]

    def make_down(meta, split):
        if hidden // blocks % 128:
            return columns_grad([([z], [cot])], meta, split, 256)
        return rows_grad(z, cot, meta, split)

    def make_up(meta, split):
        return columns_grad([([a3], [dur])], meta, split)

    up = begin(make_up, up_chains, tables["up"])
    cot, up, result_pieces[:-1] = hold_parts(cot, up, result_pieces[:-1])
    up = cross(up)
    down = begin(make_down, down_chains, tables["down"])
    r2, down, up, result_pieces = hold_parts(r2, down, up, result_pieces)
    up, down = depart(land(up)), cross(down)

    grad_packed_two, r2_low, sums_two, *r1_parts = call(
        lambda *refs: time_back_kernel(sub, *refs),
        (places // block,),
        [
            (r2, *row_block(count, width)),
            (h1, *row_block(count, width)),
            (packed_two, *row_block(count, 3 * width)),
            (total_two, *total_block),
            (perm_back, None, None),
            (bias, None, None),
            (vectors, None, None),
            (w_time_out, None, None),
            (w_time_qkv, None, None),
        ],
        [
            ((rows, 3 * width), BF16, *row_block(count, 3 * width)),
            ((rows, width), BF16, *row_block(count, width)),
            ((8, width), F32, None, None),
        ]
        + [((own_frames, places, width), BF16, *slot_block(own_frames))] * group,
        [pltpu.VMEM((count, width), BF16)],
        flops=2 * rows * width * 4 * width + 40 * rows * sub * head_flops,
    )
    grad_packed_two, up, down = hold_parts(grad_packed_two, up, down)
    r1_parts = [r1 if j == 0 else swap(r1, j) for j, r1 in enumerate(r1_parts)]
    extra = []

    def make_time(meta, split):
        pairs = [([a2], [grad_packed_two]), ([o2], [r2_low])]
        beside = [[down[1][0][0], down[2][0]], addends(up)]
        *made, down_total, up_total = columns_grad(pairs, meta, split, sums=beside)
        extra.extend((down_total, up_total))
        return made

    time = begin(make_time, time_chains, tables["time"])
    down = down[0], [[[(extra[0], False)]]], 0
    up = arrived(up, extra[1])

    dealt = 1 if p % 16 else n

    def send_back(parts):
        if dealt == 1:
            parts = [parts[0][:, at * p : (at + 1) * p] for at in range(n)]
            parts = [parts[order.index(k)] for k in range(n)]
            parts = [jnp.stack(parts[2 * j : 2 * j + 2]) for j in range(n // 2)]
        return [part if j == 0 else swap(part, 2 * j) for j, part in enumerate(parts)]

    def pass_on(came):
        crossed = swap(jnp.stack([value[1] for value in came]), 1)
        return [found for j, value in enumerate(came) for found in ((value, 0), (crossed, j))]

    def operand(found, block, index):
        return found[0], (None,) + block, lambda *i: (found[1],) + index(*i)

    def space_back(c, earlier, sums=()):
        packed, _, total = space[c]
        return call(
            lambda *refs: space_back_kernel(kinds, group, order, *refs),
            (span,),
            piece_blocks(c)
            + [(r1, *chunk_block(c * span, places, width)) for r1 in r1_parts]
            + [
                (act_space, *chunk_block(c * span, 1, width)),
                (own_hot, *chunk_block(c * span, action_table.shape[0], 1)),
                (earlier, None, None),
                (packed, *frame_block(grid_all, 3 * width)),
                (total, *frame_block(HEADS, grid_all)),
                (vectors, None, None),
                (w_space_out, None, None),
                (w_space_qkv, None, None),
            ],
            [
                ((span, grid_all, 3 * width), BF16, *frame_block(grid_all, 3 * width)),
                ((span, grid_all, width), BF16, *frame_block(grid_all, width)),
                ((span, grid_all, width), BF16, *frame_block(grid_all, width)),
                ((8 + action_table.shape[0], width), F32, None, None),
            ]
            + (
                [((span, grid_all, width), BF16, *frame_block(grid_all, width))]
                if dealt == 1
                else [
                    ((2, span, p, width), BF16, (2, 1, p, width), lambda i: (0, i, 0, 0))
                ]
                * (n // 2)
            ),
            [pltpu.VMEM((grid_all, width), BF16)],
            flops=2 * span * grid_all * width * 4 * width
            + 40 * span * grid_all * grid_all * head_flops,
            sums=sums,
        )

    r1_parts, time, up, down = hold_parts(r1_parts, time, up, down)
    up, down, time = depart(up), depart(down), cross(time)
    early = jnp.concatenate([sums_two, sums_three, bias_up.reshape(-1, width)], 0)
    back = [space_back(0, jnp.zeros((8 + action_table.shape[0], width), F32))]
    back[0], r1_parts, time, up = hold_parts(back[0], r1_parts, time, up)
    input_pieces = [send_back(back[0][4:])]
    up = depart(arrive(up))
    for c in range(1, chunks):
        beside = [[time[1][0][0], time[2][0]]] if c == 1 else []
        back.append(space_back(c, back[-1][3], beside))
        if c == 1:
            *back[c], time_total = back[c]
    time = time[0], [[[(time_total, False)]]], 0
    back, input_pieces, up, time = hold_parts(back, input_pieces, up, time)
    input_pieces[0] = pass_on(input_pieces[0])
    for c in range(1, chunks):
        input_pieces.append(send_back(back[c][4:]))
    up, time = depart(arrive(up)), depart(time)
    grads_one, a1s, r1s = list(zip(*back))[:3]

    def flat(values):
        return [value.reshape(-1, value.shape[-1]) for value in values]

    def make_space(meta, split):
        return columns_grad(
            [
                (flat(a1s), flat(grads_one)),
                (flat([o1 for _, o1, _ in space]), flat(r1s)),
            ],
            meta,
            split,
        )

    small = jnp.concatenate([back[-1][3], early], 0)
    small_hops = [("tile", 1 << b) for b in range(n.bit_length() - 1)] + clip_bits

    space_sum = begin(make_space, space_chains, tables["space"])
    where_clip, space_sum, up, down, input_pieces = hold_parts(
        where_clip, space_sum, up, down, input_pieces
    )
    space_sum = cross(space_sum)
    small_came = swap(small, small_hops[0][1], small_hops[0][0])
    up = arrive(up)
    while up[2] < len(up[0][0]):
        up = arrive(depart(up))
    up, down = last_swap(up), depart(arrive(down))
    result_out = collect_result(result_pieces, where_clip)
    space_sum, result_out, small_came = hold_parts(space_sum, result_out, small_came)
    space_sum, small = land(space_sum), small + small_came
    input_pieces[1:] = [pass_on(came) for came in input_pieces[1:]]
    time = arrive(time)

    def collect_input(input_pieces, where_chip):
        by_slot = [[pieces_of[k] for pieces_of in input_pieces] for k in range(n)]
        if regular:
            input_grad = collect(by_slot, where_chip, deal_back, tokens.shape, operand)
        else:
            input_grad = jnp.zeros((p, n, own_frames, width), BF16)
            for k, parts in enumerate(by_slot):
                piece = jnp.concatenate([value[at] for value, at in parts], 0)
                input_grad = lax.dynamic_update_slice_in_dim(
                    input_grad, piece.transpose(1, 0, 2)[:, None], me ^ k, 1
                )
            input_grad = input_grad.reshape(tokens.shape)
        return input_grad

    rounds = max(len(small_hops) - 1, len(space_sum[0][0]) + 1, 2 * len(one_way) + 1)
    for r in range(rounds):
        departed = small_came = time_moves = down_moves = None
        if r < len(space_sum[0][0]):
            if r == len(one_way):
                space_sum = merge(space_sum)
            departed = depart(space_sum)
        if r + 1 < len(small_hops):
            small_came = swap(small, small_hops[r + 1][1], small_hops[r + 1][0])
        if r >= len(one_way) and time[2] < len(time[0][0]):
            time_moves = depart(time)
        if r > len(one_way) and down[2] < len(down[0][0]):
            down_moves = depart(down)
        others = [down, input_pieces, up] if r == 0 else []
        if r == 1:
            input_grad = collect_input(input_pieces, where_chip)
            others = [input_grad]
        departed, small_came, time_moves, down_moves, *others = hold_parts(
            departed, small_came, time_moves, down_moves, *others
        )
        if r == 0:
            down, input_pieces, up = others
            down = arrive(down)
        if r == 1:
            (input_grad,) = others
        if time_moves is not None:
            time = arrive(time_moves)
            if time[2] == len(time[0][0]):
                time_last = last_swap(time)
        if down_moves is not None:
            down = arrive(down_moves)
            if down[2] == len(down[0][0]):
                down_last = last_swap(down)
        if departed is not None:
            space_sum = arrive(departed)
        if small_came is not None:
            small = small + small_came
        if r + 1 == len(space_sum[0][0]):
            space_last = last_swap(space_sum)
    at = 8 + action_table.shape[0]
    sums = small[at:]
    (down_out,) = join(*down_last, [width])
    (up_out,) = join(*up, [hidden])
    time_qkv, time_out = join(*time_last, [3 * width, width])
    space_qkv, space_out = join(*space_last, [3 * width, width])
    return (
        result_out,
        input_grad,
        jnp.concatenate([small[:2], sums[:2], sums[8:11], small[2:3]], 0),
        small[8:at],
        space_qkv,
        space_out,
        time_qkv,
        time_out,
        up_out,
        sums[16:].reshape(hidden),
        down_out,
    )


def hold_parts(*values):
    leaves, tree = jax.tree.flatten(values)
    arrays = [i for i, leaf in enumerate(leaves) if isinstance(leaf, jax.Array)]
    held = lax.optimization_barrier([leaves[i] for i in arrays])
    for i, leaf in zip(arrays, held):
        leaves[i] = leaf
    return jax.tree.unflatten(tree, leaves)


def solution(mesh):
    spread = P("tile", "clip", None, None)
    rows = P(("clip", "tile"), None)
    return jax.shard_map(
        body,
        mesh=mesh,
        in_specs=(spread, P("tile", "clip", None), P("clip", None)) + (P(),) * 9 + (spread,),
        out_specs=(spread, spread, P(), P(), rows, rows, rows, rows, rows, P(), rows),
        check_vma=False,
    )
```

```python
import jax
import jax.numpy as jnp
from jax import lax
from jax.experimental import pallas as pl
from jax.experimental.pallas import tpu as pltpu
from jax.sharding import PartitionSpec as P

HEADS = 16
HEAD_DIM = 64
PAIR = 2 * HEAD_DIM
EPSILON = 1e-05
NEGATIVE = -1e30
MASKED = 2.0**100
SEEN = 2.0**99
LOG2E = 1.4426950408889634
SCALE = HEAD_DIM**-0.5
F32 = jnp.float32
BF16 = jnp.bfloat16
VMEM_LIMIT = 60 * 1024 * 1024

NN = (((1,), (0,)), ((), ()))
NT = (((1,), (1,)), ((), ()))
TN = (((0,), (0,)), ((), ()))


def dot(left, right, form=NN):
    return lax.dot_general(left, right, form, preferred_element_type=F32)


def normalise(values):
    centred = values - jnp.mean(values, -1, keepdims=True)
    spread = lax.rsqrt(jnp.mean(centred * centred, -1, keepdims=True) + EPSILON)
    return centred * spread, spread


def norm_back(unit, spread, gain, upstream):
    scaled = upstream * gain
    return spread * (
        scaled
        - jnp.mean(scaled, -1, keepdims=True)
        - unit * jnp.mean(scaled * unit, -1, keepdims=True)
    )


def half_masks():
    lane = lax.broadcasted_iota(jnp.int32, (1, PAIR), 1)
    low = (lane < HEAD_DIM).astype(F32).astype(BF16)
    high = (lane >= HEAD_DIM).astype(F32).astype(BF16)
    return low, high


def pair_slices(packed, rows, width, pair):
    at = pair * PAIR
    return [packed[rows, part * width + at : part * width + at + PAIR] for part in range(3)]


def pair_slices(packed, rows, width, pair):
    at = pair * PAIR
    return [packed[rows, part * width + at : part * width + at + PAIR] for part in range(3)]


def attend_forward(packed, rows, width, out, total, bias, batch):
    masks = half_masks()
    lane = lax.broadcasted_iota(jnp.int32, (1, PAIR), 1)
    pairs = width // PAIR
    for first in range(0, pairs, batch):
        group = range(first, min(first + batch, pairs))
        loaded = [pair_slices(packed, rows, width, pair) for pair in group]
        scores = [
            dot(keys, queries * masks[side], NT) * (SCALE * LOG2E)
            for queries, keys, _ in loaded
            for side in range(2)
        ]
        if bias is not None:
            scores = [value + bias for value in scores]
        highest = [jnp.max(value, 0, keepdims=True) for value in scores]
        shares = [jnp.exp2(value - top) for value, top in zip(scores, highest)]
        weights = [jnp.sum(value, 0, keepdims=True) for value in shares]
        shares = [(value * (1.0 / weight)).astype(BF16) for value, weight in zip(shares, weights)]
        blended = [dot(value, loaded[i // 2][2], TN) for i, value in enumerate(shares)]
        total[2 * first : 2 * group.stop, rows] = jnp.concatenate(
            [top + jnp.log2(weight) for top, weight in zip(highest, weights)], 0
        )
        for i, pair in enumerate(group):
            out[rows, pair * PAIR : (pair + 1) * PAIR] = jnp.where(
                lane < HEAD_DIM, blended[2 * i], blended[2 * i + 1]
            ).astype(BF16)


def attend_forward_rows(packed, rows, width, out, total, batch):
    masks = half_masks()
    lane = lax.broadcasted_iota(jnp.int32, (1, PAIR), 1)
    pairs = width // PAIR
    for first in range(0, pairs, batch):
        group = range(first, min(first + batch, pairs))
        loaded = [pair_slices(packed, rows, width, pair) for pair in group]
        scores = [
            dot(queries * masks[side], keys, NT) * (SCALE * LOG2E)
            for queries, keys, _ in loaded
            for side in range(2)
        ]
        ones = [jnp.concatenate([v, jnp.ones_like(v)], 1) for _, _, v in loaded]
        highest = [jnp.max(value, 1, keepdims=True) for value in scores]
        shares = [jnp.exp2(value - top).astype(BF16) for value, top in zip(scores, highest)]
        blended = [dot(value, ones[i // 2]) for i, value in enumerate(shares)]
        sums = [b[:, PAIR:] for b in blended]
        blended = [b[:, :PAIR] * (1.0 / w) for b, w in zip(blended, sums)]
        logs = [top + jnp.log2(w) for top, w in zip(highest, sums)]
        for i, pair in enumerate(group):
            lg = jnp.where(lane < HEAD_DIM, logs[2*i], logs[2*i+1]).T
            total[2 * pair : 2 * pair + 1, rows] = lg[0:1]
            total[2 * pair + 1: 2 * pair + 2, rows] = lg[HEAD_DIM:HEAD_DIM+1]
            out[rows, pair * PAIR : (pair + 1) * PAIR] = jnp.where(
                lane < HEAD_DIM, blended[2 * i], blended[2 * i + 1]
            ).astype(BF16)


def attend_back(packed, rows, width, grad_out, total, bias, out, batch):
    masks = half_masks()
    pairs = width // PAIR
    for first in range(0, pairs, batch):
        group = range(first, min(first + batch, pairs))
        loaded = [pair_slices(packed, rows, width, pair) for pair in group]
        upstream = [grad_out[rows, pair * PAIR : (pair + 1) * PAIR] for pair in group]
        heads = [(i, side) for i in range(len(group)) for side in range(2)]
        own_q = [loaded[i][0] * masks[side] for i, side in heads]
        own_k = [loaded[i][1] * masks[side] for i, side in heads]
        own_up = [upstream[i] * masks[side] for i, side in heads]
        scores = [dot(loaded[i][1], own, NT) * (SCALE * LOG2E) for (i, _), own in zip(heads, own_q)]
        grad_shares = [dot(loaded[i][2], own, NT) for (i, _), own in zip(heads, own_up)]
        if bias is not None:
            scores = [value + bias for value in scores]
        sums = total[2 * first : 2 * group.stop, rows]
        shares = [jnp.exp2(value - sums[i : i + 1]) for i, value in enumerate(scores)]
        weighted = [value * grad for value, grad in zip(shares, grad_shares)]
        inner = [jnp.sum(value, 0, keepdims=True) for value in weighted]
        grad_scores = [
            (value - share * total_inner).astype(BF16)
            for value, share, total_inner in zip(weighted, shares, inner)
        ]
        grad_q = [dot(value, own, TN) for value, own in zip(grad_scores, own_k)]
        grad_k = [dot(value, own) for value, own in zip(grad_scores, own_q)]
        grad_v = [dot(value.astype(BF16), own) for value, own in zip(shares, own_up)]
        for i, pair in enumerate(group):
            at = pair * PAIR
            for part, (grad, scale) in enumerate(((grad_q, SCALE), (grad_k, SCALE), (grad_v, 1.0))):
                out[rows, part * width + at : part * width + at + PAIR] = (
                    (grad[2 * i] + grad[2 * i + 1]) * scale
                ).astype(BF16)


def embed(raw, vectors, actions):
    raw = raw.astype(F32)
    masked = raw > SEEN
    return jnp.where(masked, vectors[7:8, :], raw) + actions, masked


def space_forward_kernel(group, pieces, *refs):
    xs, (act, vectors, w_qkv, packed, out, total, *parts) = refs[:pieces], refs[pieces:]
    raw = jnp.concatenate([x[0] for x in xs], 0) if pieces > 1 else xs[0][0]
    count, width = raw.shape
    embedded, _ = embed(raw, vectors, act[0])
    unit, _ = normalise(embedded)
    normed = (unit * vectors[0:1, :] + vectors[1:2, :]).astype(BF16)
    packed[0] = dot(normed, w_qkv[...]).astype(BF16)
    attend_forward_rows(packed.at[0], slice(0, count), width, out.at[0], total.at[0], 8)
    share = count // group
    for j in range(group):
        parts[j][0, 0] = raw[j * share : (j + 1) * share]
        parts[j][0, 1] = out[0, j * share : (j + 1) * share]


def time_forward_kernel(sub, pieces, *refs):
    xs, o1s, refs = refs[:pieces], refs[pieces : 2 * pieces], refs[2 * pieces :]
    (act, perm, bias, vectors, w_space_out, w_qkv, w_out, h1, h2, a2, packed, o2, total) = refs
    x = jnp.concatenate([value[...] for value in xs], 0)
    o1 = jnp.concatenate([value[...] for value in o1s], 0)
    frames, places, width = x.shape
    count = frames * places
    raw = dot(perm[...], x.reshape(count, width))
    blended = dot(perm[...], o1.reshape(count, width)).astype(BF16)
    actions = jnp.broadcast_to(act[...][None], (places, frames, width)).reshape(count, width)
    embedded, _ = embed(raw, vectors, actions)
    after_space = embedded + dot(blended, w_space_out[...])
    h1[...] = after_space
    unit, _ = normalise(after_space)
    normed = (unit * vectors[2:3, :] + vectors[3:4, :]).astype(BF16)
    a2[...] = normed
    packed[...] = dot(normed, w_qkv[...]).astype(BF16)
    for start in range(0, count, sub):
        attend_forward(packed, slice(start, start + sub), width, o2, total, bias[...], 8)
    h2[...] = after_space + dot(o2[...], w_out[...])


def feed_kernel(tile, pieces, per, h2, *refs):
    cots, (vectors, b_up, w_up, w_down), refs = refs[:pieces], refs[pieces : pieces + 4], refs[pieces + 4 :]
    results, (cot, z, dur, a3, r2, sums, bias_grad) = refs[:pieces], refs[pieces:]
    piece = pl.program_id(0) // per
    for j in range(pieces):

        @pl.when(piece == j)
        def _(j=j):
            cot[...] = cots[j][...]

    @pl.when(pl.program_id(0) == 0)
    def _():
        sums[...] = jnp.zeros_like(sums)
        bias_grad[...] = jnp.zeros_like(bias_grad)

    after = h2[...]
    unit, spread = normalise(after)
    gain = vectors[4:5, :]
    normed = (unit * gain + vectors[5:6, :]).astype(BF16)
    a3[...] = normed
    upstream_low = cot[...]
    c = 0.7978845608028654
    total = after + vectors[6:7, :]
    grad_normed = jnp.zeros_like(after)
    for at in range(0, w_up.shape[1], tile):
        cols = slice(at, at + tile)
        hidden = dot(normed, w_up[:, cols]) + b_up[:, cols]
        grad_active = dot(upstream_low, w_down[cols, :], NT)
        square = hidden * hidden
        gate = 0.5 * jnp.tanh(hidden * (c + (c * 0.044715) * square)) + 0.5
        active = hidden * gate
        slope = gate + active * (1.0 - gate) * (2.0 * c + (6.0 * c * 0.044715) * square)
        grad_hidden = grad_active * slope
        bias_grad[:, cols] += jnp.sum(grad_hidden, 0, keepdims=True)
        active = active.astype(BF16)
        grad_hidden = grad_hidden.astype(BF16)
        z[:, cols] = active
        dur[:, cols] = grad_hidden
        total = total + dot(active, w_down[cols, :])
        grad_normed = grad_normed + dot(grad_hidden, w_up[:, cols], NT)
    for j in range(pieces):

        @pl.when(piece == j)
        def _(j=j):
            results[j][...] = total.astype(BF16)

    upstream = upstream_low.astype(F32)
    r2[...] = upstream + norm_back(unit, spread, gain, grad_normed)
    sums[0:1, :] += jnp.sum(grad_normed * unit, 0, keepdims=True)
    sums[1:2, :] += jnp.sum(grad_normed, 0, keepdims=True)
    sums[2:3, :] += jnp.sum(upstream, 0, keepdims=True)


def time_back_kernel(
    sub, r2, h1, packed, total, perm, bias, vectors, w_out, w_qkv, grad_packed, r2_low, sums, *rest
):
    *r1s, grad_out = rest

    @pl.when(pl.program_id(0) == 0)
    def _():
        sums[...] = jnp.zeros_like(sums)

    count, width = r2.shape
    stream = r2[...]
    low = stream.astype(BF16)
    r2_low[...] = low
    grad_out[...] = dot(low, w_out[...], NT).astype(BF16)
    for start in range(0, count, sub):
        attend_back(
            packed, slice(start, start + sub), width, grad_out, total, bias[...], grad_packed, 8
        )
    grad_normed = dot(grad_packed[...], w_qkv[...], NT)
    unit, spread = normalise(h1[...])
    stream = stream + norm_back(unit, spread, vectors[2:3, :], grad_normed)
    sums[0:1, :] += jnp.sum(grad_normed * unit, 0, keepdims=True)
    sums[1:2, :] += jnp.sum(grad_normed, 0, keepdims=True)
    r1 = dot(perm[...], stream.astype(BF16)).astype(BF16).reshape(-1, r1s[0].shape[1], width)
    share = r1s[0].shape[0]
    for j, piece in enumerate(r1s):
        piece[...] = r1[j * share : (j + 1) * share]


def space_back_kernel(pieces, group, order, *refs):
    xs, r1s, refs = refs[:pieces], refs[pieces : pieces + group], refs[pieces + group :]
    (act, hot, earlier, packed, total, vectors, w_out, w_qkv) = refs[:8]
    (grad_packed, a1, r1_all, sums), refs = refs[8:12], refs[12:]
    input_grads, (grad_out,) = refs[:-1], refs[-1:]

    @pl.when(pl.program_id(0) == 0)
    def _():
        sums[...] = earlier[...]

    raw = jnp.concatenate([x[0] for x in xs], 0) if pieces > 1 else xs[0][0]
    r1 = jnp.concatenate([value[0] for value in r1s], 0)
    r1_all[0] = r1
    count, width = raw.shape
    grad_out[...] = dot(r1, w_out[...], NT).astype(BF16)
    attend_back(
        packed.at[0], slice(0, count), width, grad_out, total.at[0], None, grad_packed.at[0], 8
    )
    grad_normed = dot(grad_packed[0], w_qkv[...], NT)
    embedded, masked = embed(raw, vectors, act[0])
    unit, spread = normalise(embedded)
    gain = vectors[0:1, :]
    a1[0] = (unit * gain + vectors[1:2, :]).astype(BF16)
    stream = r1.astype(F32) + norm_back(unit, spread, gain, grad_normed)
    kept = jnp.where(masked, 0.0, stream)
    if len(input_grads) == 1:
        input_grads[0][0] = kept.astype(BF16)
    else:
        share = count // len(order)
        for at, k in enumerate(order):
            input_grads[k // 2][k % 2, 0] = kept[at * share : (at + 1) * share].astype(BF16)
    whole_sum = jnp.sum(stream, 0, keepdims=True)
    sums[0:1, :] += jnp.sum(grad_normed * unit, 0, keepdims=True)
    sums[1:2, :] += jnp.sum(grad_normed, 0, keepdims=True)
    sums[2:3, :] += whole_sum - jnp.sum(kept, 0, keepdims=True)
    sums[8:, :] += hot[0] * whole_sum


def whole(array):
    rank = len(array.shape)
    return pl.BlockSpec(array.shape, lambda *_: (0,) * rank, pipeline_mode=pl.Buffered(1))


def struct(shape, kind):
    return jax.ShapeDtypeStruct(shape, kind)


def call(kernel, grid, operands, outs, scratch=(), flops=0, meta=None, sums=()):
    if sums:
        own, reads, makes, lead = kernel, len(operands), len(outs), meta is not None
        operands, outs = list(operands), list(outs)
        for arrays in sums:
            length = min(array.shape[0] for array in arrays)
            block = (length // grid[0],) + arrays[0].shape[1:]
            index = lambda i, *_, rank=arrays[0].ndim: (i,) + (0,) * (rank - 1)
            operands += [(array, block, index) for array in arrays]
            outs.append(((length,) + arrays[0].shape[1:], BF16, block, index))
        ends = lead + len(operands), lead + len(operands) + len(outs)

        def kernel(*refs):
            made = refs[ends[0] : ends[1]]
            own(*refs[: lead + reads], *made[:makes], *refs[ends[1] :])
            terms = refs[lead + reads : ends[0]]
            for arrays, out in zip(sums, made[makes:]):
                out[...] = sum(term[...].astype(F32) for term in terms[: len(arrays)]).astype(BF16)
                terms = terms[len(arrays) :]

    in_specs = [
        whole(array) if block is None else pl.BlockSpec(block, index)
        for array, block, index in operands
    ]
    out_specs = [
        pl.BlockSpec(shape, lambda *_, rank=len(shape): (0,) * rank)
        if block is None
        else pl.BlockSpec(block, index)
        for shape, _, block, index in outs
    ]
    moved = sum(a.size * a.dtype.itemsize for a, _, _ in operands)
    return pl.pallas_call(
        kernel,
        grid_spec=pltpu.PrefetchScalarGridSpec(
            num_scalar_prefetch=0 if meta is None else 1,
            grid=grid,
            in_specs=in_specs,
            out_specs=out_specs,
            scratch_shapes=scratch,
        ),
        out_shape=[struct(shape, kind) for shape, kind, _, _ in outs],
        cost_estimate=pl.CostEstimate(flops=flops, bytes_accessed=2 * moved, transcendentals=0),
        compiler_params=pltpu.CompilerParams(vmem_limit_bytes=VMEM_LIMIT),
    )(*(() if meta is None else (meta,)), *[a for a, _, _ in operands])


def collect_kernel(parts, meta, *refs):
    *refs, perm, out, held = refs
    chip = pl.program_id(0)
    for i in range(len(refs) // (2 * parts)):

        @pl.when(chip == i)
        def _(i=i):
            found = [ref[...] for ref in refs[2 * parts * i : 2 * parts * (i + 1)]]
            held[...] = jnp.concatenate(found, 0).reshape(held.shape)

    out[...] = dot(perm[...], held[...]).astype(BF16).reshape(out.shape)


def collect(by_slot, chips, perm, shape, operand):
    p, width = shape[0], shape[-1]
    block = 16
    steps = p // block
    parts = len(by_slot[0])
    span = sum(part.shape[-3] for part, _ in by_slot[0])
    count = len(by_slot)
    operands = []
    for k, pieces in enumerate(by_slot):

        def slot_index(i, h, meta, k=k):
            return 0, jnp.where(i == k // 2, h, jnp.where(i < k // 2, 0, steps - 1)), 0

        operands += [
            operand(piece, (piece[0].shape[-3], block, width), slot_index) for piece in pieces
        ]
    operands.append((perm, None, None))
    outs = [
        (
            (p, count * span, width),
            BF16,
            (block, 2 * span, width),
            lambda i, h, meta: (h, meta[i], 0),
        )
    ]
    return call(
        lambda *refs: collect_kernel(parts, *refs),
        (count // 2, steps),
        operands,
        outs,
        [pltpu.VMEM((block * 2 * span, width), BF16)],
        meta=chips,
    )[0].reshape(shape)


def collect_result_kernel(meta, *refs):
    *pieces, out = refs
    for j, piece in enumerate(pieces):

        @pl.when(pl.program_id(0) == j)
        def _(piece=piece):
            out[...] = piece[...]


def collect_result(pieces, where):
    p, _, frames, width = pieces[0].shape
    return call(
        collect_result_kernel,
        (len(pieces),),
        [(piece, None, None) for piece in pieces],
        [
            (
                (p, len(pieces), frames, width),
                BF16,
                (p, 1, frames, width),
                lambda j, meta: (0, meta[j], 0, 0),
            )
        ],
        meta=where,
    )[0]


def put(outs, slot, value):
    share = outs[0].shape[0]
    outs[slot // share][slot % share] = value


def columns_kernel(meta, *refs, counts, firsts, blocks, split):
    step = pl.program_id(0)
    *refs, held = refs
    local = step % firsts[-1]
    for i, count in enumerate(counts):
        lefts, rights, refs = refs[:count], refs[count : 2 * count], refs[2 * count :]

        @pl.when((local >= firsts[i]) & (local < firsts[i + 1]))
        def _(lefts=lefts, rights=rights):
            total = sum(dot(l[...], r[...], TN) for l, r in zip(lefts, rights))
            held[...] = total.astype(BF16)

    shares = len(split)
    size = held.shape[0] // blocks
    per = firsts[-1] // shares
    for part in range(2 * shares):
        two = part >= shares and split[part - shares]
        own, refs = refs[: 1 + two], refs[1 + two :]

        @pl.when(step // per == part)
        def _(first=(part % shares) * blocks, own=own):
            for slot in range(blocks):
                source = pl.multiple_of(meta[first + slot] * size, size)
                put(own, slot, held[pl.ds(source, size), :])


def columns_grad(pairs, meta, split, tile=512, sums=()):
    shares = len(split)
    blocks = (meta.shape[0] - 1) // shares
    height = pairs[0][0][0].shape[1]
    size = height // blocks
    tile = min([tile] + [rights[0].shape[1] // 2 for _, rights in pairs])
    steps = [rights[0].shape[1] // 2 // tile for _, rights in pairs]
    firsts = [sum(steps[:i]) for i in range(len(steps) + 1)]
    per = firsts[-1] // shares
    operands, flops = [], 0
    for (lefts, rights), first, count in zip(pairs, firsts, steps):
        operands += [(left, None, None) for left in lefts]
        for right in rights:

            def index(i, meta, first=first, count=count):
                core = meta[shares * blocks]
                half = jnp.where(i < firsts[-1], 1 - core, core)
                return 0, half * count + jnp.clip(i % firsts[-1] - first, 0, count - 1)

            operands.append((right, (right.shape[0], tile), index))
            flops += 2 * right.size * height

    def part_out(part, rows):
        block = (rows, size, tile), lambda i, meta: (0, 0, jnp.clip(i - part * per, 0, per - 1))
        return (rows, size, per * tile), BF16, *block

    outs = [part_out(share, blocks) for share in range(shares)]
    for share, two in enumerate(split):
        outs += [part_out(shares + share, blocks // (1 + two))] * (1 + two)
    kernel = lambda *refs: columns_kernel(
        *refs, counts=[len(lefts) for lefts, _ in pairs], firsts=firsts, blocks=blocks, split=split
    )
    scratch = [pltpu.VMEM((height, tile), BF16)]
    return call(kernel, (2 * firsts[-1],), operands, outs, scratch, flops, meta, sums)


def rows_kernel(meta, *refs, step_blocks, steps, blocks):
    step = pl.program_id(0)
    lefts, right, (sent, *outs) = refs[:step_blocks], refs[step_blocks], refs[step_blocks + 1 :]
    value = dot(jnp.concatenate([left[...] for left in lefts], 1), right[...], TN).astype(BF16)
    value = value.reshape(step_blocks, -1, value.shape[-1])
    middle = value.shape[-1] // 2
    halves = value[:, :, :middle], value[:, :, middle:]
    share = steps // len(outs)
    for core in range(2):

        @pl.when(meta[blocks] == core)
        def _(core=core):
            sent[...] = halves[1 - core]

        for i, out in enumerate(outs):

            @pl.when((meta[blocks] == core) & (step >= i * share) & (step < (i + 1) * share))
            def _(core=core, out=out):
                out[...] = halves[core]


def rows_grad(left, right, meta, split, step_blocks=2):
    blocks = meta.shape[0] - 1
    depth, height = left.shape
    size, columns = height // blocks, right.shape[1] // 2
    steps = blocks // step_blocks
    operands = [
        (left, (depth, size), lambda i, meta, j=j: (0, meta[i * step_blocks + j]))
        for j in range(step_blocks)
    ]
    operands.append((right, None, None))
    parts = 1 + split[0]
    share = steps // parts
    block = (step_blocks, size, columns)
    outs = [((blocks, size, columns), BF16, block, lambda i, meta: (i, 0, 0))]
    outs += [
        (
            (blocks // parts, size, columns),
            BF16,
            block,
            lambda i, meta, first=j * share: (jnp.clip(i - first, 0, share - 1), 0, 0),
        )
        for j in range(parts)
    ]
    kernel = lambda *refs: rows_kernel(
        *refs, step_blocks=step_blocks, steps=steps, blocks=blocks
    )
    return call(kernel, (steps,), operands, outs, flops=4 * depth * height * columns, meta=meta)


def body(
    tokens,
    mask_bits,
    action_ids,
    vectors,
    action_table,
    w_space_qkv,
    w_space_out,
    w_time_qkv,
    w_time_out,
    w_up,
    b_up,
    w_down,
    cotangent,
):
    p, clips, frames, width = tokens.shape
    n, layers = lax.axis_size("tile"), lax.axis_size("clip")
    me, layer = lax.axis_index("tile"), lax.axis_index("clip")
    core = me % 2
    group = n // clips
    own_frames = frames // group
    grid_all = n * p
    places = grid_all // group
    clip, part = me // group, me % group
    hidden = w_up.shape[1]
    rows = places * frames

    def swap(value, k, axis="tile"):
        size = lax.axis_size(axis)
        return lax.ppermute(value, axis, [(i, i ^ k) for i in range(size)])

    def row_block(*shape):
        return shape, lambda i: (i,) + (0,) * (len(shape) - 1)

    blocks = n * layers // 2
    tile_bits = [1 << b for b in range(1, n.bit_length() - 1)]

    def orders(hops):
        slots = [(0, None, 0, None)]
        for hop in hops:
            if hop == "scatter":
                choices = [(0, None, 0, c) for c in range(layers)]
            elif hop == "tiles":
                choices = [(0, t, 0, None) for t in range(n // 2)]
            elif hop == "spread":
                choices = [(0, None, c, None) for c in range(layers)]
            else:
                bit = (hop[1], None, 0, None) if hop[0] == "tile" else (0, None, hop[1], None)
                choices = [(0, None, 0, None), bit]
            slots = [
                (a ^ x, t if u is None else u, b ^ y, c if d is None else d)
                for a, t, b, c in slots
                for x, u, y, d in choices
            ]
        where = [
            (layer ^ b if c is None else c) * (n // 2) + ((me ^ a) // 2 if t is None else t)
            for a, t, b, c in slots
        ]
        return jnp.stack([jnp.asarray(w, jnp.int32) for w in where])

    def halves(value, hop):
        if hop is None or isinstance(hop, str):
            return [value]
        middle = value.shape[0] // 2
        return [value[:middle], value[middle:]]

    def meta_of(chains):
        return jnp.concatenate([orders(hops) for hops in chains] + [core.astype(jnp.int32)[None]])

    def begin(make, chains, meta):
        split = [not isinstance(hops[0], str) for hops in chains]
        made = make(meta, split)
        sent, made, parts = list(made[: len(split)]), made[len(split) :], []
        for two in split:
            parts.append(list(made[: 1 + two]))
            made = made[1 + two :]
        return chains, parts, sent

    def cross(begun):
        chains, parts, sent = begun
        return chains, parts, [swap(value, 1) for value in sent]

    def add(values, kind):
        if len(values) == 2 and all(value.dtype == kind for value in values):
            return values[0] + values[1]
        return sum(value.astype(F32) for value in values).astype(kind)

    def land(crossed):
        chains, all_parts, received = crossed
        landed = []
        for hops, parts, came in zip(chains, all_parts, received):
            if isinstance(hops[0], str):
                landed.append([[(add([parts[0], came], BF16), False)]])
            else:
                _, sent = halves(came, hops[0])
                landed.append([[(parts[0], False), (came, True)], add([parts[1], sent], BF16)])
        return chains, landed, 0

    def addends(departed):
        (chains, parts, at), coming = departed
        return [value for value, _ in parts[0][0]] + coming

    def arrived(departed, total):
        chains, parts, at = departed[0]
        hops = chains[0]
        pieces = halves(total, hops[at + 1] if at + 1 < len(hops) else None)
        return chains, [[[(total, len(pieces) == 2)]] + pieces[1:]], at + 1

    def merge(state):
        chains, parts, at = state
        kept = jnp.concatenate([own[0][0][0] for own in parts], -1)
        return chains[:1], [[[(kept, False)]]], at

    def depart(state):
        chains, parts, at = state
        coming = []
        for hops, own in zip(chains, parts):
            hop, value = hops[at], own[0][0][0]
            if hop == "scatter":
                coming.append(lax.psum_scatter(value, "clip", scatter_dimension=0, tiled=True))
            elif hop == "tiles":
                same_core = [list(range(c, n, 2)) for c in range(2)]
                coming.append(
                    lax.psum_scatter(
                        value, "tile", scatter_dimension=0, tiled=True, axis_index_groups=same_core
                    )
                )
            elif hop == "spread":
                share = value.shape[0] // layers
                coming.append(
                    [swap(value[j * share : (j + 1) * share], j, "clip") for j in range(1, layers)]
                )
            else:
                coming.append(swap(own[1], hop[1], hop[0]))
        return state, coming

    def arrive(departed):
        (chains, parts, at), coming = departed
        new_parts = []
        for hops, own, came in zip(chains, parts, coming):
            following = hops[at + 1] if at + 1 < len(hops) else None
            kind = F32 if following is None else BF16
            kept = [v[: v.shape[0] // 2] if first else v for v, first in own[0]]
            if hops[at] == "spread":
                values = [kept[0][: kept[0].shape[0] // layers]] + came
            else:
                values = [came] if isinstance(hops[at], str) else kept + [came]
            summed = [add(piece, kind) for piece in zip(*[halves(v, following) for v in values])]
            new_parts.append([[(summed[0], False)]] + summed[1:])
        return chains, new_parts, at + 1

    def last_swap(state):
        own = jnp.concatenate([own[0][0][0][0].astype(F32) for own in state[1]], 1)
        size = own.shape[0] // 2
        mine = lax.dynamic_slice_in_dim(own, core * size, size, 0)
        other = lax.dynamic_slice_in_dim(own, (1 - core) * size, size, 0)
        return mine, swap(other.astype(BF16), 1)

    def join(mine, other, widths):
        whole_parts, at = [], 0
        for w in widths:
            a, b = mine[:, at : at + w // 2], other[:, at : at + w // 2].astype(F32)
            whole_parts.append(
                jnp.where(core == 0, jnp.concatenate([a, b], 1), jnp.concatenate([b, a], 1))
            )
            at += w // 2
        return whole_parts

    one_way = [("tile", bit) for bit in tile_bits]
    other_way = one_way[::-1]
    clip_bits = [("clip", 1 << b) for b in range(layers.bit_length() - 1)]
    up_chains, down_chains = [one_way + clip_bits], [["scatter"] + one_way]
    time_chains = [["scatter"] + other_way]
    space_chains = [one_way + ["spread"], other_way + ["spread"]]

    order = [k for j in range(group) for k in range(j, n, group)]
    onehot = (action_ids[..., None] == lax.iota(jnp.int32, action_table.shape[0])).astype(F32)
    action_rows = jnp.einsum("cfa,ad->cfd", onehot, action_table, precision=lax.Precision.HIGHEST)
    act_time = lax.dynamic_index_in_dim(action_rows, clip, 0, keepdims=False)
    act_space = lax.dynamic_slice_in_dim(act_time, part * own_frames, own_frames, 0)[:, None, :]

    regular = p % 16 == 0 and 2 * own_frames == 16
    deal_back = None
    if regular:
        at = lax.iota(jnp.int32, 16 * 2 * own_frames)
        place, frame = at % 16, at // 16
        source = place * 2 * own_frames + (frame + core * own_frames) % (2 * own_frames)
        deal_back = (at[:, None] == source[None, :]).astype(BF16)
    marked = jnp.where((mask_bits > 0)[..., None], jnp.asarray(MASKED, BF16), tokens)
    marked = marked.reshape(p, n, own_frames, width)
    chunks = 2
    span = own_frames // chunks
    blocks_of = [lax.dynamic_index_in_dim(marked, me ^ k, 1, keepdims=False) for k in order]
    sources = [
        [value[:, c * span : (c + 1) * span].transpose(1, 0, 2) for value in blocks_of]
        for c in range(chunks)
    ]

    def send_out(parts):
        return [part if k == 0 else swap(part, k) for k, part in zip(order, parts)]

    cot_pieces = [
        lax.dynamic_index_in_dim(cotangent, clip ^ j, 1, keepdims=False).reshape(p * frames, width)
        for j in range(n // group)
    ]
    block = 16
    count = block * frames
    sub = min(count, 128)
    index = lax.iota(jnp.int32, count)
    slot, place = index // block, index % block
    frame_of_slot = ((part ^ (slot // own_frames)) * own_frames) + slot % own_frames
    target = place * frames + frame_of_slot
    perm_back = (target[:, None] == index[None, :]).astype(BF16)
    perm = (index[:, None] == target[None, :]).astype(BF16)
    seq = lax.iota(jnp.int32, sub)
    same = (seq[:, None] // frames) == (seq[None, :] // frames)
    bias = jnp.where(same & (seq[:, None] <= seq[None, :]), 0.0, NEGATIVE).astype(F32)
    own_hot = lax.dynamic_slice_in_dim(
        lax.dynamic_index_in_dim(onehot, clip, 0, keepdims=False), part * own_frames, own_frames, 0
    )[..., None]
    where_clip = clip ^ lax.iota(jnp.int32, clips)
    where_chip = (me // 2) ^ lax.iota(jnp.int32, n // 2)
    tables = dict(
        act_time=act_time,
        act_space=act_space,
        perm=perm,
        perm_back=perm_back,
        bias=bias,
        own_hot=own_hot,
        where_clip=where_clip,
        where_chip=where_chip,
        deal_back=deal_back,
        **{
            name: meta_of(chains)
            for name, chains in (
                ("up", up_chains),
                ("down", down_chains),
                ("time", time_chains),
                ("space", space_chains),
            )
        },
    )
    whole_at = [at for at, k in enumerate(order) if k in (0, 1, n - 1)]
    sources = [
        [blocks_of[at].transpose(1, 0, 2) if at in whole_at else part for at, part in enumerate(parts)]
        for parts in sources
    ]
    pieces = [send_out(sources[0])]
    pieces[0], sources, cot_pieces, tables = hold_parts(pieces[0], sources, cot_pieces, tables)
    for c in range(1, chunks):
        pieces.append(
            [
                pieces[0][at] if at in whole_at else swap(part, order[at])
                for at, part in enumerate(sources[c])
            ]
        )
    cot_pieces = [
        piece if j == 0 else swap(piece, j * group) for j, piece in enumerate(cot_pieces)
    ]
    if p % 16:
        pieces = [
            [
                jnp.concatenate(
                    [
                        part[c * span : (c + 1) * span] if at in whole_at else part
                        for at, part in enumerate(parts)
                    ],
                    1,
                )
            ]
            for c, parts in enumerate(pieces)
        ]

    def piece_blocks(c):
        return [
            (x, (1,) + x.shape[1:], lambda i, first=c * span * (x.shape[0] > span): (first + i, 0, 0))
            for x in pieces[c]
        ]

    kinds = len(pieces[0])
    act_time, act_space, own_hot = (tables[name] for name in ("act_time", "act_space", "own_hot"))
    perm, perm_back, bias = (tables[name] for name in ("perm", "perm_back", "bias"))
    where_clip, where_chip, deal_back = (
        tables[name] for name in ("where_clip", "where_chip", "deal_back")
    )

    head_flops = 2 * HEADS * HEAD_DIM

    def frame_block(*shape):
        return (1,) + shape, lambda i: (i, 0, 0)

    def chunk_block(first, *shape):
        return (1,) + shape, lambda i: (first + i, 0, 0)

    space, both = [], []
    for c in range(chunks):
        packed, o1, total, *parts = call(
            lambda *refs: space_forward_kernel(group, kinds, *refs),
            (span,),
            piece_blocks(c)
            + [
                (act_space, *chunk_block(c * span, 1, width)),
                (vectors, None, None),
                (w_space_qkv, None, None),
            ],
            [
                ((span, grid_all, 3 * width), BF16, *frame_block(grid_all, 3 * width)),
                ((span, grid_all, width), BF16, *frame_block(grid_all, width)),
                ((span, HEADS, grid_all), F32, *frame_block(HEADS, grid_all)),
            ]
            + [
                (
                    (span, 2, places, width),
                    BF16,
                    (1, 2, places, width),
                    lambda i: (i, 0, 0, 0),
                )
            ]
            * group,
            flops=2 * span * grid_all * width * 3 * width
            + 16 * span * grid_all * grid_all * head_flops,
        )
        space.append((packed, o1, total))
        both.append([part if j == 0 else swap(part, j) for j, part in enumerate(parts)])
    both = [both[c][j] for j in range(group) for c in range(chunks)]

    def slot_block(size):
        return (size, block, width), lambda i: (0, i, 0)

    total_block = ((HEADS, count), lambda i: (0, i))
    h1, h2, a2, packed_two, o2, total_two = call(
        lambda *refs: time_forward_kernel(sub, len(both), *refs),
        (places // block,),
        [
            (value, (span, None, block, width), lambda i, which=which: (0, which, i, 0))
            for which in range(2)
            for value in both
        ]
        + [
            (act_time, None, None),
            (perm, None, None),
            (bias, None, None),
            (vectors, None, None),
            (w_space_out, None, None),
            (w_time_qkv, None, None),
            (w_time_out, None, None),
        ],
        [
            ((rows, width), F32, *row_block(count, width)),
            ((rows, width), F32, *row_block(count, width)),
            ((rows, width), BF16, *row_block(count, width)),
            ((rows, 3 * width), BF16, *row_block(count, 3 * width)),
            ((rows, width), BF16, *row_block(count, width)),
            ((HEADS, rows), F32, *total_block),
        ],
        flops=2 * rows * width * 5 * width + 16 * rows * sub * head_flops,
    )

    step = min(p * frames, 256)
    per = p * frames // step

    def piece_block(j):
        return (step, width), lambda i, j=j: (jnp.clip(i - j * per, 0, per - 1), 0)

    *result_pieces, cot, z, dur, a3, r2, sums_three, bias_up = call(
        lambda *refs: feed_kernel(1024, len(cot_pieces), per, *refs),
        (rows // step,),
        [(h2, *row_block(step, width))]
        + [(piece, *piece_block(j)) for j, piece in enumerate(cot_pieces)]
        + [
            (vectors, None, None),
            (b_up[None, :], None, None),
            (w_up, None, None),
            (w_down, None, None),
        ],
        [((p * frames, width), BF16, *piece_block(j)) for j in range(len(cot_pieces))]
        + [
            ((rows, width), BF16, *row_block(step, width)),
            ((rows, hidden), BF16, *row_block(step, hidden)),
            ((rows, hidden), BF16, *row_block(step, hidden)),
            ((rows, width), BF16, *row_block(step, width)),
            ((rows, width), F32, *row_block(step, width)),
            ((8, width), F32, None, None),
            ((1, hidden), F32, None, None),
        ],
        flops=8 * rows * width * hidden,
    )

    result_pieces = [
        (piece if j == 0 else swap(piece, j * group)).reshape(p, 1, frames, width)
        for j, piece in enumerate(result_pieces)
    ]

    def make_down(meta, split):
        if hidden // blocks % 128:
            return columns_grad([([z], [cot])], meta, split, 256)
        return rows_grad(z, cot, meta, split)

    def make_up(meta, split):
        return columns_grad([([a3], [dur])], meta, split)

    up = begin(make_up, up_chains, tables["up"])
    cot, up, result_pieces[:-1] = hold_parts(cot, up, result_pieces[:-1])
    up = cross(up)
    down = begin(make_down, down_chains, tables["down"])
    r2, down, up, result_pieces = hold_parts(r2, down, up, result_pieces)
    up, down = depart(land(up)), cross(down)

    grad_packed_two, r2_low, sums_two, *r1_parts = call(
        lambda *refs: time_back_kernel(sub, *refs),
        (places // block,),
        [
            (r2, *row_block(count, width)),
            (h1, *row_block(count, width)),
            (packed_two, *row_block(count, 3 * width)),
            (total_two, *total_block),
            (perm_back, None, None),
            (bias, None, None),
            (vectors, None, None),
            (w_time_out, None, None),
            (w_time_qkv, None, None),
        ],
        [
            ((rows, 3 * width), BF16, *row_block(count, 3 * width)),
            ((rows, width), BF16, *row_block(count, width)),
            ((8, width), F32, None, None),
        ]
        + [((own_frames, places, width), BF16, *slot_block(own_frames))] * group,
        [pltpu.VMEM((count, width), BF16)],
        flops=2 * rows * width * 4 * width + 40 * rows * sub * head_flops,
    )
    grad_packed_two, up, down = hold_parts(grad_packed_two, up, down)
    r1_parts = [r1 if j == 0 else swap(r1, j) for j, r1 in enumerate(r1_parts)]
    extra = []

    def make_time(meta, split):
        pairs = [([a2], [grad_packed_two]), ([o2], [r2_low])]
        beside = [[down[1][0][0], down[2][0]], addends(up)]
        *made, down_total, up_total = columns_grad(pairs, meta, split, sums=beside)
        extra.extend((down_total, up_total))
        return made

    time = begin(make_time, time_chains, tables["time"])
    down = down[0], [[[(extra[0], False)]]], 0
    up = arrived(up, extra[1])

    dealt = 1 if p % 16 else n

    def send_back(parts):
        if dealt == 1:
            parts = [parts[0][:, at * p : (at + 1) * p] for at in range(n)]
            parts = [parts[order.index(k)] for k in range(n)]
            parts = [jnp.stack(parts[2 * j : 2 * j + 2]) for j in range(n // 2)]
        return [part if j == 0 else swap(part, 2 * j) for j, part in enumerate(parts)]

    def pass_on(came):
        crossed = swap(jnp.stack([value[1] for value in came]), 1)
        return [found for j, value in enumerate(came) for found in ((value, 0), (crossed, j))]

    def operand(found, block, index):
        return found[0], (None,) + block, lambda *i: (found[1],) + index(*i)

    def space_back(c, earlier, sums=()):
        packed, _, total = space[c]
        return call(
            lambda *refs: space_back_kernel(kinds, group, order, *refs),
            (span,),
            piece_blocks(c)
            + [(r1, *chunk_block(c * span, places, width)) for r1 in r1_parts]
            + [
                (act_space, *chunk_block(c * span, 1, width)),
                (own_hot, *chunk_block(c * span, action_table.shape[0], 1)),
                (earlier, None, None),
                (packed, *frame_block(grid_all, 3 * width)),
                (total, *frame_block(HEADS, grid_all)),
                (vectors, None, None),
                (w_space_out, None, None),
                (w_space_qkv, None, None),
            ],
            [
                ((span, grid_all, 3 * width), BF16, *frame_block(grid_all, 3 * width)),
                ((span, grid_all, width), BF16, *frame_block(grid_all, width)),
                ((span, grid_all, width), BF16, *frame_block(grid_all, width)),
                ((8 + action_table.shape[0], width), F32, None, None),
            ]
            + (
                [((span, grid_all, width), BF16, *frame_block(grid_all, width))]
                if dealt == 1
                else [
                    ((2, span, p, width), BF16, (2, 1, p, width), lambda i: (0, i, 0, 0))
                ]
                * (n // 2)
            ),
            [pltpu.VMEM((grid_all, width), BF16)],
            flops=2 * span * grid_all * width * 4 * width
            + 40 * span * grid_all * grid_all * head_flops,
            sums=sums,
        )

    r1_parts, time, up, down = hold_parts(r1_parts, time, up, down)
    up, down, time = depart(up), depart(down), cross(time)
    early = jnp.concatenate([sums_two, sums_three, bias_up.reshape(-1, width)], 0)
    back = [space_back(0, jnp.zeros((8 + action_table.shape[0], width), F32))]
    back[0], r1_parts, time, up = hold_parts(back[0], r1_parts, time, up)
    input_pieces = [send_back(back[0][4:])]
    up = depart(arrive(up))
    for c in range(1, chunks):
        beside = [[time[1][0][0], time[2][0]]] if c == 1 else []
        back.append(space_back(c, back[-1][3], beside))
        if c == 1:
            *back[c], time_total = back[c]
    time = time[0], [[[(time_total, False)]]], 0
    back, input_pieces, up, time = hold_parts(back, input_pieces, up, time)
    input_pieces[0] = pass_on(input_pieces[0])
    for c in range(1, chunks):
        input_pieces.append(send_back(back[c][4:]))
    up, time = depart(arrive(up)), depart(time)
    grads_one, a1s, r1s = list(zip(*back))[:3]

    def flat(values):
        return [value.reshape(-1, value.shape[-1]) for value in values]

    def make_space(meta, split):
        return columns_grad(
            [
                (flat(a1s), flat(grads_one)),
                (flat([o1 for _, o1, _ in space]), flat(r1s)),
            ],
            meta,
            split,
        )

    small = jnp.concatenate([back[-1][3], early], 0)
    small_hops = [("tile", 1 << b) for b in range(n.bit_length() - 1)] + clip_bits

    space_sum = begin(make_space, space_chains, tables["space"])
    where_clip, space_sum, up, down, input_pieces = hold_parts(
        where_clip, space_sum, up, down, input_pieces
    )
    space_sum = cross(space_sum)
    small_came = swap(small, small_hops[0][1], small_hops[0][0])
    up = arrive(up)
    while up[2] < len(up[0][0]):
        up = arrive(depart(up))
    up, down = last_swap(up), depart(arrive(down))
    result_out = collect_result(result_pieces, where_clip)
    space_sum, result_out, small_came = hold_parts(space_sum, result_out, small_came)
    space_sum, small = land(space_sum), small + small_came
    input_pieces[1:] = [pass_on(came) for came in input_pieces[1:]]
    time = arrive(time)

    def collect_input(input_pieces, where_chip):
        by_slot = [[pieces_of[k] for pieces_of in input_pieces] for k in range(n)]
        if regular:
            input_grad = collect(by_slot, where_chip, deal_back, tokens.shape, operand)
        else:
            input_grad = jnp.zeros((p, n, own_frames, width), BF16)
            for k, parts in enumerate(by_slot):
                piece = jnp.concatenate([value[at] for value, at in parts], 0)
                input_grad = lax.dynamic_update_slice_in_dim(
                    input_grad, piece.transpose(1, 0, 2)[:, None], me ^ k, 1
                )
            input_grad = input_grad.reshape(tokens.shape)
        return input_grad

    rounds = max(len(small_hops) - 1, len(space_sum[0][0]) + 1, 2 * len(one_way) + 1)
    for r in range(rounds):
        departed = small_came = time_moves = down_moves = None
        if r < len(space_sum[0][0]):
            if r == len(one_way):
                space_sum = merge(space_sum)
            departed = depart(space_sum)
        if r + 1 < len(small_hops):
            small_came = swap(small, small_hops[r + 1][1], small_hops[r + 1][0])
        if r >= len(one_way) and time[2] < len(time[0][0]):
            time_moves = depart(time)
        if r > len(one_way) and down[2] < len(down[0][0]):
            down_moves = depart(down)
        others = [down, input_pieces, up] if r == 0 else []
        if r == 1:
            input_grad = collect_input(input_pieces, where_chip)
            others = [input_grad]
        departed, small_came, time_moves, down_moves, *others = hold_parts(
            departed, small_came, time_moves, down_moves, *others
        )
        if r == 0:
            down, input_pieces, up = others
            down = arrive(down)
        if r == 1:
            (input_grad,) = others
        if time_moves is not None:
            time = arrive(time_moves)
            if time[2] == len(time[0][0]):
                time_last = last_swap(time)
        if down_moves is not None:
            down = arrive(down_moves)
            if down[2] == len(down[0][0]):
                down_last = last_swap(down)
        if departed is not None:
            space_sum = arrive(departed)
        if small_came is not None:
            small = small + small_came
        if r + 1 == len(space_sum[0][0]):
            space_last = last_swap(space_sum)
    at = 8 + action_table.shape[0]
    sums = small[at:]
    (down_out,) = join(*down_last, [width])
    (up_out,) = join(*up, [hidden])
    time_qkv, time_out = join(*time_last, [3 * width, width])
    space_qkv, space_out = join(*space_last, [3 * width, width])
    return (
        result_out,
        input_grad,
        jnp.concatenate([small[:2], sums[:2], sums[8:11], small[2:3]], 0),
        small[8:at],
        space_qkv,
        space_out,
        time_qkv,
        time_out,
        up_out,
        sums[16:].reshape(hidden),
        down_out,
    )


def hold_parts(*values):
    leaves, tree = jax.tree.flatten(values)
    arrays = [i for i, leaf in enumerate(leaves) if isinstance(leaf, jax.Array)]
    held = lax.optimization_barrier([leaves[i] for i in arrays])
    for i, leaf in zip(arrays, held):
        leaves[i] = leaf
    return jax.tree.unflatten(tree, leaves)


def solution(mesh):
    spread = P("tile", "clip", None, None)
    rows = P(("clip", "tile"), None)
    return jax.shard_map(
        body,
        mesh=mesh,
        in_specs=(spread, P("tile", "clip", None), P("clip", None)) + (P(),) * 9 + (spread,),
        out_specs=(spread, spread, P(), P(), rows, rows, rows, rows, rows, P(), rows),
        check_vma=False,
    )
```
